32 devices in a mesh: win: 8 (over z, x), grp: 4 (over y, core).
Axes of the slice: x: 2, y: 2, z: 4, core: 2. Of those that a mesh axis runs over, the one named last changes fastest.
Arguments:
- x_slots: bfloat16 [160, 196, 768], P(('win', 'grp')), may hold values from -6 to 6
- counts: int32 [32], P(('win', 'grp')), may hold values from 1 to 5, as said below
- cotangent: bfloat16 [96, 196, 768], P(('win', 'grp')), may hold values from -6 to 6
- w_qkv: bfloat16 [768, 2304], replicated, may hold values from -0.21875 to 0.21875
- w_proj: bfloat16 [768, 768], replicated, may hold values from -0.875 to 0.875
- w_fc1: bfloat16 [768, 3072], replicated, may hold values from -0.21875 to 0.21875
- w_fc2: bfloat16 [3072, 768], replicated, may hold values from -0.109375 to 0.109375
- small_params: bfloat16 [12672], replicated, may hold values from -1.5 to 1.5
- moment_qkv: float32 [768, 2304], P('win', 'grp'), may hold values from -64 to 64
- moment_proj: float32 [768, 768], P('win', 'grp'), may hold values from -64 to 64
- moment_fc1: float32 [768, 3072], P('win', 'grp'), may hold values from -64 to 64
- moment_fc2: float32 [3072, 768], P('win', 'grp'), may hold values from -64 to 64
- moment_small: float32 [12672], replicated, may hold values from -64 to 64
- square_qkv: float32 [768, 2304], P('win', 'grp'), may hold values from 1 to 96
- square_proj: float32 [768, 768], P('win', 'grp'), may hold values from 1 to 96
- square_fc1: float32 [768, 3072], P('win', 'grp'), may hold values from 1 to 96
- square_fc2: float32 [3072, 768], P('win', 'grp'), may hold values from 1 to 96
- square_small: float32 [12672], replicated, may hold values from 1 to 96
Outputs:
- block_out: bfloat16 [96, 196, 768], P(('win', 'grp'))
- input_grad: bfloat16 [160, 196, 768], P(('win', 'grp'))
- grad_qkv: float32 [768, 2304], P('win', 'grp')
- grad_proj: float32 [768, 768], P('win', 'grp')
- grad_fc1: float32 [768, 3072], P('win', 'grp')
- grad_fc2: float32 [3072, 768], P('win', 'grp')
- grad_small: float32 [12672], replicated
- next_moment_qkv: float32 [768, 2304], P('win', 'grp')
- next_moment_proj: float32 [768, 768], P('win', 'grp')
- next_moment_fc1: float32 [768, 3072], P('win', 'grp')
- next_moment_fc2: float32 [3072, 768], P('win', 'grp')
- next_moment_small: float32 [12672], replicated
- next_square_qkv: float32 [768, 2304], P('win', 'grp')
- next_square_proj: float32 [768, 768], P('win', 'grp')
- next_square_fc1: float32 [768, 3072], P('win', 'grp')
- next_square_fc2: float32 [3072, 768], P('win', 'grp')
- next_square_small: float32 [12672], replicated
- new_qkv: bfloat16 [768, 2304], P(None, 'grp')
- new_proj: bfloat16 [768, 768], P(None, 'grp')
- new_fc1: bfloat16 [768, 3072], P(None, 'grp')
- new_fc2: bfloat16 [3072, 768], P(None, 'grp')
- new_small: bfloat16 [12672], replicated
The draws below stay inside these ranges and needn't reach their ends.
Inputs may be any that keep to these rules, and one draw needn't show every extreme that they name: Device d holds the windows offset_d to offset_d + counts_d - 1, offset_d being the sum of the counts before it; offset_d differs from 3 * d by exactly one for 0 < d < 32, and the counts add up to 96.
All inputs are finite; a program needn't handle non-finite values.
Results may differ from the reference program's by a relative error of at most 0.017.
Values may be sent and summed in bfloat16 or wider, within the bound.
No kernel may reach another device: no remote copies, remote signals or barrier semaphores. Data moves between devices by JAX's collectives and lax.ppermute only.
A program may use at most 448 MiB of HBM per device.

```python
import math
import jax
import jax.numpy as jnp
from jax import lax

D = 768
HEADS = 12
HD = 64
FF = 3072
WS = 14
SIDE = 64
EPD = 3
STEP = 4
TOKW = 196
GRID = 5
RELN = 27
CAP = 5
HOLDERS = 32
WINDOWS = 96
SLOTS = 160
NSMALL = 12672


def draw_counts(key, part):
    holder_index = jnp.arange(HOLDERS, dtype=jnp.int32)
    signs = 2 * jax.random.randint(key, (HOLDERS,), 0, 2, dtype=jnp.int32) - 1
    drift = jnp.where(holder_index == 0, 0, signs)
    drift = jnp.where(holder_index == 1, -1, drift)
    drift = jnp.where(holder_index == 2, 1, drift)
    drift = jnp.where(holder_index == 3, -1, drift)
    drift_next = jnp.concatenate([drift[1:], jnp.zeros((1,), jnp.int32)])
    return (EPD + drift_next - drift).astype(jnp.int32)


def draw_small_params(key, part):
    gain_key = jax.random.fold_in(key, 11)
    bias_key = jax.random.fold_in(key, 12)
    table_key = jax.random.fold_in(key, 13)
    gains = jnp.clip(1.0 + 0.1 * jax.random.normal(gain_key, (2 * D,), jnp.float32), 0.5, 1.5)
    biases = jnp.clip(0.3 * jax.random.normal(bias_key, (6 * D + FF,), jnp.float32), -1.5, 1.5)
    tables = jnp.clip(0.08 * jax.random.normal(table_key, (2 * RELN * HD,), jnp.float32), -0.4, 0.4)
    return jnp.concatenate([gains, biases, tables]).astype(jnp.bfloat16)


def steps_of(stream_key, shape, cuts, low, top_value):
    def one(axis_at, blocks):
        steps = jax.random.uniform(jax.random.fold_in(jax.random.fold_in(stream_key, 6), axis_at), (blocks,), jnp.float32, low / len(cuts), top_value / len(cuts))
        return jnp.repeat(jnp.exp(steps), shape[axis_at] // blocks).reshape((-1,) + (1,) * (len(shape) - axis_at - 1))

    factor_of = one(*cuts[0])
    for cut in cuts[1:]:
        factor_of = factor_of * one(*cut)
    return factor_of


def noise(own_key, dims, scale, limit, shards=(), kind=jnp.bfloat16):
    gain = steps_of(own_key, dims, shards, -0.22, 0.18) if shards else 1.0
    values = jax.random.normal(own_key, dims, jnp.float32) * scale * gain
    return jnp.minimum(jnp.maximum(values, -limit), limit).astype(kind)


def setup_inputs(seed: int = 0) -> dict:
    key_of = jax.random.split(jax.random.key(seed), 19)
    return {
        "x_slots": noise(key_of[0], (SLOTS, TOKW, D), 1.0, 6.0, ((0, 32),)),
        "counts": draw_counts(jax.random.fold_in(key_of[18], 71), 0),
        "cotangent": noise(key_of[2], (WINDOWS, TOKW, D), 1.0, 6.0, ((0, 32),)),
        "w_qkv": noise(key_of[3], (D, 3 * D), D ** -0.5, 0.21875),
        "w_proj": noise(key_of[4], (D, D), (D // 16) ** -0.5, 0.875),
        "w_fc1": noise(key_of[5], (D, FF), D ** -0.5, 0.21875),
        "w_fc2": noise(key_of[6], (FF, D), FF ** -0.5, 0.109375),
        "small_params": draw_small_params(jax.random.fold_in(key_of[18], 71), 0),
        "moment_qkv": noise(key_of[8], (D, 3 * D), (WINDOWS // 8), 64.0, ((0, 8), (1, 4)), jnp.float32),
        "moment_proj": noise(key_of[9], (D, D), (WINDOWS // 8), 64.0, ((0, 8), (1, 4)), jnp.float32),
        "moment_fc1": noise(key_of[10], (D, FF), (WINDOWS // 8), 64.0, ((0, 8), (1, 4)), jnp.float32),
        "moment_fc2": noise(key_of[11], (FF, D), (WINDOWS // 8), 64.0, ((0, 8), (1, 4)), jnp.float32),
        "moment_small": noise(key_of[12], (NSMALL,), (WINDOWS // 8), 64.0, (), jnp.float32),
        "square_qkv": jnp.clip(jnp.exp(math.log(96.0) - 4.564348 * jax.random.uniform(key_of[13], (D, 3 * D), jnp.float32) ** steps_of(key_of[13], (D, 3 * D), ((0, 8), (1, 4)), -0.2, 0.2)), 1.0, 96.0),
        "square_proj": jnp.clip(jnp.exp(math.log(96.0) - 4.564348 * jax.random.uniform(key_of[14], (D, D), jnp.float32) ** steps_of(key_of[14], (D, D), ((0, 8), (1, 4)), -0.2, 0.2)), 1.0, 96.0),
        "square_fc1": jnp.clip(jnp.exp(math.log(96.0) - 4.564348 * jax.random.uniform(key_of[15], (D, FF), jnp.float32) ** steps_of(key_of[15], (D, FF), ((0, 8), (1, 4)), -0.2, 0.2)), 1.0, 96.0),
        "square_fc2": jnp.clip(jnp.exp(math.log(96.0) - 4.564348 * jax.random.uniform(key_of[16], (FF, D), jnp.float32) ** steps_of(key_of[16], (FF, D), ((0, 8), (1, 4)), -0.2, 0.2)), 1.0, 96.0),
        "square_small": jnp.clip(jnp.exp(jax.random.uniform(key_of[17], (NSMALL,), jnp.float32, math.log(1.0), math.log(96.0))), 1.0, 96.0),
    }


precise = lax.Precision.HIGHEST
learn_rate = 0.06

@jax.custom_vjp
def low(v):
    return lax.optimization_barrier(v.astype(jnp.bfloat16)).astype(jnp.float32)

@jax.custom_vjp
def low_back(v):
    return v

def low_keep(v):
    return (low(v), None)

def low_pass(kept, grad):
    return (grad,)

def back_keep(v):
    return (v, None)

def back_low(kept, grad):
    return (low(grad),)
low.defvjp(low_keep, low_pass)
low_back.defvjp(back_keep, back_low)

def unpack(small):
    gain_one = small[0:D]
    gain_two = small[D:2 * D]
    shift_one = small[2 * D:3 * D]
    shift_two = small[3 * D:4 * D]
    query_bias = small[4 * D:5 * D]
    value_bias = small[5 * D:6 * D]
    proj_bias = small[6 * D:7 * D]
    second_bias = small[7 * D:8 * D]
    first_bias = small[8 * D:8 * D + FF]
    tables = small[8 * D + FF:].reshape(2, RELN, HD)
    return (gain_one, gain_two, shift_one, shift_two, query_bias, value_bias, proj_bias, second_bias, first_bias, tables)

def relative_tables(tables):
    offsets = jnp.arange(WS)[:, None] - jnp.arange(WS)[None, :] + WS - 1
    onehot = (offsets[:, :, None] == jnp.arange(RELN)[None, None, :]).astype(jnp.float32)
    row_table = jnp.einsum('abr,rc->abc', onehot, tables[0], precision=precise)
    col_table = jnp.einsum('abr,rc->abc', onehot, tables[1], precision=precise)
    return (row_table, col_table)

def norm_parts(vector):
    centered = vector - lax.optimization_barrier(jnp.mean(vector, axis=-1, keepdims=True))
    scale_inv = lax.rsqrt(lax.optimization_barrier(jnp.mean(centered * centered, axis=-1, keepdims=True)) + 1e-06)
    return (centered * scale_inv, scale_inv)

def gelu_exact(hidden):
    return 0.5 * hidden * (1.0 + jax.scipy.special.erf(hidden * 0.7071067811865476))

def window_mask(window_index):
    grid_spot = window_index % (GRID * GRID)
    token_index = jnp.arange(TOKW, dtype=jnp.int32)
    inside_rows = (grid_spot // GRID)[:, None] * WS + (token_index // WS)[None, :] < SIDE
    inside_cols = (grid_spot % GRID)[:, None] * WS + (token_index % WS)[None, :] < SIDE
    return (inside_rows & inside_cols).astype(jnp.float32)[:, :, None]

def scores_of(query_heads, key_heads, row_table, col_table):
    window_total = query_heads.shape[0]
    direct = jnp.einsum('wtha,wsha->whts', query_heads, key_heads, precision=precise) * HD ** (-0.5)
    query_grid = query_heads.reshape(window_total, WS, WS, HEADS, HD)
    along_rows = jnp.einsum('wijhc,ikc->whijk', query_grid, row_table, precision=precise)
    along_cols = jnp.einsum('wijhc,jkc->whijk', query_grid, col_table, precision=precise)
    relative = (along_rows[:, :, :, :, :, None] + along_cols[:, :, :, :, None, :]).reshape(window_total, HEADS, TOKW, TOKW)
    return direct + relative

def block(inputs, token_mask, w_qkv, w_proj, w_fc1, w_fc2, small):
    gain_one, gain_two, shift_one, shift_two, query_bias, value_bias, proj_bias, second_bias, first_bias, tables = unpack(small)
    row_table, col_table = relative_tables(tables)
    window_total = inputs.shape[0]
    normed, scale_inv = norm_parts(inputs)
    first_normed = low((normed * gain_one + shift_one) * token_mask).reshape(window_total * TOKW, D)
    bias_all = jnp.concatenate([query_bias, jnp.zeros((D,), jnp.float32), value_bias])
    projected = low_back(jnp.dot(first_normed, w_qkv, precision=precise) + bias_all)
    query_heads = low(projected[:, :D]).reshape(window_total, TOKW, HEADS, HD)
    key_heads = low(projected[:, D:2 * D]).reshape(window_total, TOKW, HEADS, HD)
    value_heads = low(projected[:, 2 * D:]).reshape(window_total, TOKW, HEADS, HD)
    scores = low_back(scores_of(query_heads, key_heads, row_table, col_table))
    row_peak = lax.optimization_barrier(jnp.max(scores, axis=-1, keepdims=True))
    expo = jnp.exp(scores - row_peak)
    attn_probs = expo / lax.optimization_barrier(jnp.sum(expo, axis=-1, keepdims=True))
    context = jnp.einsum('whts,wsha->wtha', low(attn_probs), value_heads, precision=precise)
    context = low(low_back(context.reshape(window_total * TOKW, D)))
    branch = low_back(jnp.dot(context, w_proj, precision=precise) + proj_bias).reshape(window_total, TOKW, D)
    middle = token_mask * (inputs + branch)
    normed_two, scale_two = norm_parts(middle)
    second = low((normed_two * gain_two + shift_two) * token_mask).reshape(window_total * TOKW, D)
    hidden = low_back(jnp.dot(second, w_fc1, precision=precise) + first_bias)
    active = low(gelu_exact(hidden))
    update = low_back(jnp.dot(active, w_fc2, precision=precise) + second_bias).reshape(window_total, TOKW, D)
    return token_mask * (middle + update)

def adam_step(parameter, gradient, moment, square, first_fix, second_fix):
    moment_next = 0.5 * moment + 0.5 * gradient
    square_next = 0.999 * square + 0.001 * gradient * gradient
    fresh_weight = parameter - learn_rate * (moment_next / first_fix) / (jnp.sqrt(square_next / second_fix) + 1e-08)
    return (moment_next, square_next, fresh_weight.astype(jnp.bfloat16))

def reference(x_slots, counts, cotangent, w_qkv, w_proj, w_fc1, w_fc2, small_params, moment_qkv, moment_proj, moment_fc1, moment_fc2, moment_small, square_qkv, square_proj, square_fc1, square_fc2, square_small):
    starts = (jnp.cumsum(counts) - counts).astype(jnp.int32)
    window_index = jnp.arange(WINDOWS, dtype=jnp.int32)
    holder = (lax.optimization_barrier(jnp.sum((starts[None, :] <= window_index[:, None]).astype(jnp.int32), axis=1)) - 1).astype(jnp.int32)
    source = (holder * CAP + window_index - starts[holder]).astype(jnp.int32)
    inputs = x_slots.astype(jnp.float32)[source]
    token_mask = window_mask(window_index)
    groups = WINDOWS // 16
    weight_a = w_qkv.astype(jnp.float32)
    weight_b = w_proj.astype(jnp.float32)
    weight_c = w_fc1.astype(jnp.float32)
    weight_d = w_fc2.astype(jnp.float32)
    small = small_params.astype(jnp.float32)

    def forward(inputs, weight_a, weight_b, weight_c, weight_d, small):

        def one_group(packed):
            return block(packed[0], packed[1], weight_a, weight_b, weight_c, weight_d, small)
        grouped = (inputs.reshape(groups, 16, TOKW, D), token_mask.reshape(groups, 16, TOKW, 1))
        return lax.map(jax.checkpoint(one_group), grouped).reshape(WINDOWS, TOKW, D)
    block_out, pullback = jax.vjp(forward, inputs, weight_a, weight_b, weight_c, weight_d, small)
    gradients = pullback(cotangent.astype(jnp.float32))
    input_grad = jnp.zeros((SLOTS, TOKW, D), jnp.float32).at[source].set(gradients[0]).astype(jnp.bfloat16)
    step_value = jnp.float32(STEP)
    first_fix = 1.0 - jnp.power(jnp.float32(0.5), step_value)
    second_fix = 1.0 - jnp.power(jnp.float32(0.999), step_value)
    upd_qkv = adam_step(weight_a, gradients[1], moment_qkv, square_qkv, first_fix, second_fix)
    upd_proj = adam_step(weight_b, gradients[2], moment_proj, square_proj, first_fix, second_fix)
    upd_fc1 = adam_step(weight_c, gradients[3], moment_fc1, square_fc1, first_fix, second_fix)
    upd_fc2 = adam_step(weight_d, gradients[4], moment_fc2, square_fc2, first_fix, second_fix)
    upd_small = adam_step(small, gradients[5], moment_small, square_small, first_fix, second_fix)
    return (block_out.astype(jnp.bfloat16), input_grad, gradients[1], gradients[2], gradients[3], gradients[4], gradients[5], upd_qkv[0], upd_proj[0], upd_fc1[0], upd_fc2[0], upd_small[0], upd_qkv[1], upd_proj[1], upd_fc1[1], upd_fc2[1], upd_small[1], upd_qkv[2], upd_proj[2], upd_fc1[2], upd_fc2[2], upd_small[2])
```

```python
import functools

import jax
import jax.numpy as jnp
from jax import lax
from jax.experimental import pallas as pl
from jax.experimental.pallas import tpu as pltpu
from jax.sharding import PartitionSpec as P

D = 768
HEADS = 12
HD = 64
FF = 3072
WS = 14
SIDE = 64
STEP = 4
TOKW = 196
GRID = 5
RELN = 27
TP = 224

root_half = 0.7071067811865476
inv_root_two_pi = 0.3989422804014327
learn_rate = 0.06
bf16 = jnp.bfloat16
f32 = jnp.float32
VMEM_LIMIT = 56 << 20


def dot(a, b):
    return lax.dot_general(a, b, (((1,), (0,)), ((), ())), preferred_element_type=f32)


def dot_nt(a, b):
    return lax.dot_general(a, b, (((1,), (1,)), ((), ())), preferred_element_type=f32)


def dot_tn(a, b):
    return lax.dot_general(a, b, (((0,), (0,)), ((), ())), preferred_element_type=f32)


def iota(shape, axis):
    return lax.broadcasted_iota(jnp.int32, shape, axis)


def spread():
    row, token = iota((TP, TOKW), 0), iota((TP, TOKW), 1)
    hit = ((row & 15) < WS) & (token == WS * (row >> 4) + (row & 15))
    return hit.astype(f32).astype(bf16)


def gather_rows():
    token, row = iota((TOKW, TP), 0), iota((TOKW, TP), 1)
    hit = ((row & 15) < WS) & (token == WS * (row >> 4) + (row & 15))
    return hit.astype(f32).astype(bf16)


def key_lanes():
    row, lane = iota((TP, 128), 0), iota((TP, 128), 1)
    i, j = row >> 4, row & 15
    low = lane & 31
    hit = (low < WS) & (((lane < 64) & (low == i)) | ((lane >= 64) & (low == j)))
    shut = (lane == 127) & (j >= WS)
    return jnp.where(shut, -1e30, hit.astype(f32)).astype(bf16)


def inside(limit_row, limit_col):
    row = iota((TP, 1), 0)
    i, j = row >> 4, row & 15
    return ((i < limit_row) & (j < jnp.minimum(limit_col, WS))).astype(f32)


def norm_parts(v):
    centered = v - jnp.mean(v, axis=-1, keepdims=True)
    scale_inv = lax.rsqrt(jnp.mean(centered * centered, axis=-1, keepdims=True) + 1e-06)
    return centered * scale_inv, scale_inv


def norm_back(e, normed, scale_inv):
    return scale_inv * (
        e
        - jnp.mean(e, axis=-1, keepdims=True)
        - normed * jnp.mean(e * normed, axis=-1, keepdims=True)
    )


def lane_mask(head):
    lane = iota((1, 128), 1)
    return ((lane < HD) if head == 0 else (lane >= HD)).astype(f32).astype(bf16)


def query_rolls(table):
    lane = iota((16, 128), 1)
    out = []
    for i in range(WS):
        tile = table[16 * i : 16 * i + 16]
        by_row = pltpu.roll(tile, 51 + i, 1)
        by_col = pltpu.roll(tile, 51, 1, stride=1, stride_axis=0)
        kept = jnp.where(lane < WS, by_row, 0.0)
        out.append(jnp.where((lane >= 64) & (lane < 64 + WS), by_col, kept))
    return jnp.concatenate(out, axis=0)


def query_lanes(table):
    aug = query_rolls(table)
    high = aug.astype(bf16).astype(f32)
    full = high + pltpu.roll(aug - high, 32, 1)
    return jnp.where(iota((TP, 128), 1) == 127, 1.0, full).astype(bf16)


def fwd_kernel(
    info, xs_ref, prev_ref, next_ref, wqkv_ref, wproj_ref, vec_ref, bias_ref, tab_ref,
    xpad_ref, n1_ref, qkv_ref, pt_ref, o_ref, h_ref, n2_ref,
):
    k = pl.program_id(0)
    source = info[k, 1]
    x = jnp.where(source == 0, xs_ref[0], jnp.where(source == 1, prev_ref[0], next_ref[0]))
    big = dot(spread(), x)
    xpad_ref[0] = big.astype(bf16)
    mask = inside(info[k, 2], info[k, 3])
    vec = vec_ref[...]
    normed, _ = norm_parts(big)
    n1 = (mask * (normed * vec[0:1] + vec[2:3])).astype(bf16)
    n1_ref[0] = n1
    qkv_ref[0] = (dot(n1, wqkv_ref[...]) + bias_ref[...]).astype(bf16)
    keys_extra = key_lanes()
    for pair in range(HEADS // 2):
        at = 128 * pair
        q = qkv_ref[0, :, at : at + 128]
        key = jnp.concatenate([qkv_ref[0, :, D + at : D + at + 128], keys_extra], axis=1)
        v_t = qkv_ref[0, :, 2 * D + at : 2 * D + at + 128].T
        tables = dot(q, tab_ref[...])
        outs = []
        for head in range(2):
            extra = query_lanes(tables[:, 128 * head : 128 * head + 128])
            q_all = jnp.concatenate([q * (lane_mask(head) * 0.125), extra], axis=1)
            s_t = dot_nt(key, q_all)
            e = jnp.exp(s_t - jnp.max(s_t, axis=0, keepdims=True))
            p_t = (e * (1.0 / jnp.sum(e, axis=0, keepdims=True))).astype(bf16)
            pt_ref[0, 2 * pair + head] = p_t
            outs.append(dot(v_t[HD * head : HD * head + HD], p_t))
        o_ref[0, :, at : at + 128] = jnp.concatenate(outs, axis=0).T.astype(bf16)
    a = dot(o_ref[0], wproj_ref[...]) + vec[6:7]
    h = mask * (big + a)
    h_ref[0] = h
    normed_two, _ = norm_parts(h)
    n2_ref[0] = (mask * (normed_two * vec[1:2] + vec[3:4])).astype(bf16)


def forward_attention(info, x_slots, prev, nxt, w_qkv, w_proj, vec, bias, tab):
    windows = info.shape[0]
    one = lambda *tail: pl.BlockSpec((1,) + tail, lambda k, s: (k,) + (0,) * len(tail))
    whole = lambda a: pl.BlockSpec(a.shape, lambda k, s: (0,) * a.ndim)
    shape = lambda *tail, dtype=bf16: jax.ShapeDtypeStruct((windows,) + tail, dtype)
    return pl.pallas_call(
        fwd_kernel,
        grid_spec=pltpu.PrefetchScalarGridSpec(
            num_scalar_prefetch=1,
            grid=(windows,),
            in_specs=[
                pl.BlockSpec((1, TOKW, D), lambda k, s: (s[k, 0], 0, 0)),
                whole(prev), whole(nxt), whole(w_qkv), whole(w_proj), whole(vec), whole(bias), whole(tab),
            ],
            out_specs=[
                one(TP, D), one(TP, D), one(TP, 3 * D), one(HEADS, TP, TP), one(TP, D), one(TP, D), one(TP, D),
            ],
        ),
        out_shape=[
            shape(TP, D), shape(TP, D), shape(TP, 3 * D), shape(HEADS, TP, TP), shape(TP, D),
            shape(TP, D, dtype=f32), shape(TP, D),
        ],
        compiler_params=pltpu.CompilerParams(vmem_limit_bytes=VMEM_LIMIT),
        cost_estimate=pl.CostEstimate(flops=12 * 10**9, bytes_accessed=20 * 10**6, transcendentals=2 * 10**6),
        name="attention_forward",
    )(info, x_slots, prev, nxt, w_qkv, w_proj, vec, bias, tab)


def prepare(small):
    s = small.astype(f32)
    vec = s[: 8 * D].reshape(8, D)
    first_bias = s[8 * D : 8 * D + FF].reshape(1, FF)
    bias = jnp.concatenate([vec[4:5], jnp.zeros((1, D), f32), vec[5:6]], axis=1)
    tables = small[8 * D + FF :].reshape(2, RELN, HD)
    back_h, back_w, rel_w = tables[0, ::-1], tables[1, ::-1], tables[1]
    gap = jnp.zeros((64 - RELN, HD), bf16)
    one = jnp.concatenate([back_w, gap, back_h, gap], axis=0)
    none = jnp.zeros_like(one)
    fwd = jnp.block([[one.T, none.T], [none.T, one.T]])
    short = jnp.zeros((32 - RELN, HD), bf16)
    half = jnp.concatenate([back_h, short, rel_w, short], axis=0)
    nil = jnp.zeros_like(half)
    bwd = jnp.block([[nil, half], [half, nil]])
    return vec, first_bias, bias, fwd, bwd


def params(flops, moved, trans=0, **more):
    return dict(
        compiler_params=pltpu.CompilerParams(vmem_limit_bytes=VMEM_LIMIT),
        cost_estimate=pl.CostEstimate(flops=flops, bytes_accessed=moved, transcendentals=trans),
        **more,
    )


def whole(a):
    return pl.BlockSpec(a.shape, lambda k, *s: (0,) * a.ndim)


def sds(*dims, dtype=bf16):
    return jax.ShapeDtypeStruct(dims, dtype)


def masks(info, windows):
    return [inside(info[k, 2], info[k, 3]) for k in range(windows)]


def up_kernel(info, n2_ref, cot_ref, w1_ref, b1_ref, gl_ref, slope_ref, grad_ref, dz_ref, b2_ref, dz_t):
    windows = cot_ref.shape[0]

    @pl.when(pl.program_id(0) == 0)
    def _():
        total = jnp.zeros((1, D), f32)
        for k, mask in enumerate(masks(info, windows)):
            part = dot(spread(), cot_ref[k]) * mask
            dz_ref[TP * k : TP * k + TP] = part.astype(bf16)
            total += jnp.sum(part, axis=0, keepdims=True)
        b2_ref[...] = total
        dz_t[...] = dz_ref[...].T

    u = dot(n2_ref[...], w1_ref[...]) + b1_ref[...]
    half = 0.5 * (1.0 + lax.erf(u * root_half))
    gl = (u * half).astype(bf16)
    gl_ref[...] = gl
    slope_ref[...] = (half + u * jnp.exp(-0.5 * u * u) * inv_root_two_pi).astype(bf16)
    grad = dot(dz_t[...], gl).astype(bf16)
    for g in range(grad_ref.shape[0]):
        rows = grad_ref.shape[2]
        for w in range(grad_ref.shape[1]):
            cols = grad_ref.shape[3]
            grad_ref[g, w] = grad[rows * g : rows * g + rows, cols * w : cols * w + cols]


def feed_up(info, n2, cot, w_fc1, b1):
    rows = n2.shape[0]
    step = D
    steps = FF // step
    return pl.pallas_call(
        up_kernel,
        grid_spec=pltpu.PrefetchScalarGridSpec(
            num_scalar_prefetch=1,
            grid=(steps,),
            in_specs=[
                whole(n2), whole(cot),
                pl.BlockSpec((D, step), lambda k, s: (0, k)),
                pl.BlockSpec((1, step), lambda k, s: (0, k)),
            ],
            out_specs=[
                pl.BlockSpec((rows, step), lambda k, s: (0, k)),
                pl.BlockSpec((rows, step), lambda k, s: (0, k)),
                pl.BlockSpec((4, 2, 192, 384), lambda k, s: (0, k, 0, 0)),
                pl.BlockSpec((rows, D), lambda k, s: (0, 0)),
                pl.BlockSpec((1, D), lambda k, s: (0, 0)),
            ],
            scratch_shapes=[pltpu.VMEM((D, rows), bf16)],
        ),
        out_shape=[
            sds(rows, FF), sds(rows, FF), sds(4, 8, 192, 384), sds(rows, D), sds(1, D, dtype=f32),
        ],
        name="feed_up",
        **params(6 * 10**9, 24 * 10**6, 4 * 10**6),
    )(info, n2, cot, w_fc1, b1)


def down_kernel(
    info, dz_ref, slope_ref, n2_ref, h_ref, w1_ref, w2_ref, wproj_ref, vec_ref,
    grad_ref, b1_ref, dh_ref, da_ref, do_ref, sums_ref, n2_t, acc,
):
    step = pl.program_id(0)

    @pl.when(step == 0)
    def _():
        n2_t[...] = n2_ref[...].T
        acc[...] = jnp.zeros_like(acc)

    du = dot_nt(dz_ref[...], w2_ref[...]) * slope_ref[...].astype(f32)
    du_low = du.astype(bf16)
    b1_ref[...] = jnp.sum(du_low.astype(f32), axis=0, keepdims=True)
    grad_ref[0] = dot(n2_t[...], du_low).astype(bf16)
    acc[...] += dot_nt(du_low, w1_ref[...])

    @pl.when(step == pl.num_programs(0) - 1)
    def _():
        vec = vec_ref[...]
        windows = acc.shape[0] // TP
        gain = jnp.zeros((1, D), f32)
        shift = jnp.zeros((1, D), f32)
        bias = jnp.zeros((1, D), f32)
        for k, mask in enumerate(masks(info, windows)):
            at = slice(TP * k, TP * k + TP)
            dn = acc[at] * mask
            normed, scale_inv = norm_parts(h_ref[at])
            gain += jnp.sum(dn * normed, axis=0, keepdims=True)
            shift += jnp.sum(dn, axis=0, keepdims=True)
            dh = mask * (dz_ref[at].astype(f32) + norm_back(dn * vec[1:2], normed, scale_inv))
            dh_ref[at] = dh
            da = dh.astype(bf16)
            da_ref[at] = da
            bias += jnp.sum(da.astype(f32), axis=0, keepdims=True)
            do_ref[at] = dot_nt(da, wproj_ref[...]).astype(bf16)
        sums_ref[0:1] = gain
        sums_ref[1:2] = shift
        sums_ref[2:3] = bias
        sums_ref[3:8] = jnp.zeros((5, D), f32)


def feed_down(info, dz, slope, n2, h, w_fc1, w_fc2, w_proj, vec):
    rows = n2.shape[0]
    step = D
    steps = FF // step
    return pl.pallas_call(
        down_kernel,
        grid_spec=pltpu.PrefetchScalarGridSpec(
            num_scalar_prefetch=1,
            grid=(steps,),
            in_specs=[
                whole(dz),
                pl.BlockSpec((rows, step), lambda k, s: (0, k)),
                whole(n2), whole(h),
                pl.BlockSpec((D, step), lambda k, s: (0, k)),
                pl.BlockSpec((step, D), lambda k, s: (k, 0)),
                whole(w_proj), whole(vec),
            ],
            out_specs=[
                pl.BlockSpec((1, D, step), lambda k, s: (k, 0, 0)),
                pl.BlockSpec((1, step), lambda k, s: (0, k)),
                pl.BlockSpec((rows, D), lambda k, s: (0, 0)),
                pl.BlockSpec((rows, D), lambda k, s: (0, 0)),
                pl.BlockSpec((rows, D), lambda k, s: (0, 0)),
                pl.BlockSpec((8, D), lambda k, s: (0, 0)),
            ],
            scratch_shapes=[pltpu.VMEM((D, rows), bf16), pltpu.VMEM((rows, D), f32)],
        ),
        out_shape=[
            sds(4, D, D), sds(1, FF, dtype=f32), sds(rows, D, dtype=f32), sds(rows, D), sds(rows, D),
            sds(8, D, dtype=f32),
        ],
        name="feed_down",
        **params(9 * 10**9, 24 * 10**6),
    )(info, dz, slope, n2, h, w_fc1, w_fc2, w_proj, vec)


def out_kernel(info, gl_ref, w2_ref, h_ref, vec_ref, out_ref, acc):
    step = pl.program_id(0)

    @pl.when(step == 0)
    def _():
        acc[...] = h_ref[...]

    acc[...] += dot(gl_ref[...], w2_ref[...])

    @pl.when(step == pl.num_programs(0) - 1)
    def _():
        for k, mask in enumerate(masks(info, out_ref.shape[0])):
            at = slice(TP * k, TP * k + TP)
            y = (mask * (acc[at] + vec_ref[7:8])).astype(bf16)
            out_ref[k] = dot(gather_rows(), y).astype(bf16)


def feed_out(info, gl, w_fc2, h, vec):
    rows = gl.shape[0]
    windows = rows // TP
    step = D
    return pl.pallas_call(
        out_kernel,
        grid_spec=pltpu.PrefetchScalarGridSpec(
            num_scalar_prefetch=1,
            grid=(FF // step,),
            in_specs=[
                pl.BlockSpec((rows, step), lambda k, s: (0, k)),
                pl.BlockSpec((step, D), lambda k, s: (k, 0)),
                whole(h), whole(vec),
            ],
            out_specs=pl.BlockSpec((windows, TOKW, D), lambda k, s: (0, 0, 0)),
            scratch_shapes=[pltpu.VMEM((rows, D), f32)],
        ),
        out_shape=sds(windows, TOKW, D),
        name="feed_out",
        **params(3 * 10**9, 12 * 10**6),
    )(info, gl, w_fc2, h, vec)


def key_rows():
    lane, col = iota((64, TP), 0), iota((64, TP), 1)
    i, j = col >> 4, col & 15
    hit = ((lane < WS) & (lane == i)) | ((lane >= 32) & (lane < 32 + WS) & (lane - 32 == 13 - j))
    return hit.astype(f32).astype(bf16)


def grad_rolls(table, base):
    lane = iota((16, 128), 1)
    out = []
    for i in range(WS):
        tile = table[16 * i : 16 * i + 16]
        by_row = jnp.where((lane >= base) & (lane < base + WS), tile, 0.0)
        by_row = pltpu.roll(by_row, 13 - i, 1) if i < 13 else by_row
        by_col = jnp.where((lane >= base + 32) & (lane < base + 32 + WS), tile, 0.0)
        out.append(by_row + pltpu.roll(by_col, 0, 1, stride=1, stride_axis=0))
    return jnp.concatenate(out, axis=0)


def back_kernel(qkv_ref, pt_ref, do_ref, tab_ref, dqkv_ref, table_ref, sums_ref):
    @pl.when(pl.program_id(0) == 0)
    def _():
        table_ref[...] = jnp.zeros_like(table_ref)
        sums_ref[...] = jnp.zeros_like(sums_ref)

    rows_extra = key_rows()
    lane = iota((TP, 128), 1)
    for pair in range(HEADS // 2):
        at = 128 * pair
        q = qkv_ref[0, :, at : at + 128]
        key_t = (qkv_ref[0, :, D + at : D + at + 128] * jnp.asarray(0.125, bf16)).T
        v = qkv_ref[0, :, 2 * D + at : 2 * D + at + 128]
        do = do_ref[0, :, at : at + 128]
        ds_all, dq_all, z_all = [], [], []
        for head in range(2):
            p_t = pt_ref[0, 2 * pair + head].astype(f32)
            dp_t = dot_nt(v, do * lane_mask(head))
            mean = jnp.sum(p_t * dp_t, axis=0, keepdims=True) / jnp.sum(p_t, axis=0, keepdims=True)
            ds_t = (p_t * (dp_t - mean)).astype(bf16)
            ds_all.append(ds_t)
            if head == 0:
                left = jnp.concatenate([key_t[:HD], rows_extra], axis=0)
            else:
                left = jnp.concatenate([rows_extra, key_t[HD:]], axis=0)
            back = dot(left, ds_t).T
            dq_all.append(back)
            z_all.append(grad_rolls(back, 64 if head == 0 else 0))
        z = jnp.where(lane < HD, z_all[1], z_all[0]).astype(bf16)
        dq = jnp.where(lane < HD, dq_all[0], dq_all[1]) + dot(z, tab_ref[...])
        table_ref[...] += dot(z.T, q)
        two = lambda a: jnp.concatenate([a * lane_mask(0), a * lane_mask(1)], axis=0)
        dk = dot(jnp.concatenate(ds_all, axis=1), two(q)) * 0.125
        p_two = jnp.concatenate([pt_ref[0, 2 * pair], pt_ref[0, 2 * pair + 1]], axis=1)
        dv = dot(p_two, two(do))
        dqkv_ref[0, :, at : at + 128] = dq.astype(bf16)
        dqkv_ref[0, :, D + at : D + at + 128] = dk.astype(bf16)
        dqkv_ref[0, :, 2 * D + at : 2 * D + at + 128] = dv.astype(bf16)
    sums_ref[...] += jnp.sum(dqkv_ref[0].astype(f32), axis=0, keepdims=True)


def backward_attention(qkv, p_t, do, tab):
    windows = qkv.shape[0]
    one = lambda *tail: pl.BlockSpec((1,) + tail, lambda k: (k,) + (0,) * len(tail))
    return pl.pallas_call(
        back_kernel,
        grid=(windows,),
        in_specs=[one(TP, 3 * D), one(HEADS, TP, TP), one(TP, D), whole(tab)],
        out_specs=[
            one(TP, 3 * D),
            pl.BlockSpec((128, 128), lambda k: (0, 0)),
            pl.BlockSpec((1, 3 * D), lambda k: (0, 0)),
        ],
        out_shape=[sds(windows, TP, 3 * D), sds(128, 128, dtype=f32), sds(1, 3 * D, dtype=f32)],
        name="attention_backward",
        **params(8 * 10**9, 16 * 10**6),
    )(qkv, p_t, do, tab)


def last_kernel(
    info, n1_ref, dqkv_ref, o_ref, da_ref, wqkv_ref, xpad_ref, dh_ref, vec_ref,
    grad_ref, dx_ref, sums_ref, n1_t, o_t, acc,
):
    step = pl.program_id(0)

    @pl.when(step == 0)
    def _():
        n1_t[...] = n1_ref[...].T
        o_t[...] = o_ref[...].T
        acc[...] = jnp.zeros_like(acc)

    dqkv = dqkv_ref[...]
    part = dot(n1_t[...], dqkv)
    proj = dot(o_t[...], da_ref[...])
    lane = iota((D, 128), 1) < 64
    low = lambda a: a.astype(bf16)
    grad_ref[0, :, 0:512] = low(part[:, 0:512])
    moved = pltpu.roll(proj[:, 0:256], 64, 1)
    grad_ref[0, :, 512:640] = low(jnp.where(lane, part[:, 512:640], moved[:, 0:128]))
    grad_ref[0, :, 640:768] = low(moved[:, 128:256])
    rolled = pltpu.roll(part[:, 512:1152], 576, 1)
    grad_ref[1, :, 0:512] = low(rolled[:, 0:512])
    grad_ref[1, :, 512:640] = low(jnp.where(lane, rolled[:, 512:640], proj[:, 128:256]))
    grad_ref[1, :, 640:768] = low(proj[:, 256:384])
    acc[...] += dot_nt(dqkv, wqkv_ref[...])

    @pl.when(step == pl.num_programs(0) - 1)
    def _():
        vec = vec_ref[...]
        gain = jnp.zeros((1, D), f32)
        shift = jnp.zeros((1, D), f32)
        for k, mask in enumerate(masks(info, dx_ref.shape[0])):
            at = slice(TP * k, TP * k + TP)
            dn = acc[at] * mask
            normed, scale_inv = norm_parts(xpad_ref[at].astype(f32))
            gain += jnp.sum(dn * normed, axis=0, keepdims=True)
            shift += jnp.sum(dn, axis=0, keepdims=True)
            dx = dh_ref[at] + norm_back(dn * vec[0:1], normed, scale_inv)
            dx_ref[k] = dot(gather_rows(), dx.astype(bf16)).astype(bf16)
        sums_ref[0:1] = gain
        sums_ref[1:2] = shift
        sums_ref[2:8] = jnp.zeros((6, D), f32)


def backward_last(info, n1, dqkv, o, da, w_qkv, xpad, dh, vec):
    rows = n1.shape[0]
    windows = rows // TP
    wide = 3 * D // 2
    return pl.pallas_call(
        last_kernel,
        grid_spec=pltpu.PrefetchScalarGridSpec(
            num_scalar_prefetch=1,
            grid=(2,),
            in_specs=[
                whole(n1),
                pl.BlockSpec((rows, wide), lambda k, s: (0, k)),
                whole(o),
                pl.BlockSpec((rows, D // 2), lambda k, s: (0, k)),
                pl.BlockSpec((D, wide), lambda k, s: (0, k)),
                whole(xpad), whole(dh), whole(vec),
            ],
            out_specs=[
                pl.BlockSpec((2, D, D), lambda k, s: (k, 0, 0)),
                pl.BlockSpec((windows, TOKW, D), lambda k, s: (0, 0, 0)),
                pl.BlockSpec((8, D), lambda k, s: (0, 0)),
            ],
            scratch_shapes=[
                pltpu.VMEM((D, rows), bf16), pltpu.VMEM((D, rows), bf16), pltpu.VMEM((rows, D), f32),
            ],
        ),
        out_shape=[sds(4, D, D), sds(windows, TOKW, D), sds(8, D, dtype=f32)],
        name="backward_last",
        **params(6 * 10**9, 20 * 10**6),
    )(info, n1, dqkv, o, da, w_qkv, xpad, dh, vec)


def device_step(info, x_slots, prev, nxt, cot, w_qkv, w_proj, w_fc1, w_fc2, small):
    vec, b1, bias, tab_fwd, tab_bwd = prepare(small)
    xpad, n1, qkv, p_t, o, h, n2 = forward_attention(
        info, x_slots, prev, nxt, w_qkv, w_proj, vec, bias, tab_fwd
    )
    rows = xpad.shape[0] * TP
    flat = lambda a: a.reshape(rows, a.shape[2])
    gl, slope, grad_fc2, dz, sum_b2 = feed_up(info, flat(n2), cot, w_fc1, b1)
    grad_fc1, sum_b1, dh, da, do, sums_two = feed_down(
        info, dz, slope, flat(n2), flat(h), w_fc1, w_fc2, w_proj, vec
    )
    block_out = feed_out(info, gl, w_fc2, flat(h), vec)
    dqkv, table, sum_qkv = backward_attention(qkv, p_t, do.reshape(-1, TP, D), tab_bwd)
    grad_attn, dx, sums_one = backward_last(
        info, flat(n1), flat(dqkv), flat(o), da, w_qkv, flat(xpad), dh, vec
    )
    rel_h = (table[0:RELN, 64:] + table[64 : 64 + RELN, :64])[::-1]
    rel_w = table[32 : 32 + RELN, 64:] + table[96 : 96 + RELN, :64]
    small_grad = jnp.concatenate(
        [
            sums_one[0], sums_two[0], sums_one[1], sums_two[1], sum_qkv[0, :D], sum_qkv[0, 2 * D :],
            sums_two[2], sum_b2[0], sum_b1[0], rel_h.reshape(-1), rel_w.reshape(-1),
        ]
    )
    return block_out, dx, grad_fc2, grad_fc1, grad_attn, small_grad


def slots_kernel(info, dx_ref, prev_ref, next_ref, out_ref):
    source = info[pl.program_id(0), 1]
    zero = jnp.zeros_like(dx_ref[0])
    out_ref[0] = jnp.where(
        source == 0,
        dx_ref[0],
        jnp.where(source == 1, prev_ref[0], jnp.where(source == 2, next_ref[0], zero)),
    )


def to_slots(info, dx, prev, nxt):
    slots = info.shape[0]
    return pl.pallas_call(
        slots_kernel,
        grid_spec=pltpu.PrefetchScalarGridSpec(
            num_scalar_prefetch=1,
            grid=(slots,),
            in_specs=[pl.BlockSpec((1, TOKW, D), lambda k, s: (s[k, 0], 0, 0)), whole(prev), whole(nxt)],
            out_specs=pl.BlockSpec((1, TOKW, D), lambda k, s: (k, 0, 0)),
        ),
        out_shape=sds(slots, TOKW, D),
        name="to_slots",
        **params(10**6, 3 * 10**6),
    )(info, dx, prev, nxt)


AXES = ("win", "grp")


def bits_of(size):
    return [1 << k for k in range(size.bit_length() - 1)]


def flipped(axis, bit):
    wins, grps = lax.axis_size("win"), lax.axis_size("grp")
    out = []
    for d in range(wins * grps):
        w, g = divmod(d, grps)
        w, g = (w ^ bit, g) if axis == "win" else (w, g ^ bit)
        out.append((d, w * grps + g))
    return out


def windows_before(count):
    total, before = count, jnp.zeros_like(count)
    for axis in ("grp", "win"):
        for bit in bits_of(lax.axis_size(axis)):
            other = lax.ppermute(total, AXES, flipped(axis, bit))
            mine = (lax.axis_index(axis) & bit) != 0
            before = before + jnp.where(mine, other, 0)
            total = total + other
    return before


def neighbours(last, first):
    count = lax.axis_size("win") * lax.axis_size("grp")
    up = [(i, i + 1) for i in range(count - 1)]
    down = [(j, i) for i, j in up]
    return lax.ppermute(last, AXES, up), lax.ppermute(first, AXES, down)


def rising():
    return [(axis, bit) for axis in ("grp", "win") for bit in bits_of(lax.axis_size(axis))]


def reduce_scatter(grad, order):
    rows, columns = grad.shape[2:]
    parts = [
        (axis, bit) for axis in ("grp", "win") for bit in reversed(bits_of(lax.axis_size(axis)))
    ]
    kept = grad.reshape((2,) * len(parts) + (rows, columns))
    came = None
    for axis, bit in order:
        at = parts.index((axis, bit))
        mine = ((lax.axis_index(axis) & bit) != 0).astype(jnp.int32)

        def pick(half):
            piece = lax.dynamic_index_in_dim(kept, half, at, keepdims=False)
            if came is None:
                return piece
            other = lax.dynamic_index_in_dim(came, half, at, keepdims=False)
            return (piece.astype(f32) + other.astype(f32)).astype(bf16)

        send, kept = pick(1 - mine), pick(mine)
        came = lax.ppermute(send, AXES, flipped(axis, bit))
        parts.pop(at)
    return kept.astype(f32) + came.astype(f32)


def gather_win(block, order):
    have = block[None]
    for axis, bit in order:
        have = jnp.concatenate([have, lax.ppermute(have, AXES, flipped(axis, bit))], axis=0)
    place = lax.axis_index("win")
    out = []
    for target in range(have.shape[0]):
        apart = place ^ target
        at = sum(jnp.where((apart & bit) != 0, 1 << k, 0) for k, (_, bit) in enumerate(order))
        out.append(lax.dynamic_index_in_dim(have, at, 0, keepdims=False))
    return jnp.stack(out)


def adam_step(parameter, gradient, moment, square):
    first_fix = 1.0 - jnp.power(jnp.float32(0.5), jnp.float32(STEP))
    second_fix = 1.0 - jnp.power(jnp.float32(0.999), jnp.float32(STEP))
    moment_next = 0.5 * moment + 0.5 * gradient
    square_next = 0.999 * square + 0.001 * gradient * gradient
    fresh_weight = parameter - learn_rate * (moment_next / first_fix) / (
        jnp.sqrt(square_next / second_fix) + 1e-08
    )
    return (moment_next, square_next, fresh_weight.astype(bf16))


def per_device(
    x_slots, counts, cotangent, w_qkv, w_proj, w_fc1, w_fc2, small_params,
    moment_qkv, moment_proj, moment_fc1, moment_fc2, moment_small,
    square_qkv, square_proj, square_fc1, square_fc2, square_small,
):
    slots, per_even = x_slots.shape[0], cotangent.shape[0]
    win_at, grp_at = lax.axis_index("win"), lax.axis_index("grp")
    wins, grps = lax.axis_size("win"), lax.axis_size("grp")
    base = (win_at * grps + grp_at) * per_even
    count = counts[0]
    prev, nxt = neighbours(lax.dynamic_slice_in_dim(x_slots, count - 1, 1, 0), x_slots[:1])
    offset = windows_before(counts)[0]
    window = base + jnp.arange(per_even, dtype=jnp.int32)
    slot = window - offset
    spot = window % (GRID * GRID)
    info = jnp.stack(
        [
            jnp.clip(slot, 0, slots - 1),
            jnp.where(slot < 0, 1, jnp.where(slot >= count, 2, 0)),
            SIDE - WS * (spot // GRID),
            SIDE - WS * (spot % GRID),
        ],
        axis=1,
    ).astype(jnp.int32)
    block_out, dx, grad_fc2, grad_fc1, grad_attn, small_grad = device_step(
        info, x_slots, prev, nxt, cotangent, w_qkv, w_proj, w_fc1, w_fc2, small_params
    )
    dx_prev, dx_next = neighbours(dx[per_even - 1 :], dx[:1])
    place = offset + jnp.arange(slots, dtype=jnp.int32) - base
    live = jnp.arange(slots) < count
    back = jnp.where(place < 0, 1, jnp.where(place >= per_even, 2, 0))
    back = jnp.stack([jnp.clip(place, 0, per_even - 1), jnp.where(live, back, 3)], axis=1)
    input_grad = to_slots(back.astype(jnp.int32), dx, dx_prev, dx_next)

    blocks = lambda grad: grad.reshape(grps, wins, D // wins, D)
    fc2_blocks = grad_fc2
    if wins != grad_fc2.shape[1]:
        flat = grad_fc2.transpose(0, 2, 1, 3).reshape(grps, D // grps, wins, FF // wins)
        fc2_blocks = flat.transpose(0, 2, 1, 3)
    part_d = reduce_scatter(fc2_blocks, rising()).T
    part_c = reduce_scatter(blocks(grad_fc1), rising())
    part_ab = reduce_scatter(blocks(grad_attn), rising())
    part_a, part_b = part_ab[:, : 3 * D // grps], part_ab[:, 3 * D // grps :]
    grad_small = lax.psum(small_grad, AXES)

    def owned_part(weight, piece):
        return lax.dynamic_slice(
            weight, (win_at * piece.shape[0], grp_at * piece.shape[1]), piece.shape
        ).astype(f32)

    upd_qkv = adam_step(owned_part(w_qkv, part_a), part_a, moment_qkv, square_qkv)
    upd_proj = adam_step(owned_part(w_proj, part_b), part_b, moment_proj, square_proj)
    upd_fc1 = adam_step(owned_part(w_fc1, part_c), part_c, moment_fc1, square_fc1)
    upd_fc2 = adam_step(owned_part(w_fc2, part_d), part_d, moment_fc2, square_fc2)
    upd_small = adam_step(small_params.astype(f32), grad_small, moment_small, square_small)
    order = [one for one in reversed(rising()) if one[0] == "win"]
    new_fc2 = gather_win(upd_fc2[2].T, order).transpose(0, 2, 1).reshape(FF, D // grps)
    new_fc1 = gather_win(upd_fc1[2], order).reshape(D, FF // grps)
    both = gather_win(jnp.concatenate([upd_qkv[2], upd_proj[2]], axis=1), order).reshape(D, D)
    new_qkv, new_proj = both[:, : 3 * D // grps], both[:, 3 * D // grps :]
    return (
        block_out, input_grad, part_a, part_b, part_c, part_d, grad_small,
        upd_qkv[0], upd_proj[0], upd_fc1[0], upd_fc2[0], upd_small[0],
        upd_qkv[1], upd_proj[1], upd_fc1[1], upd_fc2[1], upd_small[1],
        new_qkv, new_proj, new_fc1, new_fc2, upd_small[2],
    )


def solution(mesh):
    data, shard, same, part = P(AXES, None, None), P("win", "grp"), P(), P(None, "grp")
    in_specs = (data, P(AXES), data) + (same,) * 5 + ((shard,) * 4 + (same,)) * 2
    out_specs = (data,) * 2 + ((shard,) * 4 + (same,)) * 3 + (part,) * 4 + (same,)
    return jax.shard_map(
        per_device, mesh=mesh, in_specs=in_specs, out_specs=out_specs, check_vma=False
    )
```

```python
import functools

import jax
import jax.numpy as jnp
from jax import lax
from jax.experimental import pallas as pl
from jax.experimental.pallas import tpu as pltpu
from jax.sharding import PartitionSpec as P

D = 768
HEADS = 12
HD = 64
FF = 3072
WS = 14
SIDE = 64
STEP = 4
TOKW = 196
GRID = 5
RELN = 27
TP = 224

root_half = 0.7071067811865476
inv_root_two_pi = 0.3989422804014327
learn_rate = 0.06
bf16 = jnp.bfloat16
f32 = jnp.float32
VMEM_LIMIT = 56 << 20


def dot(a, b):
    return lax.dot_general(a, b, (((1,), (0,)), ((), ())), preferred_element_type=f32)


def dot_nt(a, b):
    return lax.dot_general(a, b, (((1,), (1,)), ((), ())), preferred_element_type=f32)


def dot_tn(a, b):
    return lax.dot_general(a, b, (((0,), (0,)), ((), ())), preferred_element_type=f32)


def iota(shape, axis):
    return lax.broadcasted_iota(jnp.int32, shape, axis)


def spread():
    row, token = iota((TP, TOKW), 0), iota((TP, TOKW), 1)
    hit = ((row & 15) < WS) & (token == WS * (row >> 4) + (row & 15))
    return hit.astype(f32).astype(bf16)


def gather_rows():
    token, row = iota((TOKW, TP), 0), iota((TOKW, TP), 1)
    hit = ((row & 15) < WS) & (token == WS * (row >> 4) + (row & 15))
    return hit.astype(f32).astype(bf16)


def key_lanes():
    row, lane = iota((TP, 128), 0), iota((TP, 128), 1)
    i, j = row >> 4, row & 15
    low = lane & 31
    hit = (low < WS) & (((lane < 64) & (low == i)) | ((lane >= 64) & (low == j)))
    shut = (lane == 127) & (j >= WS)
    return jnp.where(shut, -1e30, hit.astype(f32)).astype(bf16)


def inside(limit_row, limit_col):
    row = iota((TP, 1), 0)
    i, j = row >> 4, row & 15
    return ((i < limit_row) & (j < jnp.minimum(limit_col, WS))).astype(f32)


def norm_parts(v):
    centered = v - jnp.mean(v, axis=-1, keepdims=True)
    scale_inv = lax.rsqrt(jnp.mean(centered * centered, axis=-1, keepdims=True) + 1e-06)
    return centered * scale_inv, scale_inv


def norm_back(e, normed, scale_inv):
    return scale_inv * (
        e
        - jnp.mean(e, axis=-1, keepdims=True)
        - normed * jnp.mean(e * normed, axis=-1, keepdims=True)
    )


def lane_mask(head):
    lane = iota((1, 128), 1)
    return ((lane < HD) if head == 0 else (lane >= HD)).astype(f32).astype(bf16)


def query_rolls(table):
    lane = iota((16, 128), 1)
    out = []
    for i in range(WS):
        tile = table[16 * i : 16 * i + 16]
        by_row = pltpu.roll(tile, 51 + i, 1)
        by_col = pltpu.roll(tile, 51, 1, stride=1, stride_axis=0)
        kept = jnp.where(lane < WS, by_row, 0.0)
        out.append(jnp.where((lane >= 64) & (lane < 64 + WS), by_col, kept))
    return jnp.concatenate(out, axis=0)


def query_lanes(table):
    aug = query_rolls(table)
    high = aug.astype(bf16).astype(f32)
    full = high + pltpu.roll(aug - high, 32, 1)
    return jnp.where(iota((TP, 128), 1) == 127, 1.0, full).astype(bf16)


def fwd_kernel(
    info, xs_ref, prev_ref, next_ref, wqkv_ref, wproj_ref, vec_ref, bias_ref, tab_ref,
    xpad_ref, n1_ref, qkv_ref, pt_ref, o_ref, h_ref, n2_ref,
):
    k = pl.program_id(0)
    source = info[k, 1]
    x = jnp.where(source == 0, xs_ref[0], jnp.where(source == 1, prev_ref[0], next_ref[0]))
    big = dot(spread(), x)
    xpad_ref[0] = big.astype(bf16)
    mask = inside(info[k, 2], info[k, 3])
    vec = vec_ref[...]
    normed, _ = norm_parts(big)
    n1 = (mask * (normed * vec[0:1] + vec[2:3])).astype(bf16)
    n1_ref[0] = n1
    qkv_ref[0] = (dot(n1, wqkv_ref[...]) + bias_ref[...]).astype(bf16)
    keys_extra = key_lanes()
    for pair in range(HEADS // 2):
        at = 128 * pair
        q = qkv_ref[0, :, at : at + 128]
        key = jnp.concatenate([qkv_ref[0, :, D + at : D + at + 128], keys_extra], axis=1)
        v_t = qkv_ref[0, :, 2 * D + at : 2 * D + at + 128].T
        tables = dot(q, tab_ref[...])
        outs = []
        for head in range(2):
            extra = query_lanes(tables[:, 128 * head : 128 * head + 128])
            q_all = jnp.concatenate([q * (lane_mask(head) * 0.125), extra], axis=1)
            s_t = dot_nt(key, q_all)
            e = jnp.exp(s_t - jnp.max(s_t, axis=0, keepdims=True))
            p_t = (e * (1.0 / jnp.sum(e, axis=0, keepdims=True))).astype(bf16)
            pt_ref[0, 2 * pair + head] = p_t
            outs.append(dot(v_t[HD * head : HD * head + HD], p_t))
        o_ref[0, :, at : at + 128] = jnp.concatenate(outs, axis=0).T.astype(bf16)
    a = dot(o_ref[0], wproj_ref[...]) + vec[6:7]
    h = mask * (big + a)
    h_ref[0] = h
    normed_two, _ = norm_parts(h)
    n2_ref[0] = (mask * (normed_two * vec[1:2] + vec[3:4])).astype(bf16)


def forward_attention(info, x_slots, prev, nxt, w_qkv, w_proj, vec, bias, tab):
    windows = info.shape[0]
    one = lambda *tail: pl.BlockSpec((1,) + tail, lambda k, s: (k,) + (0,) * len(tail))
    whole = lambda a: pl.BlockSpec(a.shape, lambda k, s: (0,) * a.ndim)
    shape = lambda *tail, dtype=bf16: jax.ShapeDtypeStruct((windows,) + tail, dtype)
    return pl.pallas_call(
        fwd_kernel,
        grid_spec=pltpu.PrefetchScalarGridSpec(
            num_scalar_prefetch=1,
            grid=(windows,),
            in_specs=[
                pl.BlockSpec((1, TOKW, D), lambda k, s: (s[k, 0], 0, 0)),
                whole(prev), whole(nxt), whole(w_qkv), whole(w_proj), whole(vec), whole(bias), whole(tab),
            ],
            out_specs=[
                one(TP, D), one(TP, D), one(TP, 3 * D), one(HEADS, TP, TP), one(TP, D), one(TP, D), one(TP, D),
            ],
        ),
        out_shape=[
            shape(TP, D), shape(TP, D), shape(TP, 3 * D), shape(HEADS, TP, TP), shape(TP, D),
            shape(TP, D, dtype=f32), shape(TP, D),
        ],
        compiler_params=pltpu.CompilerParams(vmem_limit_bytes=VMEM_LIMIT),
        cost_estimate=pl.CostEstimate(flops=0, bytes_accessed=0, transcendentals=0),
        name="attention_forward",
    )(info, x_slots, prev, nxt, w_qkv, w_proj, vec, bias, tab)


def prepare(small):
    s = small.astype(f32)
    vec = s[: 8 * D].reshape(8, D)
    first_bias = s[8 * D : 8 * D + FF].reshape(1, FF)
    bias = jnp.concatenate([vec[4:5], jnp.zeros((1, D), f32), vec[5:6]], axis=1)
    tables = small[8 * D + FF :].reshape(2, RELN, HD)
    back_h, back_w, rel_w = tables[0, ::-1], tables[1, ::-1], tables[1]
    gap = jnp.zeros((64 - RELN, HD), bf16)
    one = jnp.concatenate([back_w, gap, back_h, gap], axis=0)
    none = jnp.zeros_like(one)
    fwd = jnp.block([[one.T, none.T], [none.T, one.T]])
    short = jnp.zeros((32 - RELN, HD), bf16)
    half = jnp.concatenate([back_h, short, rel_w, short], axis=0)
    nil = jnp.zeros_like(half)
    bwd = jnp.block([[nil, half], [half, nil]])
    return vec, first_bias, bias, fwd, bwd


def params(**more):
    return dict(
        compiler_params=pltpu.CompilerParams(vmem_limit_bytes=VMEM_LIMIT),
        cost_estimate=pl.CostEstimate(flops=0, bytes_accessed=0, transcendentals=0),
        **more,
    )


def whole(a):
    return pl.BlockSpec(a.shape, lambda k, *s: (0,) * a.ndim)


def sds(*dims, dtype=bf16):
    return jax.ShapeDtypeStruct(dims, dtype)


def masks(info, windows):
    return [inside(info[k, 2], info[k, 3]) for k in range(windows)]


def up_kernel(info, core, n2_ref, cot_ref, w1_ref, b1_ref, gl_ref, slope_ref, keep_ref, send_ref, dz_ref, b2_ref, dz_t):
    windows = cot_ref.shape[0]

    @pl.when(pl.program_id(0) == 0)
    def _():
        total = jnp.zeros((1, D), f32)
        for k, mask in enumerate(masks(info, windows)):
            part = dot(spread(), cot_ref[k]) * mask
            dz_ref[TP * k : TP * k + TP] = part.astype(bf16)
            total += jnp.sum(part, axis=0, keepdims=True)
        b2_ref[...] = total
        dz_t[...] = dz_ref[...].T

    u = dot(n2_ref[...], w1_ref[...]) + b1_ref[...]
    half = 0.5 * (1.0 + lax.erf(u * root_half))
    gl = (u * half).astype(bf16)
    gl_ref[...] = gl
    slope_ref[...] = (half + u * jnp.exp(-0.5 * u * u) * inv_root_two_pi).astype(bf16)
    grad = dot(dz_t[...], gl).astype(bf16)
    even = core[0] == 0
    rows, cols = keep_ref.shape[2:]
    for y in range(keep_ref.shape[0]):
        for w in range(keep_ref.shape[1]):
            at = slice(cols * w, cols * w + cols)
            first = grad[2 * rows * y : 2 * rows * y + rows, at]
            second = grad[2 * rows * y + rows : 2 * rows * y + 2 * rows, at]
            keep_ref[y, w] = jnp.where(even, first, second)
            send_ref[y, w] = jnp.where(even, second, first)


def feed_up(info, core, n2, cot, w_fc1, b1):
    rows = n2.shape[0]
    step = D
    steps = FF // step
    flat = pl.BlockSpec((rows, step), lambda k, *s: (0, k))
    half = pl.BlockSpec((2, 2, 192, 384), lambda k, *s: (0, k, 0, 0))
    return pl.pallas_call(
        up_kernel,
        grid_spec=pltpu.PrefetchScalarGridSpec(
            num_scalar_prefetch=2,
            grid=(steps,),
            in_specs=[
                whole(n2), whole(cot),
                pl.BlockSpec((D, step), lambda k, *s: (0, k)),
                pl.BlockSpec((1, step), lambda k, *s: (0, k)),
            ],
            out_specs=[
                flat, flat, half, half,
                pl.BlockSpec((rows, D), lambda k, *s: (0, 0)),
                pl.BlockSpec((1, D), lambda k, *s: (0, 0)),
            ],
            scratch_shapes=[pltpu.VMEM((D, rows), bf16)],
        ),
        out_shape=[
            sds(rows, FF), sds(rows, FF), sds(2, 8, 192, 384), sds(2, 8, 192, 384), sds(rows, D),
            sds(1, D, dtype=f32),
        ],
        name="feed_up",
        **params(),
    )(info, core, n2, cot, w_fc1, b1)


def down_kernel(
    info, core, dz_ref, slope_ref, n2_ref, w1_ref, w2_ref, h_ref, wproj_ref, vec_ref,
    keep_ref, send_ref, b1_ref, dh_ref, da_ref, do_ref, sums_ref, n2_t, acc,
):
    step = pl.program_id(0)

    @pl.when(step == 0)
    def _():
        n2_t[...] = n2_ref[...].T
        acc[...] = jnp.zeros_like(acc)

    du = dot_nt(dz_ref[...], w2_ref[...]) * slope_ref[...].astype(f32)
    du_low = du.astype(bf16)
    b1_ref[...] = jnp.sum(du_low.astype(f32), axis=0, keepdims=True)
    mine = (step & 1) == core[0]
    grad = dot(n2_t[...], du_low).astype(bf16)

    @pl.when(mine)
    def _():
        keep_ref[0] = grad

    @pl.when(jnp.logical_not(mine))
    def _():
        send_ref[0] = grad

    acc[...] += dot_nt(du_low, w1_ref[...])

    @pl.when(step == pl.num_programs(0) - 1)
    def _():
        vec = vec_ref[...]
        windows = acc.shape[0] // TP
        gain = jnp.zeros((1, D), f32)
        shift = jnp.zeros((1, D), f32)
        bias = jnp.zeros((1, D), f32)
        for k, mask in enumerate(masks(info, windows)):
            at = slice(TP * k, TP * k + TP)
            dn = acc[at] * mask
            normed, scale_inv = norm_parts(h_ref[at])
            gain += jnp.sum(dn * normed, axis=0, keepdims=True)
            shift += jnp.sum(dn, axis=0, keepdims=True)
            dh = mask * (dz_ref[at].astype(f32) + norm_back(dn * vec[1:2], normed, scale_inv))
            dh_ref[at] = dh
            da = dh.astype(bf16)
            da_ref[at] = da
            bias += jnp.sum(da.astype(f32), axis=0, keepdims=True)
            do_ref[at] = dot_nt(da, wproj_ref[...]).astype(bf16)
        sums_ref[0:1] = gain
        sums_ref[1:2] = shift
        sums_ref[2:3] = bias
        sums_ref[3:8] = jnp.zeros((5, D), f32)


def feed_down(info, core, dz, slope, n2, h, w_fc1, w_fc2, w_proj, vec):
    rows = n2.shape[0]
    step = D
    half = pl.BlockSpec((1, D, step), lambda k, *s: (k // 2, 0, 0))
    flat = pl.BlockSpec((rows, D), lambda k, *s: (0, 0))
    return pl.pallas_call(
        down_kernel,
        grid_spec=pltpu.PrefetchScalarGridSpec(
            num_scalar_prefetch=2,
            grid=(FF // step,),
            in_specs=[
                whole(dz),
                pl.BlockSpec((rows, step), lambda k, *s: (0, k)),
                whole(n2),
                pl.BlockSpec((D, step), lambda k, *s: (0, k)),
                pl.BlockSpec((step, D), lambda k, *s: (k, 0)),
                whole(h), whole(w_proj), whole(vec),
            ],
            out_specs=[
                half, half,
                pl.BlockSpec((1, step), lambda k, *s: (0, k)),
                flat, flat, flat,
                pl.BlockSpec((8, D), lambda k, *s: (0, 0)),
            ],
            scratch_shapes=[pltpu.VMEM((D, rows), bf16), pltpu.VMEM((rows, D), f32)],
        ),
        out_shape=[
            sds(2, D, D), sds(2, D, D), sds(1, FF, dtype=f32), sds(rows, D, dtype=f32), sds(rows, D),
            sds(rows, D), sds(8, D, dtype=f32),
        ],
        name="feed_down",
        **params(),
    )(info, core, dz, slope, n2, w_fc1, w_fc2, h, w_proj, vec)


def out_kernel(info, gl_ref, w2_ref, h_ref, vec_ref, out_ref, acc):
    step = pl.program_id(0)

    @pl.when(step == 0)
    def _():
        acc[...] = h_ref[...]

    acc[...] += dot(gl_ref[...], w2_ref[...])

    @pl.when(step == pl.num_programs(0) - 1)
    def _():
        for k, mask in enumerate(masks(info, out_ref.shape[0])):
            at = slice(TP * k, TP * k + TP)
            y = (mask * (acc[at] + vec_ref[7:8])).astype(bf16)
            out_ref[k] = dot(gather_rows(), y).astype(bf16)


def feed_out(info, gl, w_fc2, h, vec):
    rows = gl.shape[0]
    windows = rows // TP
    step = D
    return pl.pallas_call(
        out_kernel,
        grid_spec=pltpu.PrefetchScalarGridSpec(
            num_scalar_prefetch=1,
            grid=(FF // step,),
            in_specs=[
                pl.BlockSpec((rows, step), lambda k, s: (0, k)),
                pl.BlockSpec((step, D), lambda k, s: (k, 0)),
                whole(h), whole(vec),
            ],
            out_specs=pl.BlockSpec((windows, TOKW, D), lambda k, s: (0, 0, 0)),
            scratch_shapes=[pltpu.VMEM((rows, D), f32)],
        ),
        out_shape=sds(windows, TOKW, D),
        name="feed_out",
        **params(),
    )(info, gl, w_fc2, h, vec)


def key_rows():
    lane, col = iota((64, TP), 0), iota((64, TP), 1)
    i, j = col >> 4, col & 15
    hit = ((lane < WS) & (lane == i)) | ((lane >= 32) & (lane < 32 + WS) & (lane - 32 == 13 - j))
    return hit.astype(f32).astype(bf16)


def grad_rolls(table, base):
    lane = iota((16, 128), 1)
    out = []
    for i in range(WS):
        tile = table[16 * i : 16 * i + 16]
        by_row = jnp.where((lane >= base) & (lane < base + WS), tile, 0.0)
        by_row = pltpu.roll(by_row, 13 - i, 1) if i < 13 else by_row
        by_col = jnp.where((lane >= base + 32) & (lane < base + 32 + WS), tile, 0.0)
        out.append(by_row + pltpu.roll(by_col, 0, 1, stride=1, stride_axis=0))
    return jnp.concatenate(out, axis=0)


def back_kernel(qkv_ref, pt_ref, do_ref, tab_ref, *refs):
    dqkv_ref, table_ref, sums_ref = refs[-3:]

    @pl.when(pl.program_id(0) == 0)
    def _():
        table_ref[...] = jnp.zeros_like(table_ref)
        sums_ref[...] = jnp.zeros_like(sums_ref)

    rows_extra = key_rows()
    lane = iota((TP, 128), 1)
    for pair in range(HEADS // 2):
        at = 128 * pair
        q = qkv_ref[0, :, at : at + 128]
        key_t = (qkv_ref[0, :, D + at : D + at + 128] * jnp.asarray(0.125, bf16)).T
        v = qkv_ref[0, :, 2 * D + at : 2 * D + at + 128]
        do = do_ref[0, :, at : at + 128]
        ds_all, dq_all, z_all = [], [], []
        for head in range(2):
            p_t = pt_ref[0, 2 * pair + head].astype(f32)
            dp_t = dot_nt(v, do * lane_mask(head))
            mean = jnp.sum(p_t * dp_t, axis=0, keepdims=True) / jnp.sum(p_t, axis=0, keepdims=True)
            ds_t = (p_t * (dp_t - mean)).astype(bf16)
            ds_all.append(ds_t)
            if head == 0:
                left = jnp.concatenate([key_t[:HD], rows_extra], axis=0)
            else:
                left = jnp.concatenate([rows_extra, key_t[HD:]], axis=0)
            back = dot(left, ds_t).T
            dq_all.append(back)
            z_all.append(grad_rolls(back, 64 if head == 0 else 0))
        z = jnp.where(lane < HD, z_all[1], z_all[0]).astype(bf16)
        dq = jnp.where(lane < HD, dq_all[0], dq_all[1]) + dot(z, tab_ref[...])
        table_ref[...] += dot(z.T, q)
        two = lambda a: jnp.concatenate([a * lane_mask(0), a * lane_mask(1)], axis=0)
        dk = dot(jnp.concatenate(ds_all, axis=1), two(q)) * 0.125
        p_two = jnp.concatenate([pt_ref[0, 2 * pair], pt_ref[0, 2 * pair + 1]], axis=1)
        dv = dot(p_two, two(do))
        dqkv_ref[0, :, at : at + 128] = dq.astype(bf16)
        dqkv_ref[0, :, D + at : D + at + 128] = dk.astype(bf16)
        dqkv_ref[0, :, 2 * D + at : 2 * D + at + 128] = dv.astype(bf16)
    sums_ref[...] += jnp.sum(dqkv_ref[0].astype(f32), axis=0, keepdims=True)


def backward_attention(qkv, p_t, do, tab, begin, count, into=None):
    windows = qkv.shape[0]
    one = lambda *tail: pl.BlockSpec((1,) + tail, lambda k: (k + begin,) + (0,) * len(tail))
    inputs = [qkv, p_t, do, tab]
    in_specs = [one(TP, 3 * D), one(HEADS, TP, TP), one(TP, D), whole(tab)]
    if into is not None:
        inputs.append(into)
        in_specs.append(pl.BlockSpec(memory_space=pl.ANY))
    return pl.pallas_call(
        back_kernel,
        grid=(count,),
        in_specs=in_specs,
        out_specs=[
            one(TP, 3 * D),
            pl.BlockSpec((128, 128), lambda k: (0, 0)),
            pl.BlockSpec((1, 3 * D), lambda k: (0, 0)),
        ],
        out_shape=[sds(windows, TP, 3 * D), sds(128, 128, dtype=f32), sds(1, 3 * D, dtype=f32)],
        input_output_aliases={} if into is None else {4: 0},
        name="attention_backward",
        **params(),
    )(*inputs)


def weight_kernel(
    core, n1_ref, dqkv_ref, o_ref, da_ref, keep_ref, send_ref, n1_t, o_t
):
    @pl.when(pl.program_id(0) == 0)
    def _():
        n1_t[...] = n1_ref[...].T
        o_t[...] = o_ref[...].T

    part = dot(n1_t[...], dqkv_ref[...])
    proj = dot(o_t[...], da_ref[...])
    lane = iota((D, 128), 1) < 64
    even = core[0] == 0

    def put(at, first, second):
        first, second = first.astype(bf16), second.astype(bf16)
        keep_ref[0, :, at] = jnp.where(even, first, second)
        send_ref[0, :, at] = jnp.where(even, second, first)

    moved = pltpu.roll(proj[:, 0:256], 64, 1)
    rolled = pltpu.roll(part[:, 512:1152], 576, 1)
    put(slice(0, 512), part[:, 0:512], rolled[:, 0:512])
    put(
        slice(512, 640),
        jnp.where(lane, part[:, 512:640], moved[:, 0:128]),
        jnp.where(lane, rolled[:, 512:640], proj[:, 128:256]),
    )
    put(slice(640, 768), moved[:, 128:256], proj[:, 256:384])


def attention_weights(core, n1, dqkv, o, da):
    rows = n1.shape[0]
    wide = 3 * D // 2
    half = pl.BlockSpec((1, D, D), lambda k, *s: (k, 0, 0))
    return pl.pallas_call(
        weight_kernel,
        grid_spec=pltpu.PrefetchScalarGridSpec(
            num_scalar_prefetch=1,
            grid=(2,),
            in_specs=[
                whole(n1),
                pl.BlockSpec((rows, wide), lambda k, *s: (0, k)),
                whole(o),
                pl.BlockSpec((rows, D // 2), lambda k, *s: (0, k)),
            ],
            out_specs=[half] * 2,
            scratch_shapes=[pltpu.VMEM((D, rows), bf16), pltpu.VMEM((D, rows), bf16)],
        ),
        out_shape=[sds(2, D, D)] * 2,
        name="attention_weights",
        **params(),
    )(core, n1, dqkv, o, da)


def input_kernel(info, dqkv_ref, wqkv_ref, xpad_ref, dh_ref, vec_ref, dx_ref, sums_ref):
    vec = vec_ref[...]
    acc = dot_nt(dqkv_ref[...], wqkv_ref[...])
    k = pl.program_id(0)
    mask = inside(info[k, 2], info[k, 3])
    dn = acc * mask
    normed, scale_inv = norm_parts(xpad_ref[...].astype(f32))
    dx = dh_ref[...] + norm_back(dn * vec[0:1], normed, scale_inv)
    dx_ref[0] = dot(gather_rows(), dx.astype(bf16)).astype(bf16)

    @pl.when(k == 0)
    def _():
        sums_ref[...] = jnp.zeros_like(sums_ref)

    sums_ref[0:1] += jnp.sum(dn * normed, axis=0, keepdims=True)
    sums_ref[1:2] += jnp.sum(dn, axis=0, keepdims=True)


def input_gradient(info, dqkv, w_qkv, xpad, dh, vec):
    rows = xpad.shape[0]
    windows = rows // TP
    return pl.pallas_call(
        input_kernel,
        grid_spec=pltpu.PrefetchScalarGridSpec(
            num_scalar_prefetch=1,
            grid=(windows,),
            in_specs=[
                pl.BlockSpec((TP, 3 * D), lambda k, s: (k, 0)),
                whole(w_qkv),
                pl.BlockSpec((TP, D), lambda k, s: (k, 0)),
                pl.BlockSpec((TP, D), lambda k, s: (k, 0)),
                whole(vec),
            ],
            out_specs=[
                pl.BlockSpec((1, TOKW, D), lambda k, s: (k, 0, 0)),
                pl.BlockSpec((8, D), lambda k, s: (0, 0)),
            ],
        ),
        out_shape=[sds(windows, TOKW, D), sds(8, D, dtype=f32)],
        name="input_gradient",
        **params(),
    )(info, dqkv, w_qkv, xpad, dh, vec)


def slots_kernel(info, dx_ref, prev_ref, next_ref, out_ref):
    source = info[pl.program_id(0), 1]
    zero = jnp.zeros_like(dx_ref[0])
    out_ref[0] = jnp.where(
        source == 0,
        dx_ref[0],
        jnp.where(source == 1, prev_ref[0], jnp.where(source == 2, next_ref[0], zero)),
    )


def to_slots(info, dx, prev, nxt):
    slots = info.shape[0]
    return pl.pallas_call(
        slots_kernel,
        grid_spec=pltpu.PrefetchScalarGridSpec(
            num_scalar_prefetch=1,
            grid=(slots,),
            in_specs=[pl.BlockSpec((1, TOKW, D), lambda k, s: (s[k, 0], 0, 0)), whole(prev), whole(nxt)],
            out_specs=pl.BlockSpec((1, TOKW, D), lambda k, s: (k, 0, 0)),
        ),
        out_shape=sds(slots, TOKW, D),
        name="to_slots",
        **params(),
    )(info, dx, prev, nxt)


AXES = ("win", "grp")


def bits_of(size):
    return [1 << k for k in range(size.bit_length() - 1)]


def flipped(axis, bit):
    wins, grps = lax.axis_size("win"), lax.axis_size("grp")
    out = []
    for d in range(wins * grps):
        w, g = divmod(d, grps)
        w, g = (w ^ bit, g) if axis == "win" else (w, g ^ bit)
        out.append((d, w * grps + g))
    return out


def windows_before(count):
    total, before = count, jnp.zeros_like(count)
    for axis in ("grp", "win"):
        for bit in bits_of(lax.axis_size(axis)):
            other = lax.ppermute(total, AXES, flipped(axis, bit))
            mine = (lax.axis_index(axis) & bit) != 0
            before = before + jnp.where(mine, other, 0)
            total = total + other
    return before


def neighbours(last, first):
    count = lax.axis_size("win") * lax.axis_size("grp")
    up = [(i, i + 1) for i in range(count - 1)]
    down = [(j, i) for i, j in up]
    return lax.ppermute(last, AXES, up), lax.ppermute(first, AXES, down)


def rising():
    return [(axis, bit) for axis in ("grp", "win") for bit in bits_of(lax.axis_size(axis))]


def tie(value, *others):
    return lax.optimization_barrier((value, *others))[0]


def placed(have, order):
    place = lax.axis_index("win")
    out = []
    for target in range(have.shape[0]):
        apart = place ^ target
        at = sum(jnp.where((apart & bit) != 0, 1 << k, 0) for k, (_, bit) in enumerate(order))
        out.append(lax.dynamic_index_in_dim(have, at, 0, keepdims=False))
    return jnp.stack(out)


class Piece:
    def __init__(self, kept, came, parts):
        self.kept, self.came, self.parts = kept, came, parts

    def halve(self, which, at=None):
        axis, bit = which
        place = self.parts.index(which)
        parts = self.parts[:place] + self.parts[place + 1 :]
        mine = ((lax.axis_index(axis) & bit) != 0).astype(jnp.int32)
        split = (1 << place, 2, -1) + self.kept.shape[-2:]
        kept, came = self.kept.reshape(split), self.came.reshape(split)

        def pick(half):
            piece = lax.dynamic_index_in_dim(kept, half, 1, keepdims=False)
            other = lax.dynamic_index_in_dim(came, half, 1, keepdims=False)
            if at is not None:
                piece, other = piece[..., at[0], at[1]], other[..., at[0], at[1]]
            return (piece.astype(f32) + other.astype(f32)).astype(bf16)

        send, kept = pick(1 - mine), pick(mine)
        return send, Piece(kept, lax.ppermute(send, AXES, flipped(axis, bit)), parts)


class Chunk:
    def __init__(self, keep, send, axis, finish):
        near, *self.grp = [one for one in rising() if one[0] == "grp"]
        self.win = [one for one in rising() if one[0] == "win"]
        parts = list(reversed(self.grp)) + list(reversed(self.win))
        self.pieces = [Piece(keep, lax.ppermute(send, AXES, flipped(*near)), parts)]
        self.block, self.axis, self.finish = keep.shape[-2:], axis, finish
        self.cross = [(self.grp[-1], self.win[0]), (self.win[0], self.grp[-1])]
        self.order = self.grp[:-1] + self.win[1:]
        self.ways, self.back = list(reversed(self.win)), list(reversed(self.win))
        self.have = None

    def left(self):
        return bool(self.cross or self.order or self.ways)

    def after(self, *others):
        if others:
            for piece in self.pieces:
                piece.came = tie(piece.came, *others)

    def step(self, *others):
        self.after(*others)
        if self.cross:
            whole, half = slice(None), self.block[self.axis] // 2
            cuts = [slice(0, half), slice(half, None)]
            ats = [(c, whole) if self.axis == 0 else (whole, c) for c in cuts]
            first, second = self.cross.pop(0)
            if len(self.pieces) == 1:
                (one,) = self.pieces
                made = [one.halve(first, ats[0]), one.halve(second, ats[1])]
            else:
                made = [self.pieces[0].halve(first), self.pieces[1].halve(second)]
            self.pieces = [piece for _, piece in made]
            return tuple(send for send, _ in made)
        if len(self.pieces) == 2:
            joined = lambda a, b: jnp.concatenate([a, b], axis=self.axis - 2)
            one, two = self.pieces
            shape = lambda a: a.reshape((-1,) + a.shape[-2:])
            self.pieces = [
                Piece(
                    joined(shape(one.kept), shape(two.kept)),
                    joined(shape(one.came), shape(two.came)),
                    one.parts,
                )
            ]
        (piece,) = self.pieces
        if self.order:
            send, piece = piece.halve(self.order.pop(0))
            self.pieces = [piece]
            return send
        if self.have is None:
            total = (piece.kept.astype(f32) + piece.came.astype(f32)).reshape(self.block)
            self.result, fresh = self.finish(total)
            self.have = fresh[None]
        else:
            self.have = jnp.concatenate([self.have, piece.came], axis=0)
        piece.came = lax.ppermute(self.have, AXES, flipped(*self.ways.pop(0)))
        return self.have

    def all(self):
        return placed(jnp.concatenate([self.have, self.pieces[0].came], axis=0), self.back)


class Total:
    def __init__(self, vector):
        self.vector, self.order = vector, rising()

    def left(self):
        return bool(self.order)

    def step(self, *after):
        mine = tie(self.vector, *after)
        self.vector = mine + lax.ppermute(mine, AXES, flipped(*self.order.pop(0)))
        return mine


def adam_step(parameter, gradient, moment, square):
    first_fix = 1.0 - jnp.power(jnp.float32(0.5), jnp.float32(STEP))
    second_fix = 1.0 - jnp.power(jnp.float32(0.999), jnp.float32(STEP))
    moment_next = 0.5 * moment + 0.5 * gradient
    square_next = 0.999 * square + 0.001 * gradient * gradient
    fresh_weight = parameter - learn_rate * (moment_next / first_fix) / (
        jnp.sqrt(square_next / second_fix) + 1e-08
    )
    return (moment_next, square_next, fresh_weight.astype(bf16))


def per_device(
    x_slots, counts, cotangent, w_qkv, w_proj, w_fc1, w_fc2, small_params,
    moment_qkv, moment_proj, moment_fc1, moment_fc2, moment_small,
    square_qkv, square_proj, square_fc1, square_fc2, square_small,
):
    slots, per_even = x_slots.shape[0], cotangent.shape[0]
    win_at, grp_at = lax.axis_index("win"), lax.axis_index("grp")
    wins, grps = lax.axis_size("win"), lax.axis_size("grp")
    base = (win_at * grps + grp_at) * per_even
    count = counts[0]
    prev, nxt = neighbours(lax.dynamic_slice_in_dim(x_slots, count - 1, 1, 0), x_slots[:1])
    offset = windows_before(counts)[0]
    window = base + jnp.arange(per_even, dtype=jnp.int32)
    slot = window - offset
    spot = window % (GRID * GRID)
    info = jnp.stack(
        [
            jnp.clip(slot, 0, slots - 1),
            jnp.where(slot < 0, 1, jnp.where(slot >= count, 2, 0)),
            SIDE - WS * (spot // GRID),
            SIDE - WS * (spot % GRID),
        ],
        axis=1,
    ).astype(jnp.int32)
    vec, b1, bias, tab_fwd, tab_bwd = prepare(small_params)
    blocks = lambda grad: grad.reshape(grps // 2, wins, D // wins, grad.shape[2])
    core = (grp_at & 1).astype(jnp.int32).reshape(1)
    flat = lambda a: a.reshape(per_even * TP, a.shape[2])
    def owned(weight, piece):
        at = (win_at * piece.shape[0], grp_at * piece.shape[1])
        return lax.dynamic_slice(weight, at, piece.shape).astype(f32)

    wide = 3 * D // grps
    both = lambda a, b: jnp.concatenate([a, b], axis=1)
    own_attn = both(owned(w_qkv, moment_qkv), owned(w_proj, moment_proj))
    moment_attn, square_attn = both(moment_qkv, moment_proj), both(square_qkv, square_proj)
    own_fc1, own_fc2 = owned(w_fc1, moment_fc1), owned(w_fc2, moment_fc2)

    def finish_fc2(total):
        grad = total.T
        moment, square, fresh = adam_step(own_fc2, grad, moment_fc2, square_fc2)
        return (grad, moment, square), fresh.T

    def finish_fc1(total):
        moment, square, fresh = adam_step(own_fc1, total, moment_fc1, square_fc1)
        return (total, moment, square), fresh

    def finish_attn(total):
        moment, square, fresh = adam_step(own_attn, total, moment_attn, square_attn)
        return (total, moment, square), fresh

    xpad, n1, qkv, p_t, o, h, n2 = forward_attention(
        info, x_slots, prev, nxt, w_qkv, w_proj, vec, bias, tab_fwd
    )
    n2, h, n1, o, xpad = flat(n2), flat(h), flat(n1), flat(o), flat(xpad)
    gl, slope, keep, send, dz, sum_b2 = feed_up(info, core, n2, cotangent, w_fc1, b1)
    if wins != keep.shape[1]:
        again = lambda a: a.transpose(0, 2, 1, 3).reshape(grps // 2, D // grps, wins, FF // wins).transpose(0, 2, 1, 3)
        keep, send = again(keep), again(send)
    fc2 = Chunk(keep, send, 0, finish_fc2)
    block_out = feed_out(info, gl, w_fc2, h, vec)
    sent = fc2.step(block_out)
    keep, send, sum_b1, dh, da, do, sums_two = feed_down(
        info, core, tie(dz, *sent), slope, n2, h, w_fc1, w_fc2, w_proj, vec
    )
    do = do.reshape(per_even, TP, D)
    sent = fc2.step(do)
    fc1 = Chunk(blocks(tie(keep, *sent)), blocks(tie(send, *sent)), 1, finish_fc1)
    dqkv, table, sum_qkv = backward_attention(qkv, p_t, tie(do, send, *sent), tab_bwd, 0, 1)
    sent = fc1.step(table)
    sent = (*sent, fc2.step(*sent))
    dqkv, table_two, sum_two = backward_attention(
        qkv, p_t, tie(do, *sent), tab_bwd, 1, per_even - 1, dqkv
    )
    table, sum_qkv = table + table_two, sum_qkv + sum_two
    sent = fc1.step(table_two)
    sent = (*sent, fc2.step(*sent))
    dqkv = flat(dqkv)
    keep, send = attention_weights(core, n1, tie(dqkv, *sent), o, da)
    sent = fc1.step(keep)
    attn = Chunk(blocks(tie(keep, sent)), blocks(tie(send, sent)), 1, finish_attn)
    dx, sums_one = input_gradient(info, tie(dqkv, send, sent), w_qkv, xpad, dh, vec)
    rel_h = (table[0:RELN, 64:] + table[64 : 64 + RELN, :64])[::-1]
    rel_w = table[32 : 32 + RELN, 64:] + table[96 : 96 + RELN, :64]
    small_grad = jnp.concatenate(
        [
            sums_one[0], sums_two[0], sums_one[1], sums_two[1], sum_qkv[0, :D], sum_qkv[0, 2 * D :],
            sums_two[2], sum_b2[0], sum_b1[0], rel_h.reshape(-1), rel_w.reshape(-1),
        ]
    )
    sent = attn.step(sums_one)
    token = fc2.step(*sent)
    token = fc1.step(token)
    dx, small_grad = tie((dx, small_grad), token)
    dx_prev, dx_next = neighbours(dx[per_even - 1 :], dx[:1])
    small = Total(small_grad)
    place = offset + jnp.arange(slots, dtype=jnp.int32) - base
    live = jnp.arange(slots) < count
    back = jnp.where(place < 0, 1, jnp.where(place >= per_even, 2, 0))
    back = jnp.stack([jnp.clip(place, 0, per_even - 1), jnp.where(live, back, 3)], axis=1)
    rounds, input_grad = 0, None
    while any(chunk.left() for chunk in (attn, fc2, fc1, small)):
        for chunk in (attn, fc2, fc1, small):
            if chunk.left():
                token = chunk.step(token)
                token = token[0] if isinstance(token, tuple) else token
        rounds += 1
        if rounds == 2:
            input_grad = to_slots(tie(back.astype(jnp.int32), token), dx, dx_prev, dx_next)
            token = input_grad
    (part_d, next_m_fc2, next_v_fc2), all_fc2 = fc2.result, fc2.all()
    (part_c, next_m_fc1, next_v_fc1), all_fc1 = fc1.result, fc1.all()
    parted = [(a[:, :wide], a[:, wide:]) for a in attn.result]
    (part_a, part_b), (next_m_qkv, next_m_proj), (next_v_qkv, next_v_proj) = parted
    all_attn = attn.all()
    new_qkv = all_attn[:, :, :wide].reshape(D, -1)
    new_proj = all_attn[:, :, wide:].reshape(D, -1)
    new_fc1 = all_fc1.reshape(D, -1)
    new_fc2 = all_fc2.transpose(0, 2, 1).reshape(FF, -1)
    grad_small = small.vector
    upd_small = adam_step(small_params.astype(f32), grad_small, moment_small, square_small)
    return (
        block_out, input_grad, part_a, part_b, part_c, part_d, grad_small,
        next_m_qkv, next_m_proj, next_m_fc1, next_m_fc2, upd_small[0],
        next_v_qkv, next_v_proj, next_v_fc1, next_v_fc2, upd_small[1],
        new_qkv, new_proj, new_fc1, new_fc2, upd_small[2],
    )


def solution(mesh):
    data, shard, same, part = P(AXES, None, None), P("win", "grp"), P(), P(None, "grp")
    in_specs = (data, P(AXES), data) + (same,) * 5 + ((shard,) * 4 + (same,)) * 2
    out_specs = (data,) * 2 + ((shard,) * 4 + (same,)) * 3 + (part,) * 4 + (same,)
    return jax.shard_map(
        per_device, mesh=mesh, in_specs=in_specs, out_specs=out_specs, check_vma=False
    )
```

```python
import functools

import jax
import jax.numpy as jnp
import numpy as np
from jax import lax
from jax.experimental import pallas as pl
from jax.experimental.pallas import tpu as pltpu
from jax.sharding import PartitionSpec as P

D = 768
HEADS = 12
HD = 64
FF = 3072
WS = 14
SIDE = 64
STEP = 4
TOKW = 196
GRID = 5
RELN = 27
TP = 224

root_half = 0.7071067811865476
inv_root_two_pi = 0.3989422804014327
learn_rate = 0.06
bf16 = jnp.bfloat16
f32 = jnp.float32
VMEM_LIMIT = 56 << 20


def dot(a, b):
    return lax.dot_general(a, b, (((1,), (0,)), ((), ())), preferred_element_type=f32)


def dot_nt(a, b):
    return lax.dot_general(a, b, (((1,), (1,)), ((), ())), preferred_element_type=f32)


def dot_tn(a, b):
    return lax.dot_general(a, b, (((0,), (0,)), ((), ())), preferred_element_type=f32)


def iota(shape, axis):
    return lax.broadcasted_iota(jnp.int32, shape, axis)


def spread():
    row, token = iota((TP, TOKW), 0), iota((TP, TOKW), 1)
    hit = ((row & 15) < WS) & (token == WS * (row >> 4) + (row & 15))
    return hit.astype(f32).astype(bf16)


def gather_rows():
    token, row = iota((TOKW, TP), 0), iota((TOKW, TP), 1)
    hit = ((row & 15) < WS) & (token == WS * (row >> 4) + (row & 15))
    return hit.astype(f32).astype(bf16)


def key_lanes():
    row, lane = iota((TP, 128), 0), iota((TP, 128), 1)
    i, j = row >> 4, row & 15
    hit = (lane == i) | ((lane >= 64) & (lane < 64 + WS) & (lane - 64 == j))
    shut = (lane == 127) & (j >= WS)
    hit = hit.astype(f32)
    return hit.astype(bf16), jnp.where(shut, -1e30, hit).astype(bf16)


def inside(limit_row, limit_col):
    row = iota((TP, 1), 0)
    i, j = row >> 4, row & 15
    return ((i < limit_row) & (j < jnp.minimum(limit_col, WS))).astype(f32)


def norm_parts(v):
    centered = v - jnp.mean(v, axis=-1, keepdims=True)
    scale_inv = lax.rsqrt(jnp.mean(centered * centered, axis=-1, keepdims=True) + 1e-06)
    return centered * scale_inv, scale_inv


def norm_back(e, normed, scale_inv):
    return scale_inv * (
        e
        - jnp.mean(e, axis=-1, keepdims=True)
        - normed * jnp.mean(e * normed, axis=-1, keepdims=True)
    )


def lane_mask(head):
    lane = iota((1, 128), 1)
    return ((lane < HD) if head == 0 else (lane >= HD)).astype(f32).astype(bf16)


def query_lanes(table):
    lane = iota((16, 128), 1)
    out = []
    for i in range(WS):
        tile = table[16 * i : 16 * i + 16]
        by_row = pltpu.roll(tile, 51 + i, 1)
        by_col = pltpu.roll(tile, 51, 1, stride=1, stride_axis=0)
        out.append(jnp.where(lane < 64, by_row, by_col))
    aug = jnp.concatenate(out, axis=0)
    high = aug.astype(bf16)
    low = (aug - high.astype(f32)).astype(bf16)
    return high, jnp.where(iota((TP, 128), 1) == 127, jnp.asarray(1.0, bf16), low)


def fwd_kernel(
    info, xs_ref, prev_ref, next_ref, wqkv_ref, wproj_ref, vec_ref, tab_ref,
    xpad_ref, n1_ref, qkv_ref, pt_ref, o_ref, h_ref, n2_ref,
):
    k = pl.program_id(0)
    source = info[k, 1]
    x = jnp.where(source == 0, xs_ref[0], jnp.where(source == 1, prev_ref[0], next_ref[0]))
    big = dot(spread(), x)
    xpad_ref[0] = big.astype(bf16)
    mask = inside(info[k, 2], info[k, 3])
    vec = vec_ref[...]
    normed, _ = norm_parts(big)
    n1 = (mask * (normed * vec[0:1] + vec[2:3])).astype(bf16)
    n1_ref[0] = n1
    for part, bias in enumerate((vec[4:5], 0.0, vec[5:6])):
        at = slice(D * part, D * part + D)
        qkv_ref[0, :, at] = (dot(n1, wqkv_ref[:, at]) + bias).astype(bf16)
    keys_open, keys_extra = key_lanes()
    for pair in range(HEADS // 2):
        at = 128 * pair
        q = qkv_ref[0, :, at : at + 128]
        key = jnp.concatenate([qkv_ref[0, :, D + at : D + at + 128], keys_open, keys_extra], axis=1)
        v_t = qkv_ref[0, :, 2 * D + at : 2 * D + at + 128].T
        tables = dot(q, tab_ref[...])
        sides = [query_lanes(tables[:, 128 * head : 128 * head + 128]) for head in range(2)]
        scores = [
            dot_nt(key, jnp.concatenate([q * (lane_mask(head) * 0.125), *sides[head]], axis=1))
            for head in range(2)
        ]
        peaks = [jnp.max(s, axis=0, keepdims=True) for s in scores]
        es = [jnp.exp(s - m) for s, m in zip(scores, peaks)]
        sums = [jnp.sum(e, axis=0, keepdims=True) for e in es]
        ps = [(e * (1.0 / l)).astype(bf16) for e, l in zip(es, sums)]
        outs = []
        for head in range(2):
            pt_ref[0, 2 * pair + head] = ps[head]
            outs.append(dot(v_t[HD * head : HD * head + HD], ps[head]))
        o_ref[0, :, at : at + 128] = jnp.concatenate(outs, axis=0).T.astype(bf16)
    a = dot(o_ref[0], wproj_ref[...]) + vec[6:7]
    h = mask * (big + a)
    h_ref[0] = h
    normed_two, _ = norm_parts(h)
    n2_ref[0] = (mask * (normed_two * vec[1:2] + vec[3:4])).astype(bf16)


def forward_attention(info, x_slots, prev, nxt, w_qkv, w_proj, vec, tab):
    windows = info.shape[0]
    one = lambda *tail: pl.BlockSpec((1,) + tail, lambda k, s: (k,) + (0,) * len(tail))
    whole = lambda a: pl.BlockSpec(a.shape, lambda k, s: (0,) * a.ndim)
    shape = lambda *tail, dtype=bf16: jax.ShapeDtypeStruct((windows,) + tail, dtype)
    return pl.pallas_call(
        fwd_kernel,
        grid_spec=pltpu.PrefetchScalarGridSpec(
            num_scalar_prefetch=1,
            grid=(windows,),
            in_specs=[
                pl.BlockSpec((1, TOKW, D), lambda k, s: (s[k, 0], 0, 0)),
                whole(prev), whole(nxt), whole(w_qkv), whole(w_proj), whole(vec), whole(tab),
            ],
            out_specs=[
                one(TP, D), one(TP, D), one(TP, 3 * D), one(HEADS, TP, TP), one(TP, D), one(TP, D), one(TP, D),
            ],
        ),
        out_shape=[
            shape(TP, D), shape(TP, D), shape(TP, 3 * D), shape(HEADS, TP, TP), shape(TP, D),
            shape(TP, D, dtype=f32), shape(TP, D),
        ],
        compiler_params=pltpu.CompilerParams(vmem_limit_bytes=VMEM_LIMIT),
        cost_estimate=pl.CostEstimate(flops=0, bytes_accessed=0, transcendentals=0),
        name="attention_forward",
    )(info, x_slots, prev, nxt, w_qkv, w_proj, vec, tab)


def vectors(small):
    return small[: 8 * D].astype(f32).reshape(8, D)


def forward_tables(small):
    tables = small[8 * D + FF :].reshape(2, RELN, HD)[:, ::-1]
    gap = jnp.zeros((64 - RELN, HD), bf16)
    one = jnp.concatenate([tables[1], gap, tables[0], gap], axis=0).T
    none = jnp.zeros_like(one)
    return jnp.block([[one, none], [none, one]])


def backward_tables(small):
    tables = small[8 * D + FF :].reshape(2, RELN, HD)
    gap = jnp.zeros((32 - RELN, HD), bf16)
    half = jnp.concatenate([tables[0, ::-1], gap, tables[1], gap], axis=0)
    nil = jnp.zeros_like(half)
    return jnp.block([[nil, half], [half, nil]])


def params(**more):
    return dict(
        compiler_params=pltpu.CompilerParams(vmem_limit_bytes=VMEM_LIMIT),
        cost_estimate=pl.CostEstimate(flops=0, bytes_accessed=0, transcendentals=0),
        **more,
    )


def whole(a):
    return pl.BlockSpec(a.shape, lambda k, *s: (0,) * a.ndim)


def sds(*dims, dtype=bf16):
    return jax.ShapeDtypeStruct(dims, dtype)


def masks(info, windows):
    return [inside(info[k, 2], info[k, 3]) for k in range(windows)]


def up_kernel(info, core, n2_ref, cot_ref, w1_ref, b1_ref, gl_ref, slope_ref, keep_ref, send_ref, dz_ref, b2_ref, dz_t):
    windows = cot_ref.shape[0]

    @pl.when(pl.program_id(0) == 0)
    def _():
        total = jnp.zeros((1, D), f32)
        for k, mask in enumerate(masks(info, windows)):
            part = dot(spread(), cot_ref[k]) * mask
            dz_ref[TP * k : TP * k + TP] = part.astype(bf16)
            total += jnp.sum(part, axis=0, keepdims=True)
        b2_ref[...] = total
        dz_t[...] = dz_ref[...].T

    u = dot(n2_ref[...], w1_ref[...]) + b1_ref[...]
    half = 0.5 * (1.0 + lax.erf(u * root_half))
    gl = (u * half).astype(bf16)
    gl_ref[...] = gl
    slope_ref[...] = (half + u * jnp.exp(-0.5 * u * u) * inv_root_two_pi).astype(bf16)
    grad = dot(dz_t[...], gl).astype(bf16)
    even = core[0] == 0
    rows, cols = keep_ref.shape[2:]
    for y in range(keep_ref.shape[0]):
        for w in range(keep_ref.shape[1]):
            at = slice(cols * w, cols * w + cols)
            first = grad[2 * rows * y : 2 * rows * y + rows, at]
            second = grad[2 * rows * y + rows : 2 * rows * y + 2 * rows, at]
            keep_ref[y, w] = jnp.where(even, first, second)
            send_ref[y, w] = jnp.where(even, second, first)


def feed_up(info, core, n2, cot, w_fc1, b1):
    rows = n2.shape[0]
    step = D
    steps = FF // step
    flat = pl.BlockSpec((rows, step), lambda k, *s: (0, k))
    half = pl.BlockSpec((2, 2, 192, 384), lambda k, *s: (0, k, 0, 0))
    return pl.pallas_call(
        up_kernel,
        grid_spec=pltpu.PrefetchScalarGridSpec(
            num_scalar_prefetch=2,
            grid=(steps,),
            in_specs=[
                whole(n2), whole(cot),
                pl.BlockSpec((D, step), lambda k, *s: (0, k)),
                pl.BlockSpec((1, step), lambda k, *s: (0, k)),
            ],
            out_specs=[
                flat, flat, half, half,
                pl.BlockSpec((rows, D), lambda k, *s: (0, 0)),
                pl.BlockSpec((1, D), lambda k, *s: (0, 0)),
            ],
            scratch_shapes=[pltpu.VMEM((D, rows), bf16)],
        ),
        out_shape=[
            sds(rows, FF), sds(rows, FF), sds(2, 8, 192, 384), sds(2, 8, 192, 384), sds(rows, D),
            sds(1, D, dtype=f32),
        ],
        name="feed_up",
        **params(),
    )(info, core, n2, cot, w_fc1, b1)


def down_kernel(
    info, core, dz_ref, slope_ref, n2_ref, w1_ref, w2_ref, *refs, last,
):
    if last:
        h_hbm, wproj_hbm, vec_ref, _, _, _, acc_hbm = refs[:7]
        keep_ref, send_ref, b1_ref, dh_ref, da_ref, do_ref, sums_ref = refs[7:14]
        n2_t, acc, h_ref, wproj_ref, acc_in, sems = refs[14:]
        copies = [
            pltpu.make_async_copy(src, dst, sems.at[k])
            for k, (src, dst) in enumerate(((acc_hbm, acc_in), (h_hbm, h_ref), (wproj_hbm, wproj_ref)))
        ]
    else:
        keep_ref, send_ref, b1_ref, acc, n2_t = refs
    step = pl.program_id(0)

    @pl.when(step == 0)
    def _():
        if last:
            for copy in copies:
                copy.start()
        n2_t[...] = n2_ref[...].T
        acc[...] = jnp.zeros_like(acc)

    du = dot_nt(dz_ref[...], w2_ref[...]) * slope_ref[...].astype(f32)
    du_low = du.astype(bf16)
    b1_ref[...] = jnp.sum(du_low.astype(f32), axis=0, keepdims=True)
    mine = (step & 1) == core[0]
    grad = dot(n2_t[...], du_low).astype(bf16)

    @pl.when(mine)
    def _():
        keep_ref[0] = grad

    @pl.when(jnp.logical_not(mine))
    def _():
        send_ref[0] = grad

    acc[...] += dot_nt(du_low, w1_ref[...])
    if not last:
        return

    @pl.when(step == pl.num_programs(0) - 1)
    def _():
        for copy in copies:
            copy.wait()
        vec = vec_ref[...]
        windows = acc.shape[0] // TP
        gain = jnp.zeros((1, D), f32)
        shift = jnp.zeros((1, D), f32)
        bias = jnp.zeros((1, D), f32)
        for k, mask in enumerate(masks(info, windows)):
            at = slice(TP * k, TP * k + TP)
            dn = (acc[at] + acc_in[at]) * mask
            normed, scale_inv = norm_parts(h_ref[at])
            gain += jnp.sum(dn * normed, axis=0, keepdims=True)
            shift += jnp.sum(dn, axis=0, keepdims=True)
            dh = mask * (dz_ref[at].astype(f32) + norm_back(dn * vec[1:2], normed, scale_inv))
            dh_ref[at] = dh
            da = dh.astype(bf16)
            da_ref[at] = da
            bias += jnp.sum(da.astype(f32), axis=0, keepdims=True)
            do_ref[at] = dot_nt(da, wproj_ref[...]).astype(bf16)
        sums_ref[0:1] = gain
        sums_ref[1:2] = shift
        sums_ref[2:3] = bias
        sums_ref[3:8] = jnp.zeros((5, D), f32)


def feed_down(info, core, dz, slope, n2, w_fc1, w_fc2, begin, steps, more=()):
    rows = n2.shape[0]
    step = D
    last = bool(more)
    hbm = pl.BlockSpec(memory_space=pl.ANY)
    inputs = [dz, slope, n2, w_fc1, w_fc2, *more]
    in_specs = [
        whole(dz),
        pl.BlockSpec((rows, step), lambda k, *s: (0, k + begin)),
        whole(n2),
        pl.BlockSpec((D, step), lambda k, *s: (0, k + begin)),
        pl.BlockSpec((step, D), lambda k, *s: (k + begin, 0)),
    ]
    half = pl.BlockSpec((1, D, step), lambda k, *s: ((k + begin) // 2, 0, 0))
    out_specs = [half, half, pl.BlockSpec((1, step), lambda k, *s: (0, k + begin))]
    out_shape = [sds(2, D, D), sds(2, D, D), sds(1, FF, dtype=f32)]
    flat = pl.BlockSpec((rows, D), lambda k, *s: (0, 0))
    scratch = [pltpu.VMEM((D, rows), bf16)]
    aliases = {}
    if last:
        h, w_proj, vec, keep, send, b1, acc = more
        in_specs += [hbm, hbm, whole(vec), hbm, hbm, hbm, hbm]
        aliases = {10: 0, 11: 1, 12: 2}
        out_specs += [flat] * 3 + [pl.BlockSpec((8, D), lambda k, *s: (0, 0))]
        out_shape += [sds(rows, D, dtype=f32), sds(rows, D), sds(rows, D), sds(8, D, dtype=f32)]
        scratch += [
            pltpu.VMEM((rows, D), f32), pltpu.VMEM((rows, D), f32), pltpu.VMEM((D, D), bf16),
            pltpu.VMEM((rows, D), f32), pltpu.SemaphoreType.DMA((3,)),
        ]
    else:
        out_specs += [flat]
        out_shape += [sds(rows, D, dtype=f32)]
    return pl.pallas_call(
        functools.partial(down_kernel, last=last),
        grid_spec=pltpu.PrefetchScalarGridSpec(
            num_scalar_prefetch=2, grid=(steps,), in_specs=in_specs, out_specs=out_specs,
            scratch_shapes=scratch,
        ),
        out_shape=out_shape,
        input_output_aliases=aliases,
        name="feed_down",
        **params(),
    )(info, core, *inputs)


def out_kernel(info, gl_ref, w2_ref, h_ref, vec_ref, out_ref, acc):
    step = pl.program_id(0)

    @pl.when(step == 0)
    def _():
        acc[...] = h_ref[...]

    acc[...] += dot(gl_ref[...], w2_ref[...])

    @pl.when(step == pl.num_programs(0) - 1)
    def _():
        for k, mask in enumerate(masks(info, out_ref.shape[0])):
            at = slice(TP * k, TP * k + TP)
            y = (mask * (acc[at] + vec_ref[7:8])).astype(bf16)
            out_ref[k] = dot(gather_rows(), y).astype(bf16)


def feed_out(info, gl, w_fc2, h, vec):
    rows = gl.shape[0]
    windows = rows // TP
    step = D
    return pl.pallas_call(
        out_kernel,
        grid_spec=pltpu.PrefetchScalarGridSpec(
            num_scalar_prefetch=1,
            grid=(FF // step,),
            in_specs=[
                pl.BlockSpec((rows, step), lambda k, s: (0, k)),
                pl.BlockSpec((step, D), lambda k, s: (k, 0)),
                whole(h), whole(vec),
            ],
            out_specs=pl.BlockSpec((windows, TOKW, D), lambda k, s: (0, 0, 0)),
            scratch_shapes=[pltpu.VMEM((rows, D), f32)],
        ),
        out_shape=sds(windows, TOKW, D),
        name="feed_out",
        **params(),
    )(info, gl, w_fc2, h, vec)


def key_rows():
    lane, col = iota((64, TP), 0), iota((64, TP), 1)
    i, j = col >> 4, col & 15
    hit = ((lane < WS) & (lane == i)) | ((lane >= 32) & (lane < 32 + WS) & (lane - 32 == 13 - j))
    return hit.astype(f32).astype(bf16)


def grad_rolls(table, base):
    lane = iota((16, 128), 1)
    out = []
    for i in range(WS):
        tile = table[16 * i : 16 * i + 16]
        by_row = jnp.where((lane >= base) & (lane < base + WS), tile, 0.0)
        by_row = pltpu.roll(by_row, 13 - i, 1) if i < 13 else by_row
        by_col = jnp.where((lane >= base + 32) & (lane < base + 32 + WS), tile, 0.0)
        out.append(by_row + pltpu.roll(by_col, 0, 1, stride=1, stride_axis=0))
    return jnp.concatenate(out, axis=0)


def back_kernel(qkv_ref, pt_ref, do_ref, tab_ref, *refs):
    dqkv_ref, table_ref, sums_ref = refs[-3:]

    @pl.when(pl.program_id(0) == 0)
    def _():
        table_ref[...] = jnp.zeros_like(table_ref)
        sums_ref[...] = jnp.zeros_like(sums_ref)

    rows_extra = key_rows()
    lane = iota((TP, 128), 1)
    for pair in range(HEADS // 2):
        at = 128 * pair
        q = qkv_ref[0, :, at : at + 128]
        key_t = (qkv_ref[0, :, D + at : D + at + 128] * jnp.asarray(0.125, bf16)).T
        v = qkv_ref[0, :, 2 * D + at : 2 * D + at + 128]
        do = do_ref[0, :, at : at + 128]
        ds_all, dq_all, z_all = [], [], []
        for head in range(2):
            p_t = pt_ref[0, 2 * pair + head].astype(f32)
            dp_t = dot_nt(v, do * lane_mask(head))
            mean = jnp.sum(p_t * dp_t, axis=0, keepdims=True) / jnp.sum(p_t, axis=0, keepdims=True)
            ds_t = (p_t * (dp_t - mean)).astype(bf16)
            ds_all.append(ds_t)
            if head == 0:
                left = jnp.concatenate([key_t[:HD], rows_extra], axis=0)
            else:
                left = jnp.concatenate([rows_extra, key_t[HD:]], axis=0)
            back = dot(left, ds_t).T
            dq_all.append(back)
            z_all.append(grad_rolls(back, 64 if head == 0 else 0))
        z = jnp.where(lane < HD, z_all[1], z_all[0]).astype(bf16)
        dq = jnp.where(lane < HD, dq_all[0], dq_all[1]) + dot(z, tab_ref[...])
        table_ref[...] += dot(z.T, q)
        two = lambda a: jnp.concatenate([a * lane_mask(0), a * lane_mask(1)], axis=0)
        dk = dot(jnp.concatenate(ds_all, axis=1), two(q)) * 0.125
        p_two = jnp.concatenate([pt_ref[0, 2 * pair], pt_ref[0, 2 * pair + 1]], axis=1)
        dv = dot(p_two, two(do))
        dqkv_ref[0, :, at : at + 128] = dq.astype(bf16)
        dqkv_ref[0, :, D + at : D + at + 128] = dk.astype(bf16)
        dqkv_ref[0, :, 2 * D + at : 2 * D + at + 128] = dv.astype(bf16)
    sums_ref[...] += jnp.sum(dqkv_ref[0].astype(f32), axis=0, keepdims=True)


def backward_attention(qkv, p_t, do, tab, begin, count, into=None):
    windows = qkv.shape[0]
    one = lambda *tail: pl.BlockSpec((1,) + tail, lambda k: (k + begin,) + (0,) * len(tail))
    inputs = [qkv, p_t, do, tab]
    in_specs = [one(TP, 3 * D), one(HEADS, TP, TP), one(TP, D), whole(tab)]
    if into is not None:
        inputs.append(into)
        in_specs.append(pl.BlockSpec(memory_space=pl.ANY))
    return pl.pallas_call(
        back_kernel,
        grid=(count,),
        in_specs=in_specs,
        out_specs=[
            one(TP, 3 * D),
            pl.BlockSpec((128, 128), lambda k: (0, 0)),
            pl.BlockSpec((1, 3 * D), lambda k: (0, 0)),
        ],
        out_shape=[sds(windows, TP, 3 * D), sds(128, 128, dtype=f32), sds(1, 3 * D, dtype=f32)],
        input_output_aliases={} if into is None else {4: 0},
        name="attention_backward",
        **params(),
    )(*inputs)


def weight_kernel(
    core, n1_ref, dqkv_ref, o_ref, da_ref, keep_ref, send_ref, n1_t, o_t
):
    @pl.when(pl.program_id(0) == 0)
    def _():
        n1_t[...] = n1_ref[...].T
        o_t[...] = o_ref[...].T

    part = dot(n1_t[...], dqkv_ref[...])
    proj = dot(o_t[...], da_ref[...])
    lane = iota((D, 128), 1) < 64
    even = core[0] == 0

    def put(at, first, second):
        first, second = first.astype(bf16), second.astype(bf16)
        keep_ref[0, :, at] = jnp.where(even, first, second)
        send_ref[0, :, at] = jnp.where(even, second, first)

    moved = pltpu.roll(proj[:, 0:256], 64, 1)
    rolled = pltpu.roll(part[:, 512:1152], 576, 1)
    put(slice(0, 512), part[:, 0:512], rolled[:, 0:512])
    put(
        slice(512, 640),
        jnp.where(lane, part[:, 512:640], moved[:, 0:128]),
        jnp.where(lane, rolled[:, 512:640], proj[:, 128:256]),
    )
    put(slice(640, 768), moved[:, 128:256], proj[:, 256:384])


def attention_weights(core, n1, dqkv, o, da):
    rows = n1.shape[0]
    wide = 3 * D // 2
    half = pl.BlockSpec((1, D, D), lambda k, *s: (k, 0, 0))
    return pl.pallas_call(
        weight_kernel,
        grid_spec=pltpu.PrefetchScalarGridSpec(
            num_scalar_prefetch=1,
            grid=(2,),
            in_specs=[
                whole(n1),
                pl.BlockSpec((rows, wide), lambda k, *s: (0, k)),
                whole(o),
                pl.BlockSpec((rows, D // 2), lambda k, *s: (0, k)),
            ],
            out_specs=[half] * 2,
            scratch_shapes=[pltpu.VMEM((D, rows), bf16), pltpu.VMEM((D, rows), bf16)],
        ),
        out_shape=[sds(2, D, D)] * 2,
        name="attention_weights",
        **params(),
    )(core, n1, dqkv, o, da)


def input_kernel(info, dqkv_ref, wqkv_ref, xpad_ref, dh_ref, vec_ref, dx_ref, sums_ref):
    vec = vec_ref[...]
    acc = dot_nt(dqkv_ref[...], wqkv_ref[...])
    k = pl.program_id(0)
    mask = inside(info[k, 2], info[k, 3])
    dn = acc * mask
    normed, scale_inv = norm_parts(xpad_ref[...].astype(f32))
    dx = dh_ref[...] + norm_back(dn * vec[0:1], normed, scale_inv)
    dx_ref[0] = dot(gather_rows(), dx.astype(bf16)).astype(bf16)

    @pl.when(k == 0)
    def _():
        sums_ref[...] = jnp.zeros_like(sums_ref)

    sums_ref[0:1] += jnp.sum(dn * normed, axis=0, keepdims=True)
    sums_ref[1:2] += jnp.sum(dn, axis=0, keepdims=True)


def input_gradient(info, dqkv, w_qkv, xpad, dh, vec):
    rows = xpad.shape[0]
    windows = rows // TP
    return pl.pallas_call(
        input_kernel,
        grid_spec=pltpu.PrefetchScalarGridSpec(
            num_scalar_prefetch=1,
            grid=(windows,),
            in_specs=[
                pl.BlockSpec((TP, 3 * D), lambda k, s: (k, 0)),
                whole(w_qkv),
                pl.BlockSpec((TP, D), lambda k, s: (k, 0)),
                pl.BlockSpec((TP, D), lambda k, s: (k, 0)),
                whole(vec),
            ],
            out_specs=[
                pl.BlockSpec((1, TOKW, D), lambda k, s: (k, 0, 0)),
                pl.BlockSpec((8, D), lambda k, s: (0, 0)),
            ],
        ),
        out_shape=[sds(windows, TOKW, D), sds(8, D, dtype=f32)],
        name="input_gradient",
        **params(),
    )(info, dqkv, w_qkv, xpad, dh, vec)


first_fix = 1.0 - 0.5**STEP
second_fix = float(np.float32(1.0) - np.power(np.float32(0.999), np.float32(STEP)))


def adam_step(parameter, gradient, moment, square):
    moment_next = 0.5 * moment + 0.5 * gradient
    square_next = 0.999 * square + 0.001 * gradient * gradient
    fresh_weight = parameter - learn_rate * (moment_next / first_fix) / (
        jnp.sqrt(square_next / second_fix) + 1e-08
    )
    return moment_next, square_next, fresh_weight.astype(bf16)


def adam_kernel(kept_ref, came_ref, own_ref, *refs):
    parts = (len(refs) - 1) // 5
    moments, squares, grads, moments_next, squares_next = (
        refs[parts * k : parts * k + parts] for k in range(5)
    )
    total = kept_ref[...].astype(f32) + came_ref[...].astype(f32)
    own = own_ref[...].astype(f32)
    begin, fresh = 0, []
    for k in range(parts):
        at = slice(begin, begin + moments[k].shape[1])
        grads[k][...] = total[:, at]
        moment, square, weight = adam_step(own[:, at], total[:, at], moments[k][...], squares[k][...])
        moments_next[k][...] = moment
        squares_next[k][...] = square
        fresh.append(weight.astype(f32))
        begin = at.stop
    fresh = fresh[0] if parts == 1 else jnp.concatenate(fresh, axis=1)
    refs[-1][...] = fresh.astype(bf16)


def adam(kept, came, own, moments, squares):
    shapes = [sds(*m.shape, dtype=f32) for m in moments]
    out = pl.pallas_call(
        adam_kernel,
        out_shape=shapes * 3 + [sds(*kept.shape)],
        name="adam",
        **params(),
    )(kept, came, own, *moments, *squares)
    parts = len(moments)
    return [out[parts * k : parts * k + parts] for k in range(3)], out[-1]


def own_kernel(at, qkv_hbm, proj_hbm, fc1_hbm, fc2_hbm, attn_ref, fc1_ref, fc2_ref, qkv, proj, fc1, fc2, sems):
    win, grp = at[0], at[1]
    odd = (grp & 1) == 1

    def columns(width, more):
        return pl.ds(pl.multiple_of(width * grp - 64 * (grp & 1), 128), more)

    rows = fc1_ref.shape[0]
    some = pl.ds(pl.multiple_of(win * rows, 16), rows)
    many = pl.ds(pl.multiple_of(win * fc2.shape[0], 16), fc2.shape[0])
    copies = [
        pltpu.make_async_copy(qkv_hbm.at[some, columns(3 * D // 4, 640)], qkv, sems.at[0]),
        pltpu.make_async_copy(proj_hbm.at[some, columns(D // 4, 256)], proj, sems.at[1]),
        pltpu.make_async_copy(fc1_hbm.at[some, pl.ds(pl.multiple_of(D * grp, 128), D)], fc1, sems.at[2]),
        pltpu.make_async_copy(fc2_hbm.at[many, columns(D // 4, 256)], fc2, sems.at[3]),
    ]
    for copy in copies:
        copy.start()
    for copy in copies:
        copy.wait()

    def aligned(ref):
        whole = ref[...].astype(f32)
        return jnp.where(odd, pltpu.roll(whole, whole.shape[1] - 64, 1), whole)

    left, right = aligned(qkv), aligned(proj)
    attn_ref[:, 0:512] = left[:, 0:512].astype(bf16)
    right = pltpu.roll(right, 64, 1)
    lane = iota((rows, 128), 1) < 64
    attn_ref[:, 512:640] = jnp.where(lane, left[:, 512:640], right[:, 0:128]).astype(bf16)
    attn_ref[:, 640:768] = right[:, 128:256].astype(bf16)
    fc1_ref[...] = fc1[...]
    fc2_ref[...] = aligned(fc2).T[0 : D // 4].astype(bf16)


def own_blocks(win, grp, wins, grps, w_qkv, w_proj, w_fc1, w_fc2):
    rows, many = D // wins, FF // wins
    if grps != 4 or rows % 16 or many % 128:
        cut = lambda w, r, c: lax.dynamic_slice(w, (win * r, grp * c), (r, c))
        attn = [cut(w_qkv, rows, 3 * D // grps), cut(w_proj, rows, D // grps)]
        return jnp.concatenate(attn, axis=1), cut(w_fc1, rows, FF // grps), cut(w_fc2, many, D // grps).T
    hbm = pl.BlockSpec(memory_space=pl.ANY)
    vmem = pl.BlockSpec(memory_space=pltpu.VMEM)
    return pl.pallas_call(
        own_kernel,
        in_specs=[pl.BlockSpec(memory_space=pltpu.SMEM)] + [hbm] * 4,
        out_specs=[vmem] * 3,
        out_shape=[sds(rows, D), sds(rows, D), sds(D // 4, many)],
        scratch_shapes=[
            pltpu.VMEM((rows, 640), bf16), pltpu.VMEM((rows, 256), bf16), pltpu.VMEM((rows, D), bf16),
            pltpu.VMEM((many, 256), bf16), pltpu.SemaphoreType.DMA((4,)),
        ],
        name="own_blocks",
        **params(),
    )(jnp.stack([win, grp]).astype(jnp.int32), w_qkv, w_proj, w_fc1, w_fc2)


def place_kernel(at, have_ref, came_ref, *refs, way):
    half = have_ref.shape[0]
    rows, columns = have_ref.shape[1:]
    for target in range(2 * half):
        place = at[target]
        near = have_ref[jnp.minimum(place, half - 1)]
        far = came_ref[jnp.maximum(place - half, 0)]
        block = jnp.where(place < half, near, far)
        if way == "lanes":
            refs[0][:, columns * target : columns * target + columns] = block
        else:
            refs[-1 if way == "turned" else 0][rows * target : rows * target + rows] = block
    if way == "turned":
        whole = refs[-1][...].T
        begin = 0
        for out in refs[:-1]:
            out[...] = whole[begin : begin + out.shape[0]]
            begin += out.shape[0]


def put_in_place(at, have, came, way, widths=()):
    count, rows, columns = 2 * have.shape[0], have.shape[1], have.shape[2]
    smem = pl.BlockSpec(memory_space=pltpu.SMEM)
    vmem = pl.BlockSpec(memory_space=pltpu.VMEM)
    scratch = []
    if way == "lanes":
        shapes = [sds(rows, count * columns)]
    elif way == "rows":
        shapes = [sds(count * rows, columns)]
    else:
        shapes = [sds(width, count * rows) for width in widths]
        scratch = [pltpu.VMEM((count * rows, columns), bf16)]
    return pl.pallas_call(
        functools.partial(place_kernel, way=way),
        in_specs=[smem, vmem, vmem],
        out_specs=[vmem] * len(shapes),
        out_shape=shapes,
        scratch_shapes=scratch,
        name="put_in_place",
        **params(),
    )(at, have, came)


def slots_kernel(info, dx_hbm, prev_hbm, next_hbm, out_hbm, zero, sems):
    zero[...] = jnp.zeros_like(zero)

    def each(act):
        for slot in range(out_hbm.shape[0]):
            source = info[slot, 1]
            for kind, ref in enumerate((dx_hbm.at[info[slot, 0]], prev_hbm.at[0], next_hbm.at[0], zero)):

                @pl.when(source == kind)
                def _(ref=ref, slot=slot):
                    act(pltpu.make_async_copy(ref, out_hbm.at[slot], sems.at[slot]))

    each(lambda copy: copy.start())
    each(lambda copy: copy.wait())


def to_slots(info, dx, prev, nxt):
    slots = info.shape[0]
    hbm = pl.BlockSpec(memory_space=pl.ANY)
    return pl.pallas_call(
        slots_kernel,
        in_specs=[pl.BlockSpec(memory_space=pltpu.SMEM), hbm, hbm, hbm],
        out_specs=hbm,
        out_shape=sds(slots, TOKW, D),
        scratch_shapes=[pltpu.VMEM((TOKW, D), bf16), pltpu.SemaphoreType.DMA((slots,))],
        name="to_slots",
        **params(),
    )(info, dx, prev, nxt)


AXES = ("win", "grp")


def bits_of(size):
    return [1 << k for k in range(size.bit_length() - 1)]


def flipped(axis, bit):
    wins, grps = lax.axis_size("win"), lax.axis_size("grp")
    out = []
    for d in range(wins * grps):
        w, g = divmod(d, grps)
        w, g = (w ^ bit, g) if axis == "win" else (w, g ^ bit)
        out.append((d, w * grps + g))
    return out


def windows_before(count, windows):
    total, before = count, jnp.zeros_like(count)
    bits = [(axis, bit) for axis in ("grp", "win") for bit in bits_of(lax.axis_size(axis))]
    for axis, bit in bits:
        last = (axis, bit) == bits[-1]
        other = windows - total if last else lax.ppermute(total, AXES, flipped(axis, bit))
        mine = (lax.axis_index(axis) & bit) != 0
        before = before + jnp.where(mine, other, 0)
        total = total + other
    return before


def neighbours(last, first):
    count = lax.axis_size("win") * lax.axis_size("grp")
    up = [(i, i + 1) for i in range(count - 1)]
    down = [(j, i) for i, j in up]
    return lax.ppermute(last, AXES, up), lax.ppermute(first, AXES, down)


def rising():
    return [(axis, bit) for axis in ("grp", "win") for bit in bits_of(lax.axis_size(axis))]


def tie(value, *others):
    return lax.optimization_barrier((value, *others))[0]


def places(order):
    apart = lax.axis_index("win") ^ jnp.arange(lax.axis_size("win"), dtype=jnp.int32)
    return sum(((apart & bit) != 0).astype(jnp.int32) << k for k, (_, bit) in enumerate(order))


class Piece:
    def __init__(self, kept, came, parts):
        self.kept, self.came, self.parts = kept, came, parts

    def halve(self, which, at=None):
        axis, bit = which
        place = self.parts.index(which)
        parts = self.parts[:place] + self.parts[place + 1 :]
        mine = ((lax.axis_index(axis) & bit) != 0).astype(jnp.int32)
        split = (1 << place, 2, -1) + self.kept.shape[-2:]
        kept, came = self.kept.reshape(split), self.came.reshape(split)

        def pick(half):
            piece = lax.dynamic_index_in_dim(kept, half, 1, keepdims=False)
            other = lax.dynamic_index_in_dim(came, half, 1, keepdims=False)
            if at is not None:
                piece, other = piece[..., at[0], at[1]], other[..., at[0], at[1]]
            return (piece.astype(f32) + other.astype(f32)).astype(bf16)

        send, kept = pick(1 - mine), pick(mine)
        return send, Piece(kept, lax.ppermute(send, AXES, flipped(axis, bit)), parts)


class Chunk:
    def __init__(self, keep, send, axis):
        near, *self.grp = [one for one in rising() if one[0] == "grp"]
        self.win = [one for one in rising() if one[0] == "win"]
        parts = list(reversed(self.grp)) + list(reversed(self.win))
        self.pieces = [Piece(keep, lax.ppermute(send, AXES, flipped(*near)), parts)]
        self.block, self.axis, self.finish = keep.shape[-2:], axis, None
        self.cross = [(self.grp[-1], self.win[0]), (self.win[0], self.grp[-1])]
        self.order = self.grp[:-1] + self.win[1:]
        self.ways, self.back = list(reversed(self.win)), list(reversed(self.win))
        self.have = None

    def left(self):
        return bool(self.cross or self.order or self.ways)

    def after(self, *others):
        if others:
            for piece in self.pieces:
                piece.came = tie(piece.came, *others)

    def step(self, *others):
        self.after(*others)
        if self.cross:
            whole, half = slice(None), self.block[self.axis] // 2
            cuts = [slice(0, half), slice(half, None)]
            ats = [(c, whole) if self.axis == 0 else (whole, c) for c in cuts]
            first, second = self.cross.pop(0)
            if len(self.pieces) == 1:
                (one,) = self.pieces
                made = [one.halve(first, ats[0]), one.halve(second, ats[1])]
            else:
                made = [self.pieces[0].halve(first), self.pieces[1].halve(second)]
            self.pieces = [piece for _, piece in made]
            return tuple(send for send, _ in made)
        if len(self.pieces) == 2:
            joined = lambda a, b: jnp.concatenate([a, b], axis=self.axis - 2)
            one, two = self.pieces
            shape = lambda a: a.reshape((-1,) + a.shape[-2:])
            self.pieces = [
                Piece(
                    joined(shape(one.kept), shape(two.kept)),
                    joined(shape(one.came), shape(two.came)),
                    one.parts,
                )
            ]
        (piece,) = self.pieces
        if self.order:
            send, piece = piece.halve(self.order.pop(0))
            self.pieces = [piece]
            return send
        if self.have is None:
            self.result, fresh = self.finish(piece.kept.reshape(self.block), piece.came.reshape(self.block))
            self.have = fresh[None]
        else:
            self.have = jnp.concatenate([self.have, piece.came], axis=0)
        piece.came = lax.ppermute(self.have, AXES, flipped(*self.ways.pop(0)))
        return self.have

    def all(self, way, widths=()):
        have, came = self.have, self.pieces[0].came
        if self.block[0] % 16 == 0 and self.block[1] % 128 == 0:
            return put_in_place(places(self.back), have, came, way, widths)
        blocks = jnp.concatenate([have, came], axis=0)[places(self.back)]
        if way == "lanes":
            return [blocks.transpose(1, 0, 2).reshape(blocks.shape[1], -1)]
        blocks = blocks.reshape(-1, blocks.shape[2])
        return [blocks] if way == "rows" else jnp.split(blocks.T, np.cumsum(widths)[:-1], axis=0)


class Total:
    def __init__(self, vector):
        self.vector, self.order = vector, rising()

    def left(self):
        return bool(self.order)

    def step(self, *after):
        mine = tie(self.vector, *after)
        self.vector = mine + lax.ppermute(mine, AXES, flipped(*self.order.pop(0)))
        return mine


def per_device(
    x_slots, counts, cotangent, w_qkv, w_proj, w_fc1, w_fc2, small_params,
    moment_qkv, moment_proj, moment_fc1, moment_fc2, moment_small,
    square_qkv, square_proj, square_fc1, square_fc2, square_small,
):
    slots, per_even = x_slots.shape[0], cotangent.shape[0]
    win_at, grp_at = lax.axis_index("win"), lax.axis_index("grp")
    wins, grps = lax.axis_size("win"), lax.axis_size("grp")
    base = (win_at * grps + grp_at) * per_even
    count = counts[0]
    prev, nxt = neighbours(lax.dynamic_slice_in_dim(x_slots, count - 1, 1, 0), x_slots[:1])
    offset = windows_before(counts, per_even * wins * grps)[0]
    window = base + jnp.arange(per_even, dtype=jnp.int32)
    slot = window - offset
    spot = window % (GRID * GRID)
    info = jnp.stack(
        [
            jnp.clip(slot, 0, slots - 1),
            jnp.where(slot < 0, 1, jnp.where(slot >= count, 2, 0)),
            SIDE - WS * (spot // GRID),
            SIDE - WS * (spot % GRID),
        ],
        axis=1,
    ).astype(jnp.int32)
    vec, tab_fwd = vectors(small_params), forward_tables(small_params)
    blocks = lambda grad: grad.reshape(grps // 2, wins, D // wins, grad.shape[2])
    core = (grp_at & 1).astype(jnp.int32).reshape(1)
    flat = lambda a: a.reshape(per_even * TP, a.shape[2])
    xpad, n1, qkv, p_t, o, h, n2 = forward_attention(
        info, x_slots, prev, nxt, w_qkv, w_proj, vec, tab_fwd
    )
    later = tie(small_params, n2)
    b1 = later[8 * D : 8 * D + FF].astype(f32).reshape(1, FF)
    tab_bwd = backward_tables(later)
    n2, h, n1, o, xpad = flat(n2), flat(h), flat(n1), flat(o), flat(xpad)
    gl, slope, keep, send, dz, sum_b2 = feed_up(info, core, n2, cotangent, w_fc1, b1)
    if wins != keep.shape[1]:
        again = lambda a: a.transpose(0, 2, 1, 3).reshape(grps // 2, D // grps, wins, FF // wins).transpose(0, 2, 1, 3)
        keep, send = again(keep), again(send)
    fc2 = Chunk(keep, send, 0)
    fc2.finish = lambda kept, came: adam(kept, came, own_fc2, [moment_fc2.T], [square_fc2.T])
    *half, acc = feed_down(info, core, dz, slope, n2, w_fc1, w_fc2, 0, 2)
    sent = fc2.step(acc)
    keep, send, sum_b1, dh, da, do, sums_two = feed_down(
        info, core, tie(dz, *sent), slope, n2, w_fc1, w_fc2, 2, 2, (h, w_proj, vec, *half, acc)
    )
    do = do.reshape(per_even, TP, D)
    sent = fc2.step(do)
    fc1 = Chunk(blocks(tie(keep, *sent)), blocks(tie(send, *sent)), 1)
    fc1.finish = lambda kept, came: adam(kept, came, own_fc1, [moment_fc1], [square_fc1])
    dqkv, table, sum_qkv = backward_attention(qkv, p_t, tie(do, send, *sent), tab_bwd, 0, 1)
    sent = fc1.step(table)
    sent = (*sent, fc2.step(*sent))
    dqkv, table_two, sum_two = backward_attention(
        qkv, p_t, tie(do, *sent), tab_bwd, 1, per_even - 1, dqkv
    )
    table, sum_qkv = table + table_two, sum_qkv + sum_two
    sent = fc1.step(table_two)
    sent = (*sent, fc2.step(*sent))
    dqkv = flat(dqkv)
    keep, send = attention_weights(core, n1, tie(dqkv, *sent), o, da)
    sent = fc1.step(keep)
    attn = Chunk(blocks(tie(keep, sent)), blocks(tie(send, sent)), 1)
    attn.finish = lambda kept, came: adam(
        kept, came, own_attn, [moment_qkv, moment_proj], [square_qkv, square_proj]
    )
    dx, sums_one = input_gradient(info, tie(dqkv, send, sent), w_qkv, xpad, dh, vec)
    sent = attn.step(sums_one)
    sums = (table, sum_qkv, sums_one, sums_two, sum_b1, sum_b2)
    sums, offset, dx, win_later = tie((sums, offset, dx, win_at), *sent)
    table, sum_qkv, sums_one, sums_two, sum_b1, sum_b2 = sums
    dx_prev, dx_next = neighbours(dx[per_even - 1 :], dx[:1])
    own_attn, own_fc1, own_fc2 = own_blocks(win_later, grp_at, wins, grps, w_qkv, w_proj, w_fc1, w_fc2)
    rel_h = (table[0:RELN, 64:] + table[64 : 64 + RELN, :64])[::-1]
    rel_w = table[32 : 32 + RELN, 64:] + table[96 : 96 + RELN, :64]
    small = Total(
        jnp.concatenate(
            [
                sums_one[0], sums_two[0], sums_one[1], sums_two[1], sum_qkv[0, :D], sum_qkv[0, 2 * D :],
                sums_two[2], sum_b2[0], sum_b1[0], rel_h.reshape(-1), rel_w.reshape(-1),
            ]
        )
    )
    place = offset + jnp.arange(slots, dtype=jnp.int32) - base
    live = jnp.arange(slots) < count
    back = jnp.where(place < 0, 1, jnp.where(place >= per_even, 2, 0))
    back = jnp.stack([jnp.clip(place, 0, per_even - 1), jnp.where(live, back, 3)], axis=1)
    token = fc2.step(*sent, own_fc2)
    token = fc1.step(token)
    made = {}

    def slots_gap(token):
        made["dx"] = to_slots(tie(back.astype(jnp.int32), token), dx, dx_prev, dx_next)
        return made["dx"]

    def place_gap(name, chunk, way):
        def gap(token):
            chunk.pieces[0].came = tie(chunk.pieces[0].came, token)
            made[name] = chunk.all(way)
            return made[name][0]

        return gap

    ends = [(fc2, place_gap("fc2", fc2, "lanes")), (fc1, place_gap("fc1", fc1, "rows"))]
    while attn.left() or fc2.left() or fc1.left() or small.left():
        done = [end for end in ends if not end[0].left()]
        for chunk in (attn, fc2, fc1, small):
            if chunk.left():
                token = chunk.step(token)
        for end in done[:1]:
            token = end[1](token)
            ends.remove(end)
    for end in ends:
        token = end[1](token)
    made["out"] = token = feed_out(info, tie(gl, token), w_fc2, h, vec)
    token = slots_gap(token)
    attn.pieces[0].came = tie(attn.pieces[0].came, token)
    block_out, input_grad = made["out"], made["dx"]
    part_d, next_m_fc2, next_v_fc2 = (one[0].T for one in fc2.result)
    (part_c,), (next_m_fc1,), (next_v_fc1,) = fc1.result
    (part_a, part_b), (next_m_qkv, next_m_proj), (next_v_qkv, next_v_proj) = attn.result
    new_fc2, new_fc1 = made["fc2"][0].T, made["fc1"][0]
    new_qkv, new_proj = (part.T for part in attn.all("turned", (3 * D // grps, D // grps)))
    grad_small = small.vector
    upd_small = adam_step(small_params.astype(f32), grad_small, moment_small, square_small)
    return (
        block_out, input_grad, part_a, part_b, part_c, part_d, grad_small,
        next_m_qkv, next_m_proj, next_m_fc1, next_m_fc2, upd_small[0],
        next_v_qkv, next_v_proj, next_v_fc1, next_v_fc2, upd_small[1],
        new_qkv, new_proj, new_fc1, new_fc2, upd_small[2],
    )


def solution(mesh):
    data, shard, same, part = P(AXES, None, None), P("win", "grp"), P(), P(None, "grp")
    in_specs = (data, P(AXES), data) + (same,) * 5 + ((shard,) * 4 + (same,)) * 2
    out_specs = (data,) * 2 + ((shard,) * 4 + (same,)) * 3 + (part,) * 4 + (same,)
    return jax.shard_map(
        per_device, mesh=mesh, in_specs=in_specs, out_specs=out_specs, check_vma=False
    )
```

```python
import functools

import jax
import jax.numpy as jnp
import numpy as np
from jax import lax
from jax.experimental import pallas as pl
from jax.experimental.pallas import tpu as pltpu
from jax.sharding import PartitionSpec as P

D = 768
HEADS = 12
HD = 64
FF = 3072
WS = 14
SIDE = 64
STEP = 4
TOKW = 196
GRID = 5
RELN = 27
TP = 224

root_half = 0.7071067811865476
inv_root_two_pi = 0.3989422804014327
learn_rate = 0.06
bf16 = jnp.bfloat16
f32 = jnp.float32
VMEM_LIMIT = 56 << 20


def dot(a, b):
    return lax.dot_general(a, b, (((1,), (0,)), ((), ())), preferred_element_type=f32)


def dot_nt(a, b):
    return lax.dot_general(a, b, (((1,), (1,)), ((), ())), preferred_element_type=f32)


def dot_tn(a, b):
    return lax.dot_general(a, b, (((0,), (0,)), ((), ())), preferred_element_type=f32)


def iota(shape, axis):
    return lax.broadcasted_iota(jnp.int32, shape, axis)


def spread():
    row, token = iota((TP, TOKW), 0), iota((TP, TOKW), 1)
    hit = ((row & 15) < WS) & (token == WS * (row >> 4) + (row & 15))
    return hit.astype(f32).astype(bf16)


def gather_rows():
    token, row = iota((TOKW, TP), 0), iota((TOKW, TP), 1)
    hit = ((row & 15) < WS) & (token == WS * (row >> 4) + (row & 15))
    return hit.astype(f32).astype(bf16)


def key_lanes():
    row, lane = iota((TP, 128), 0), iota((TP, 128), 1)
    i, j = row >> 4, row & 15
    hit = (lane == i) | ((lane >= 64) & (lane < 64 + WS) & (lane - 64 == j))
    shut = (lane == 127) & (j >= WS)
    hit = hit.astype(f32)
    return hit.astype(bf16), jnp.where(shut, -1e30, hit).astype(bf16)


def inside(limit_row, limit_col):
    row = iota((TP, 1), 0)
    i, j = row >> 4, row & 15
    return ((i < limit_row) & (j < jnp.minimum(limit_col, WS))).astype(f32)


def norm_parts(v):
    centered = v - jnp.mean(v, axis=-1, keepdims=True)
    scale_inv = lax.rsqrt(jnp.mean(centered * centered, axis=-1, keepdims=True) + 1e-06)
    return centered * scale_inv, scale_inv


def norm_back(e, normed, scale_inv):
    return scale_inv * (
        e
        - jnp.mean(e, axis=-1, keepdims=True)
        - normed * jnp.mean(e * normed, axis=-1, keepdims=True)
    )


def lane_mask(head):
    lane = iota((1, 128), 1)
    return ((lane < HD) if head == 0 else (lane >= HD)).astype(f32).astype(bf16)


def query_lanes(table):
    lane = iota((16, 128), 1)
    out = []
    for i in range(WS):
        tile = table[16 * i : 16 * i + 16]
        by_row = pltpu.roll(tile, 51 + i, 1)
        by_col = pltpu.roll(tile, 51, 1, stride=1, stride_axis=0)
        out.append(jnp.where(lane < 64, by_row, by_col))
    aug = jnp.concatenate(out, axis=0)
    high = aug.astype(bf16)
    low = (aug - high.astype(f32)).astype(bf16)
    return high, jnp.where(iota((TP, 128), 1) == 127, jnp.asarray(1.0, bf16), low)


def fwd_kernel(
    info, xs_ref, prev_ref, next_ref, wqkv_ref, wproj_ref, vec_ref, tab_ref,
    xpad_ref, n1_ref, qkv_ref, pt_ref, o_ref, h_ref, n2_ref,
):
    k = pl.program_id(0)
    source = info[k, 1]
    x = jnp.where(source == 0, xs_ref[0], jnp.where(source == 1, prev_ref[0], next_ref[0]))
    big = dot(spread(), x)
    xpad_ref[0] = big.astype(bf16)
    mask = inside(info[k, 2], info[k, 3])
    vec = vec_ref[...]
    normed, _ = norm_parts(big)
    n1 = (mask * (normed * vec[0:1] + vec[2:3])).astype(bf16)
    n1_ref[0] = n1
    for part, bias in enumerate((vec[4:5], 0.0, vec[5:6])):
        at = slice(D * part, D * part + D)
        qkv_ref[0, :, at] = (dot(n1, wqkv_ref[:, at]) + bias).astype(bf16)
    keys_open, keys_extra = key_lanes()
    for pair in range(HEADS // 2):
        at = 128 * pair
        q = qkv_ref[0, :, at : at + 128]
        key = jnp.concatenate([qkv_ref[0, :, D + at : D + at + 128], keys_open, keys_extra], axis=1)
        v_t = qkv_ref[0, :, 2 * D + at : 2 * D + at + 128].T
        tables = dot(q, tab_ref[...])
        sides = [query_lanes(tables[:, 128 * head : 128 * head + 128]) for head in range(2)]
        scores = [
            dot_nt(key, jnp.concatenate([q * (lane_mask(head) * 0.125), *sides[head]], axis=1))
            for head in range(2)
        ]
        peaks = [jnp.max(s, axis=0, keepdims=True) for s in scores]
        es = [jnp.exp(s - m) for s, m in zip(scores, peaks)]
        sums = [jnp.sum(e, axis=0, keepdims=True) for e in es]
        ps = [(e * (1.0 / l)).astype(bf16) for e, l in zip(es, sums)]
        outs = []
        for head in range(2):
            pt_ref[0, 2 * pair + head] = ps[head]
            outs.append(dot(v_t[HD * head : HD * head + HD], ps[head]))
        o_ref[0, :, at : at + 128] = jnp.concatenate(outs, axis=0).T.astype(bf16)
    a = dot(o_ref[0], wproj_ref[...]) + vec[6:7]
    h = mask * (big + a)
    h_ref[0] = h
    normed_two, _ = norm_parts(h)
    n2_ref[0] = (mask * (normed_two * vec[1:2] + vec[3:4])).astype(bf16)


def forward_attention(info, x_slots, prev, nxt, w_qkv, w_proj, vec, tab):
    windows = info.shape[0]
    one = lambda *tail: pl.BlockSpec((1,) + tail, lambda k, s: (k,) + (0,) * len(tail))
    whole = lambda a: pl.BlockSpec(a.shape, lambda k, s: (0,) * a.ndim)
    shape = lambda *tail, dtype=bf16: jax.ShapeDtypeStruct((windows,) + tail, dtype)
    return pl.pallas_call(
        fwd_kernel,
        grid_spec=pltpu.PrefetchScalarGridSpec(
            num_scalar_prefetch=1,
            grid=(windows,),
            in_specs=[
                pl.BlockSpec((1, TOKW, D), lambda k, s: (s[k, 0], 0, 0)),
                whole(prev), whole(nxt), whole(w_qkv), whole(w_proj), whole(vec), whole(tab),
            ],
            out_specs=[
                one(TP, D), one(TP, D), one(TP, 3 * D), one(HEADS, TP, TP), one(TP, D), one(TP, D), one(TP, D),
            ],
        ),
        out_shape=[
            shape(TP, D), shape(TP, D), shape(TP, 3 * D), shape(HEADS, TP, TP), shape(TP, D),
            shape(TP, D, dtype=f32), shape(TP, D),
        ],
        compiler_params=pltpu.CompilerParams(vmem_limit_bytes=VMEM_LIMIT),
        cost_estimate=pl.CostEstimate(flops=0, bytes_accessed=0, transcendentals=0),
        name="attention_forward",
    )(info, x_slots, prev, nxt, w_qkv, w_proj, vec, tab)


def vectors(small):
    return small[: 8 * D].astype(f32).reshape(8, D)


def forward_tables(small):
    tables = small[8 * D + FF :].reshape(2, RELN, HD)[:, ::-1]
    gap = jnp.zeros((64 - RELN, HD), bf16)
    one = jnp.concatenate([tables[1], gap, tables[0], gap], axis=0).T
    none = jnp.zeros_like(one)
    return jnp.block([[one, none], [none, one]])


def backward_tables(small):
    tables = small[8 * D + FF :].reshape(2, RELN, HD)
    gap = jnp.zeros((32 - RELN, HD), bf16)
    half = jnp.concatenate([tables[0, ::-1], gap, tables[1], gap], axis=0)
    nil = jnp.zeros_like(half)
    return jnp.block([[nil, half], [half, nil]])


def params(**more):
    return dict(
        compiler_params=pltpu.CompilerParams(vmem_limit_bytes=VMEM_LIMIT),
        cost_estimate=pl.CostEstimate(flops=0, bytes_accessed=0, transcendentals=0),
        **more,
    )


def whole(a):
    return pl.BlockSpec(a.shape, lambda k, *s: (0,) * a.ndim)


def sds(*dims, dtype=bf16):
    return jax.ShapeDtypeStruct(dims, dtype)


def masks(info, windows):
    return [inside(info[k, 2], info[k, 3]) for k in range(windows)]


def up_kernel(info, core, n2_ref, cot_ref, w1_ref, b1_ref, gl_ref, slope_ref, keep_ref, send_ref, dz_ref, b2_ref, dz_t):
    windows = cot_ref.shape[0]

    @pl.when(pl.program_id(0) == 0)
    def _():
        total = jnp.zeros((1, D), f32)
        for k, mask in enumerate(masks(info, windows)):
            part = dot(spread(), cot_ref[k]) * mask
            dz_ref[TP * k : TP * k + TP] = part.astype(bf16)
            total += jnp.sum(part, axis=0, keepdims=True)
        b2_ref[...] = total
        dz_t[...] = dz_ref[...].T

    u = dot(n2_ref[...], w1_ref[...]) + b1_ref[...]
    half = 0.5 * (1.0 + lax.erf(u * root_half))
    gl = (u * half).astype(bf16)
    gl_ref[...] = gl
    slope_ref[...] = (half + u * jnp.exp(-0.5 * u * u) * inv_root_two_pi).astype(bf16)
    grad = dot(dz_t[...], gl).astype(bf16)
    even = core[0] == 0
    rows, cols = keep_ref.shape[2:]
    for y in range(keep_ref.shape[0]):
        for w in range(keep_ref.shape[1]):
            at = slice(cols * w, cols * w + cols)
            first = grad[2 * rows * y : 2 * rows * y + rows, at]
            second = grad[2 * rows * y + rows : 2 * rows * y + 2 * rows, at]
            keep_ref[y, w] = jnp.where(even, first, second)
            send_ref[y, w] = jnp.where(even, second, first)


def feed_up(info, core, n2, cot, w_fc1, b1):
    rows = n2.shape[0]
    step = D
    steps = FF // step
    flat = pl.BlockSpec((rows, step), lambda k, *s: (0, k))
    half = pl.BlockSpec((2, 2, 192, 384), lambda k, *s: (0, k, 0, 0))
    return pl.pallas_call(
        up_kernel,
        grid_spec=pltpu.PrefetchScalarGridSpec(
            num_scalar_prefetch=2,
            grid=(steps,),
            in_specs=[
                whole(n2), whole(cot),
                pl.BlockSpec((D, step), lambda k, *s: (0, k)),
                pl.BlockSpec((1, step), lambda k, *s: (0, k)),
            ],
            out_specs=[
                flat, flat, half, half,
                pl.BlockSpec((rows, D), lambda k, *s: (0, 0)),
                pl.BlockSpec((1, D), lambda k, *s: (0, 0)),
            ],
            scratch_shapes=[pltpu.VMEM((D, rows), bf16)],
        ),
        out_shape=[
            sds(rows, FF), sds(rows, FF), sds(2, 8, 192, 384), sds(2, 8, 192, 384), sds(rows, D),
            sds(1, D, dtype=f32),
        ],
        name="feed_up",
        **params(),
    )(info, core, n2, cot, w_fc1, b1)


def down_kernel(
    info, core, dz_ref, slope_ref, n2_ref, w1_ref, w2_ref, *refs, last,
):
    if last:
        h_hbm, wproj_hbm, vec_ref, _, _, _, acc_hbm = refs[:7]
        keep_ref, send_ref, b1_ref, dh_ref, da_ref, do_ref, sums_ref = refs[7:14]
        n2_t, acc, h_ref, wproj_ref, acc_in, sems = refs[14:]
        copies = [
            pltpu.make_async_copy(src, dst, sems.at[k])
            for k, (src, dst) in enumerate(((acc_hbm, acc_in), (h_hbm, h_ref), (wproj_hbm, wproj_ref)))
        ]
    else:
        keep_ref, send_ref, b1_ref, acc, n2_t = refs
    step = pl.program_id(0)

    @pl.when(step == 0)
    def _():
        if last:
            for copy in copies:
                copy.start()
        n2_t[...] = n2_ref[...].T
        acc[...] = jnp.zeros_like(acc)

    du = dot_nt(dz_ref[...], w2_ref[...]) * slope_ref[...].astype(f32)
    du_low = du.astype(bf16)
    b1_ref[...] = jnp.sum(du_low.astype(f32), axis=0, keepdims=True)
    mine = (step & 1) == core[0]
    grad = dot(n2_t[...], du_low).astype(bf16)

    @pl.when(mine)
    def _():
        keep_ref[0] = grad

    @pl.when(jnp.logical_not(mine))
    def _():
        send_ref[0] = grad

    acc[...] += dot_nt(du_low, w1_ref[...])
    if not last:
        return

    @pl.when(step == pl.num_programs(0) - 1)
    def _():
        for copy in copies:
            copy.wait()
        vec = vec_ref[...]
        windows = acc.shape[0] // TP
        gain = jnp.zeros((1, D), f32)
        shift = jnp.zeros((1, D), f32)
        bias = jnp.zeros((1, D), f32)
        for k, mask in enumerate(masks(info, windows)):
            at = slice(TP * k, TP * k + TP)
            dn = (acc[at] + acc_in[at]) * mask
            normed, scale_inv = norm_parts(h_ref[at])
            gain += jnp.sum(dn * normed, axis=0, keepdims=True)
            shift += jnp.sum(dn, axis=0, keepdims=True)
            dh = mask * (dz_ref[at].astype(f32) + norm_back(dn * vec[1:2], normed, scale_inv))
            dh_ref[at] = dh
            da = dh.astype(bf16)
            da_ref[at] = da
            bias += jnp.sum(da.astype(f32), axis=0, keepdims=True)
            do_ref[at] = dot_nt(da, wproj_ref[...]).astype(bf16)
        sums_ref[0:1] = gain
        sums_ref[1:2] = shift
        sums_ref[2:3] = bias
        sums_ref[3:8] = jnp.zeros((5, D), f32)


def feed_down(info, core, dz, slope, n2, w_fc1, w_fc2, begin, steps, more=()):
    rows = n2.shape[0]
    step = D
    last = bool(more)
    hbm = pl.BlockSpec(memory_space=pl.ANY)
    inputs = [dz, slope, n2, w_fc1, w_fc2, *more]
    in_specs = [
        whole(dz),
        pl.BlockSpec((rows, step), lambda k, *s: (0, k + begin)),
        whole(n2),
        pl.BlockSpec((D, step), lambda k, *s: (0, k + begin)),
        pl.BlockSpec((step, D), lambda k, *s: (k + begin, 0)),
    ]
    half = pl.BlockSpec((1, D, step), lambda k, *s: ((k + begin) // 2, 0, 0))
    out_specs = [half, half, pl.BlockSpec((1, step), lambda k, *s: (0, k + begin))]
    out_shape = [sds(2, D, D), sds(2, D, D), sds(1, FF, dtype=f32)]
    flat = pl.BlockSpec((rows, D), lambda k, *s: (0, 0))
    scratch = [pltpu.VMEM((D, rows), bf16)]
    aliases = {}
    if last:
        h, w_proj, vec, keep, send, b1, acc = more
        in_specs += [hbm, hbm, whole(vec), hbm, hbm, hbm, hbm]
        aliases = {10: 0, 11: 1, 12: 2}
        out_specs += [flat] * 3 + [pl.BlockSpec((8, D), lambda k, *s: (0, 0))]
        out_shape += [sds(rows, D, dtype=f32), sds(rows, D), sds(rows, D), sds(8, D, dtype=f32)]
        scratch += [
            pltpu.VMEM((rows, D), f32), pltpu.VMEM((rows, D), f32), pltpu.VMEM((D, D), bf16),
            pltpu.VMEM((rows, D), f32), pltpu.SemaphoreType.DMA((3,)),
        ]
    else:
        out_specs += [flat]
        out_shape += [sds(rows, D, dtype=f32)]
    return pl.pallas_call(
        functools.partial(down_kernel, last=last),
        grid_spec=pltpu.PrefetchScalarGridSpec(
            num_scalar_prefetch=2, grid=(steps,), in_specs=in_specs, out_specs=out_specs,
            scratch_shapes=scratch,
        ),
        out_shape=out_shape,
        input_output_aliases=aliases,
        name="feed_down",
        **params(),
    )(info, core, *inputs)


def out_kernel(info, gl_ref, w2_ref, h_ref, vec_ref, out_ref, acc):
    step = pl.program_id(0)

    @pl.when(step == 0)
    def _():
        acc[...] = h_ref[...]

    acc[...] += dot(gl_ref[...], w2_ref[...])

    @pl.when(step == pl.num_programs(0) - 1)
    def _():
        for k, mask in enumerate(masks(info, out_ref.shape[0])):
            at = slice(TP * k, TP * k + TP)
            y = (mask * (acc[at] + vec_ref[7:8])).astype(bf16)
            out_ref[k] = dot(gather_rows(), y).astype(bf16)


def feed_out(info, gl, w_fc2, h, vec):
    rows = gl.shape[0]
    windows = rows // TP
    step = D
    return pl.pallas_call(
        out_kernel,
        grid_spec=pltpu.PrefetchScalarGridSpec(
            num_scalar_prefetch=1,
            grid=(FF // step,),
            in_specs=[
                pl.BlockSpec((rows, step), lambda k, s: (0, k)),
                pl.BlockSpec((step, D), lambda k, s: (k, 0)),
                whole(h), whole(vec),
            ],
            out_specs=pl.BlockSpec((windows, TOKW, D), lambda k, s: (0, 0, 0)),
            scratch_shapes=[pltpu.VMEM((rows, D), f32)],
        ),
        out_shape=sds(windows, TOKW, D),
        name="feed_out",
        **params(),
    )(info, gl, w_fc2, h, vec)


def key_rows():
    lane, col = iota((64, TP), 0), iota((64, TP), 1)
    i, j = col >> 4, col & 15
    hit = ((lane < WS) & (lane == i)) | ((lane >= 32) & (lane < 32 + WS) & (lane - 32 == 13 - j))
    return hit.astype(f32).astype(bf16)


def grad_rolls(table, base):
    lane = iota((16, 128), 1)
    out = []
    for i in range(WS):
        tile = table[16 * i : 16 * i + 16]
        by_row = jnp.where((lane >= base) & (lane < base + WS), tile, 0.0)
        by_row = pltpu.roll(by_row, 13 - i, 1) if i < 13 else by_row
        by_col = jnp.where((lane >= base + 32) & (lane < base + 32 + WS), tile, 0.0)
        out.append(by_row + pltpu.roll(by_col, 0, 1, stride=1, stride_axis=0))
    return jnp.concatenate(out, axis=0)


def back_kernel(qkv_ref, pt_ref, do_ref, tab_ref, *refs):
    dqkv_ref, table_ref, sums_ref = refs[-3:]

    @pl.when(pl.program_id(0) == 0)
    def _():
        table_ref[...] = jnp.zeros_like(table_ref)
        sums_ref[...] = jnp.zeros_like(sums_ref)

    rows_extra = key_rows()
    lane = iota((TP, 128), 1)
    for pair in range(HEADS // 2):
        at = 128 * pair
        q = qkv_ref[0, :, at : at + 128]
        key_t = (qkv_ref[0, :, D + at : D + at + 128] * jnp.asarray(0.125, bf16)).T
        v = qkv_ref[0, :, 2 * D + at : 2 * D + at + 128]
        do = do_ref[0, :, at : at + 128]
        ds_all, dq_all, z_all = [], [], []
        for head in range(2):
            p_t = pt_ref[0, 2 * pair + head].astype(f32)
            dp_t = dot_nt(v, do * lane_mask(head))
            mean = jnp.sum(p_t * dp_t, axis=0, keepdims=True) / jnp.sum(p_t, axis=0, keepdims=True)
            ds_t = (p_t * (dp_t - mean)).astype(bf16)
            ds_all.append(ds_t)
            if head == 0:
                left = jnp.concatenate([key_t[:HD], rows_extra], axis=0)
            else:
                left = jnp.concatenate([rows_extra, key_t[HD:]], axis=0)
            back = dot(left, ds_t).T
            dq_all.append(back)
            z_all.append(grad_rolls(back, 64 if head == 0 else 0))
        z = jnp.where(lane < HD, z_all[1], z_all[0]).astype(bf16)
        dq = jnp.where(lane < HD, dq_all[0], dq_all[1]) + dot(z, tab_ref[...])
        table_ref[...] += dot(z.T, q)
        two = lambda a: jnp.concatenate([a * lane_mask(0), a * lane_mask(1)], axis=0)
        dk = dot(jnp.concatenate(ds_all, axis=1), two(q)) * 0.125
        p_two = jnp.concatenate([pt_ref[0, 2 * pair], pt_ref[0, 2 * pair + 1]], axis=1)
        dv = dot(p_two, two(do))
        dqkv_ref[0, :, at : at + 128] = dq.astype(bf16)
        dqkv_ref[0, :, D + at : D + at + 128] = dk.astype(bf16)
        dqkv_ref[0, :, 2 * D + at : 2 * D + at + 128] = dv.astype(bf16)
    sums_ref[...] += jnp.sum(dqkv_ref[0].astype(f32), axis=0, keepdims=True)


def backward_attention(qkv, p_t, do, tab, begin, count, into=None):
    windows = qkv.shape[0]
    one = lambda *tail: pl.BlockSpec((1,) + tail, lambda k: (k + begin,) + (0,) * len(tail))
    inputs = [qkv, p_t, do, tab]
    in_specs = [one(TP, 3 * D), one(HEADS, TP, TP), one(TP, D), whole(tab)]
    if into is not None:
        inputs.append(into)
        in_specs.append(pl.BlockSpec(memory_space=pl.ANY))
    return pl.pallas_call(
        back_kernel,
        grid=(count,),
        in_specs=in_specs,
        out_specs=[
            one(TP, 3 * D),
            pl.BlockSpec((128, 128), lambda k: (0, 0)),
            pl.BlockSpec((1, 3 * D), lambda k: (0, 0)),
        ],
        out_shape=[sds(windows, TP, 3 * D), sds(128, 128, dtype=f32), sds(1, 3 * D, dtype=f32)],
        input_output_aliases={} if into is None else {4: 0},
        name="attention_backward",
        **params(),
    )(*inputs)


def weight_kernel(
    core, n1_ref, dqkv_ref, o_ref, da_ref, keep_ref, send_ref, n1_t, o_t
):
    @pl.when(pl.program_id(0) == 0)
    def _():
        n1_t[...] = n1_ref[...].T
        o_t[...] = o_ref[...].T

    part = dot(n1_t[...], dqkv_ref[...])
    proj = dot(o_t[...], da_ref[...])
    lane = iota((D, 128), 1) < 64
    even = core[0] == 0

    def put(at, first, second):
        first, second = first.astype(bf16), second.astype(bf16)
        keep_ref[0, :, at] = jnp.where(even, first, second)
        send_ref[0, :, at] = jnp.where(even, second, first)

    moved = pltpu.roll(proj[:, 0:256], 64, 1)
    rolled = pltpu.roll(part[:, 512:1152], 576, 1)
    put(slice(0, 512), part[:, 0:512], rolled[:, 0:512])
    put(
        slice(512, 640),
        jnp.where(lane, part[:, 512:640], moved[:, 0:128]),
        jnp.where(lane, rolled[:, 512:640], proj[:, 128:256]),
    )
    put(slice(640, 768), moved[:, 128:256], proj[:, 256:384])


def attention_weights(core, n1, dqkv, o, da):
    rows = n1.shape[0]
    wide = 3 * D // 2
    half = pl.BlockSpec((1, D, D), lambda k, *s: (k, 0, 0))
    return pl.pallas_call(
        weight_kernel,
        grid_spec=pltpu.PrefetchScalarGridSpec(
            num_scalar_prefetch=1,
            grid=(2,),
            in_specs=[
                whole(n1),
                pl.BlockSpec((rows, wide), lambda k, *s: (0, k)),
                whole(o),
                pl.BlockSpec((rows, D // 2), lambda k, *s: (0, k)),
            ],
            out_specs=[half] * 2,
            scratch_shapes=[pltpu.VMEM((D, rows), bf16), pltpu.VMEM((D, rows), bf16)],
        ),
        out_shape=[sds(2, D, D)] * 2,
        name="attention_weights",
        **params(),
    )(core, n1, dqkv, o, da)


def input_kernel(info, dqkv_ref, wqkv_ref, xpad_ref, dh_ref, vec_ref, dx_ref, sums_ref):
    vec = vec_ref[...]
    acc = dot_nt(dqkv_ref[...], wqkv_ref[...])
    k = pl.program_id(0)
    mask = inside(info[k, 2], info[k, 3])
    dn = acc * mask
    normed, scale_inv = norm_parts(xpad_ref[...].astype(f32))
    dx = dh_ref[...] + norm_back(dn * vec[0:1], normed, scale_inv)
    dx_ref[0] = dot(gather_rows(), dx.astype(bf16)).astype(bf16)

    @pl.when(k == 0)
    def _():
        sums_ref[...] = jnp.zeros_like(sums_ref)

    sums_ref[0:1] += jnp.sum(dn * normed, axis=0, keepdims=True)
    sums_ref[1:2] += jnp.sum(dn, axis=0, keepdims=True)


def input_gradient(info, dqkv, w_qkv, xpad, dh, vec):
    rows = xpad.shape[0]
    windows = rows // TP
    return pl.pallas_call(
        input_kernel,
        grid_spec=pltpu.PrefetchScalarGridSpec(
            num_scalar_prefetch=1,
            grid=(windows,),
            in_specs=[
                pl.BlockSpec((TP, 3 * D), lambda k, s: (k, 0)),
                whole(w_qkv),
                pl.BlockSpec((TP, D), lambda k, s: (k, 0)),
                pl.BlockSpec((TP, D), lambda k, s: (k, 0)),
                whole(vec),
            ],
            out_specs=[
                pl.BlockSpec((1, TOKW, D), lambda k, s: (k, 0, 0)),
                pl.BlockSpec((8, D), lambda k, s: (0, 0)),
            ],
        ),
        out_shape=[sds(windows, TOKW, D), sds(8, D, dtype=f32)],
        name="input_gradient",
        **params(),
    )(info, dqkv, w_qkv, xpad, dh, vec)


first_fix = 1.0 - 0.5**STEP
second_fix = float(np.float32(1.0) - np.power(np.float32(0.999), np.float32(STEP)))


def adam_step(parameter, gradient, moment, square):
    moment_next = 0.5 * moment + 0.5 * gradient
    square_next = 0.999 * square + 0.001 * gradient * gradient
    fresh_weight = parameter - learn_rate * (moment_next / first_fix) / (
        jnp.sqrt(square_next / second_fix) + 1e-08
    )
    return moment_next, square_next, fresh_weight.astype(bf16)


def adam_kernel(kept_ref, came_ref, own_ref, *refs):
    parts = (len(refs) - 1) // 5
    moments, squares, grads, moments_next, squares_next = (
        refs[parts * k : parts * k + parts] for k in range(5)
    )
    total = kept_ref[...].astype(f32) + came_ref[...].astype(f32)
    own = own_ref[...].astype(f32)
    begin, fresh = 0, []
    for k in range(parts):
        at = slice(begin, begin + moments[k].shape[1])
        grads[k][...] = total[:, at]
        moment, square, weight = adam_step(own[:, at], total[:, at], moments[k][...], squares[k][...])
        moments_next[k][...] = moment
        squares_next[k][...] = square
        fresh.append(weight.astype(f32))
        begin = at.stop
    fresh = fresh[0] if parts == 1 else jnp.concatenate(fresh, axis=1)
    refs[-1][...] = fresh.astype(bf16)


def adam(kept, came, own, moments, squares):
    shapes = [sds(*m.shape, dtype=f32) for m in moments]
    out = pl.pallas_call(
        adam_kernel,
        out_shape=shapes * 3 + [sds(*kept.shape)],
        name="adam",
        **params(),
    )(kept, came, own, *moments, *squares)
    parts = len(moments)
    return [out[parts * k : parts * k + parts] for k in range(3)], out[-1]


def own_kernel(at, qkv_hbm, proj_hbm, fc1_hbm, fc2_hbm, attn_ref, fc1_ref, fc2_ref, qkv, proj, fc1, fc2, sems):
    win, grp = at[0], at[1]
    odd = (grp & 1) == 1

    def columns(width, more):
        return pl.ds(pl.multiple_of(width * grp - 64 * (grp & 1), 128), more)

    rows = fc1_ref.shape[0]
    some = pl.ds(pl.multiple_of(win * rows, 16), rows)
    many = pl.ds(pl.multiple_of(win * fc2.shape[0], 16), fc2.shape[0])
    copies = [
        pltpu.make_async_copy(qkv_hbm.at[some, columns(3 * D // 4, 640)], qkv, sems.at[0]),
        pltpu.make_async_copy(proj_hbm.at[some, columns(D // 4, 256)], proj, sems.at[1]),
        pltpu.make_async_copy(fc1_hbm.at[some, pl.ds(pl.multiple_of(D * grp, 128), D)], fc1, sems.at[2]),
        pltpu.make_async_copy(fc2_hbm.at[many, columns(D // 4, 256)], fc2, sems.at[3]),
    ]
    for copy in copies:
        copy.start()
    for copy in copies:
        copy.wait()

    def aligned(ref):
        whole = ref[...].astype(f32)
        return jnp.where(odd, pltpu.roll(whole, whole.shape[1] - 64, 1), whole)

    left, right = aligned(qkv), aligned(proj)
    attn_ref[:, 0:512] = left[:, 0:512].astype(bf16)
    right = pltpu.roll(right, 64, 1)
    lane = iota((rows, 128), 1) < 64
    attn_ref[:, 512:640] = jnp.where(lane, left[:, 512:640], right[:, 0:128]).astype(bf16)
    attn_ref[:, 640:768] = right[:, 128:256].astype(bf16)
    fc1_ref[...] = fc1[...]
    fc2_ref[...] = aligned(fc2).T[0 : D // 4].astype(bf16)


def own_blocks(win, grp, wins, grps, w_qkv, w_proj, w_fc1, w_fc2):
    rows, many = D // wins, FF // wins
    if grps != 4 or rows % 16 or many % 128:
        cut = lambda w, r, c: lax.dynamic_slice(w, (win * r, grp * c), (r, c))
        attn = [cut(w_qkv, rows, 3 * D // grps), cut(w_proj, rows, D // grps)]
        return jnp.concatenate(attn, axis=1), cut(w_fc1, rows, FF // grps), cut(w_fc2, many, D // grps).T
    hbm = pl.BlockSpec(memory_space=pl.ANY)
    vmem = pl.BlockSpec(memory_space=pltpu.VMEM)
    return pl.pallas_call(
        own_kernel,
        in_specs=[pl.BlockSpec(memory_space=pltpu.SMEM)] + [hbm] * 4,
        out_specs=[vmem] * 3,
        out_shape=[sds(rows, D), sds(rows, D), sds(D // 4, many)],
        scratch_shapes=[
            pltpu.VMEM((rows, 640), bf16), pltpu.VMEM((rows, 256), bf16), pltpu.VMEM((rows, D), bf16),
            pltpu.VMEM((many, 256), bf16), pltpu.SemaphoreType.DMA((4,)),
        ],
        name="own_blocks",
        **params(),
    )(jnp.stack([win, grp]).astype(jnp.int32), w_qkv, w_proj, w_fc1, w_fc2)


def place_kernel(at, have_ref, came_ref, *refs, way):
    half = have_ref.shape[0]
    rows, columns = have_ref.shape[1:]
    for target in range(2 * half):
        place = at[target]
        near = have_ref[jnp.minimum(place, half - 1)]
        far = came_ref[jnp.maximum(place - half, 0)]
        block = jnp.where(place < half, near, far)
        if way == "lanes":
            refs[0][:, columns * target : columns * target + columns] = block
        else:
            refs[-1 if way == "turned" else 0][rows * target : rows * target + rows] = block
    if way == "turned":
        whole = refs[-1][...].T
        begin = 0
        for out in refs[:-1]:
            out[...] = whole[begin : begin + out.shape[0]]
            begin += out.shape[0]


def put_in_place(at, have, came, way, widths=()):
    count, rows, columns = 2 * have.shape[0], have.shape[1], have.shape[2]
    smem = pl.BlockSpec(memory_space=pltpu.SMEM)
    vmem = pl.BlockSpec(memory_space=pltpu.VMEM)
    scratch = []
    if way == "lanes":
        shapes = [sds(rows, count * columns)]
    elif way == "rows":
        shapes = [sds(count * rows, columns)]
    else:
        shapes = [sds(width, count * rows) for width in widths]
        scratch = [pltpu.VMEM((count * rows, columns), bf16)]
    return pl.pallas_call(
        functools.partial(place_kernel, way=way),
        in_specs=[smem, vmem, vmem],
        out_specs=[vmem] * len(shapes),
        out_shape=shapes,
        scratch_shapes=scratch,
        name="put_in_place",
        **params(),
    )(at, have, came)


def slots_kernel(at, dx_hbm, prev_hbm, next_hbm, out_hbm, held, sems):
    count = dx_hbm.shape[0]
    loads = [
        pltpu.make_async_copy(ref, held.at[pl.ds(begin, ref.shape[0])], sems.at[k])
        for k, (begin, ref) in enumerate(((0, dx_hbm), (count, prev_hbm), (count + 1, next_hbm)))
    ]
    for load in loads:
        load.start()
    held[count + 2] = jnp.zeros(held.shape[1:], bf16)
    for load in loads:
        load.wait()
    stores = [
        pltpu.make_async_copy(held.at[at[slot]], out_hbm.at[slot], sems.at[3 + slot])
        for slot in range(out_hbm.shape[0])
    ]
    for store in stores:
        store.start()
    for store in stores:
        store.wait()


def to_slots(at, dx, prev, nxt):
    slots, count = at.shape[0], dx.shape[0]
    hbm = pl.BlockSpec(memory_space=pl.ANY)
    return pl.pallas_call(
        slots_kernel,
        in_specs=[pl.BlockSpec(memory_space=pltpu.SMEM), hbm, hbm, hbm],
        out_specs=hbm,
        out_shape=sds(slots, TOKW, D),
        scratch_shapes=[
            pltpu.VMEM((count + 3, TOKW, D), bf16), pltpu.SemaphoreType.DMA((3 + slots,)),
        ],
        name="to_slots",
        **params(),
    )(at, dx, prev, nxt)


AXES = ("win", "grp")


def bits_of(size):
    return [1 << k for k in range(size.bit_length() - 1)]


def flipped(axis, bit):
    wins, grps = lax.axis_size("win"), lax.axis_size("grp")
    out = []
    for d in range(wins * grps):
        w, g = divmod(d, grps)
        w, g = (w ^ bit, g) if axis == "win" else (w, g ^ bit)
        out.append((d, w * grps + g))
    return out


def windows_before(count, windows):
    total, before = count, jnp.zeros_like(count)
    bits = [(axis, bit) for axis in ("grp", "win") for bit in bits_of(lax.axis_size(axis))]
    for axis, bit in bits:
        last = (axis, bit) == bits[-1]
        other = windows - total if last else lax.ppermute(total, AXES, flipped(axis, bit))
        mine = (lax.axis_index(axis) & bit) != 0
        before = before + jnp.where(mine, other, 0)
        total = total + other
    return before


def neighbours(last, first):
    count = lax.axis_size("win") * lax.axis_size("grp")
    up = [(i, i + 1) for i in range(count - 1)]
    down = [(j, i) for i, j in up]
    return lax.ppermute(last, AXES, up), lax.ppermute(first, AXES, down)


def rising():
    return [(axis, bit) for axis in ("grp", "win") for bit in bits_of(lax.axis_size(axis))]


def tie(value, *others):
    return lax.optimization_barrier((value, *others))[0]


def places(order):
    apart = lax.axis_index("win") ^ jnp.arange(lax.axis_size("win"), dtype=jnp.int32)
    return sum(((apart & bit) != 0).astype(jnp.int32) << k for k, (_, bit) in enumerate(order))


class Piece:
    def __init__(self, kept, came, parts):
        self.kept, self.came, self.parts = kept, came, parts

    def halve(self, which, at=None, rider=None):
        axis, bit = which
        place = self.parts.index(which)
        parts = self.parts[:place] + self.parts[place + 1 :]
        mine = ((lax.axis_index(axis) & bit) != 0).astype(jnp.int32)
        split = (1 << place, 2, -1) + self.kept.shape[-2:]
        kept, came = self.kept.reshape(split), self.came.reshape(split)

        def pick(half):
            piece = lax.dynamic_index_in_dim(kept, half, 1, keepdims=False)
            other = lax.dynamic_index_in_dim(came, half, 1, keepdims=False)
            if at is not None:
                piece, other = piece[..., at[0], at[1]], other[..., at[0], at[1]]
            return (piece.astype(f32) + other.astype(f32)).astype(bf16)

        send, kept = pick(1 - mine), pick(mine)
        if rider is None:
            return send, Piece(kept, lax.ppermute(send, AXES, flipped(axis, bit)), parts)
        shape, columns = send.shape, send.shape[-1]
        send = jnp.concatenate([send.reshape(-1, columns), rider.rows(columns)], axis=0)
        came = lax.ppermute(send, AXES, flipped(axis, bit))
        rows = kept.size // columns
        rider.add(came[rows:])
        return send, Piece(kept, came[:rows].reshape(shape), parts)


class Chunk:
    def __init__(self, keep, send, axis):
        near, *self.grp = [one for one in rising() if one[0] == "grp"]
        self.win = [one for one in rising() if one[0] == "win"]
        parts = list(reversed(self.grp)) + list(reversed(self.win))
        self.pieces = [Piece(keep, lax.ppermute(send, AXES, flipped(*near)), parts)]
        self.block, self.axis, self.finish = keep.shape[-2:], axis, None
        self.cross = [(self.grp[-1], self.win[0]), (self.win[0], self.grp[-1])]
        self.order = self.grp[:-1] + self.win[1:]
        self.ways, self.back = list(reversed(self.win)), list(reversed(self.win))
        self.have, self.rider = None, None

    def left(self):
        return bool(self.cross or self.order or self.ways)

    def after(self, *others):
        if others:
            for piece in self.pieces:
                piece.came = tie(piece.came, *others)

    def step(self, *others):
        self.after(*others)
        if self.cross:
            whole, half = slice(None), self.block[self.axis] // 2
            cuts = [slice(0, half), slice(half, None)]
            ats = [(c, whole) if self.axis == 0 else (whole, c) for c in cuts]
            first, second = self.cross.pop(0)
            if len(self.pieces) == 1:
                (one,) = self.pieces
                made = [one.halve(first, ats[0]), one.halve(second, ats[1])]
            else:
                made = [self.pieces[0].halve(first, rider=self.rider), self.pieces[1].halve(second)]
            self.pieces = [piece for _, piece in made]
            return tuple(send for send, _ in made)
        if len(self.pieces) == 2:
            joined = lambda a, b: jnp.concatenate([a, b], axis=self.axis - 2)
            one, two = self.pieces
            shape = lambda a: a.reshape((-1,) + a.shape[-2:])
            self.pieces = [
                Piece(
                    joined(shape(one.kept), shape(two.kept)),
                    joined(shape(one.came), shape(two.came)),
                    one.parts,
                )
            ]
        (piece,) = self.pieces
        if self.order:
            send, piece = piece.halve(self.order.pop(0), rider=self.rider)
            self.pieces = [piece]
            return send
        if self.have is None:
            self.result, fresh = self.finish(piece.kept.reshape(self.block), piece.came.reshape(self.block))
            self.have = fresh[None]
        else:
            self.have = jnp.concatenate([self.have, piece.came], axis=0)
        piece.came = lax.ppermute(self.have, AXES, flipped(*self.ways.pop(0)))
        return self.have

    def all(self, way, widths=()):
        have, came = self.have, self.pieces[0].came
        if self.block[0] % 16 == 0 and self.block[1] % 128 == 0:
            return put_in_place(places(self.back), have, came, way, widths)
        blocks = jnp.concatenate([have, came], axis=0)[places(self.back)]
        if way == "lanes":
            return [blocks.transpose(1, 0, 2).reshape(blocks.shape[1], -1)]
        blocks = blocks.reshape(-1, blocks.shape[2])
        return [blocks] if way == "rows" else jnp.split(blocks.T, np.cumsum(widths)[:-1], axis=0)


class Total:
    def __init__(self, vector):
        self.vector = vector
        self.order = [one for one in rising() if one[0] == "grp"]

    def rows(self, columns):
        flat = jnp.pad(self.vector, (0, -self.vector.shape[0] % columns))
        return flat.reshape(-1, columns).astype(bf16)

    def add(self, rows):
        self.vector = self.vector + rows.reshape(-1)[: self.vector.shape[0]].astype(f32)

    def left(self):
        return bool(self.order)

    def step(self, *after):
        mine = tie(self.vector, *after)
        self.vector = mine + lax.ppermute(mine, AXES, flipped(*self.order.pop(0)))
        return mine


def per_device(
    x_slots, counts, cotangent, w_qkv, w_proj, w_fc1, w_fc2, small_params,
    moment_qkv, moment_proj, moment_fc1, moment_fc2, moment_small,
    square_qkv, square_proj, square_fc1, square_fc2, square_small,
):
    slots, per_even = x_slots.shape[0], cotangent.shape[0]
    win_at, grp_at = lax.axis_index("win"), lax.axis_index("grp")
    wins, grps = lax.axis_size("win"), lax.axis_size("grp")
    base = (win_at * grps + grp_at) * per_even
    count = counts[0]
    prev, nxt = neighbours(lax.dynamic_slice_in_dim(x_slots, count - 1, 1, 0), x_slots[:1])
    offset = windows_before(counts, per_even * wins * grps)[0]
    window = base + jnp.arange(per_even, dtype=jnp.int32)
    slot = window - offset
    spot = window % (GRID * GRID)
    info = jnp.stack(
        [
            jnp.clip(slot, 0, slots - 1),
            jnp.where(slot < 0, 1, jnp.where(slot >= count, 2, 0)),
            SIDE - WS * (spot // GRID),
            SIDE - WS * (spot % GRID),
        ],
        axis=1,
    ).astype(jnp.int32)
    vec, tab_fwd = vectors(small_params), forward_tables(small_params)
    blocks = lambda grad: grad.reshape(grps // 2, wins, D // wins, grad.shape[2])
    core = (grp_at & 1).astype(jnp.int32).reshape(1)
    flat = lambda a: a.reshape(per_even * TP, a.shape[2])
    xpad, n1, qkv, p_t, o, h, n2 = forward_attention(
        info, x_slots, prev, nxt, w_qkv, w_proj, vec, tab_fwd
    )
    later = tie(small_params, n2)
    b1 = later[8 * D : 8 * D + FF].astype(f32).reshape(1, FF)
    tab_bwd = backward_tables(later)
    n2, h, n1, o, xpad = flat(n2), flat(h), flat(n1), flat(o), flat(xpad)
    gl, slope, keep, send, dz, sum_b2 = feed_up(info, core, n2, cotangent, w_fc1, b1)
    if wins != keep.shape[1]:
        again = lambda a: a.transpose(0, 2, 1, 3).reshape(grps // 2, D // grps, wins, FF // wins).transpose(0, 2, 1, 3)
        keep, send = again(keep), again(send)
    fc2 = Chunk(keep, send, 0)
    fc2.finish = lambda kept, came: adam(kept, came, own_fc2, [moment_fc2.T], [square_fc2.T])
    *half, acc = feed_down(info, core, dz, slope, n2, w_fc1, w_fc2, 0, 2)
    sent = fc2.step(acc)
    keep, send, sum_b1, dh, da, do, sums_two = feed_down(
        info, core, tie(dz, *sent), slope, n2, w_fc1, w_fc2, 2, 2, (h, w_proj, vec, *half, acc)
    )
    do = do.reshape(per_even, TP, D)
    sent = fc2.step(do)
    fc1 = Chunk(blocks(tie(keep, *sent)), blocks(tie(send, *sent)), 1)
    fc1.finish = lambda kept, came: adam(kept, came, own_fc1, [moment_fc1], [square_fc1])
    dqkv, table, sum_qkv = backward_attention(qkv, p_t, tie(do, send, *sent), tab_bwd, 0, 1)
    sent = fc1.step(table)
    sent = (*sent, fc2.step(*sent))
    dqkv, table_two, sum_two = backward_attention(
        qkv, p_t, tie(do, *sent), tab_bwd, 1, per_even - 1, dqkv
    )
    table, sum_qkv = table + table_two, sum_qkv + sum_two
    sent = fc1.step(table_two)
    sent = (*sent, fc2.step(*sent))
    dqkv = flat(dqkv)
    keep, send = attention_weights(core, n1, tie(dqkv, *sent), o, da)
    fc1.after(keep)
    fc2.after(keep)
    send = tie(send, *(piece.came for piece in fc1.pieces + fc2.pieces))
    attn = Chunk(blocks(keep), blocks(send), 1)
    attn.finish = lambda kept, came: adam(
        kept, came, own_attn, [moment_qkv, moment_proj], [square_qkv, square_proj]
    )
    sent = fc1.step(send)
    win_later = tie(win_at, sent)
    own_attn, own_fc1, own_fc2 = own_blocks(win_later, grp_at, wins, grps, w_qkv, w_proj, w_fc1, w_fc2)
    sent = fc2.step(own_fc2)
    sent = attn.step(sent)
    dx, sums_one = input_gradient(info, tie(dqkv, *sent), w_qkv, xpad, dh, vec)
    sums = (table, sum_qkv, sums_one, sums_two, sum_b1, sum_b2)
    sums, offset = tie((sums, offset), sums_one)
    table, sum_qkv, sums_one, sums_two, sum_b1, sum_b2 = sums
    rel_h = (table[0:RELN, 64:] + table[64 : 64 + RELN, :64])[::-1]
    rel_w = table[32 : 32 + RELN, 64:] + table[96 : 96 + RELN, :64]
    small = Total(
        jnp.concatenate(
            [
                sums_one[0], sums_two[0], sums_one[1], sums_two[1], sum_qkv[0, :D], sum_qkv[0, 2 * D :],
                sums_two[2], sum_b2[0], sum_b1[0], rel_h.reshape(-1), rel_w.reshape(-1),
            ]
        )
    )
    place = offset + jnp.arange(slots, dtype=jnp.int32) - base
    back = jnp.where(place < 0, per_even, jnp.where(place >= per_even, per_even + 1, place))
    back = jnp.where(jnp.arange(slots) < count, back, per_even + 2).astype(jnp.int32)
    token = fc2.step(dx)
    token = fc1.step(token)
    attn.rider = small
    made = {}

    def slots_gap(token):
        made["dx"] = to_slots(tie(back, token), dx, dx_prev, dx_next)
        return made["dx"]

    def place_gap(name, chunk, way):
        def gap(token):
            chunk.pieces[0].came = tie(chunk.pieces[0].came, token)
            made[name] = chunk.all(way)
            return made[name][0]

        return gap

    ends = [(fc2, place_gap("fc2", fc2, "lanes")), (fc1, place_gap("fc1", fc1, "rows"))]
    while attn.left() or fc2.left() or fc1.left() or small.left():
        done = [end for end in ends if not end[0].left()]
        for chunk in (attn, fc2, fc1, small):
            if chunk.left() and (chunk is not small or not attn.order):
                token = chunk.step(token)
        for end in done[:1]:
            token = end[1](token)
            ends.remove(end)
    dx_prev, dx_next = neighbours(*tie((dx[per_even - 1 :], dx[:1]), token))
    made["out"] = token = feed_out(info, tie(gl, token), w_fc2, h, vec)
    for end in ends:
        token = end[1](token)
    attn.pieces[0].came = tie(attn.pieces[0].came, token)
    block_out = made["out"]
    made["attn"] = attn.all("turned", (3 * D // grps, D // grps))
    input_grad = slots_gap(made["attn"])
    part_d, next_m_fc2, next_v_fc2 = (one[0].T for one in fc2.result)
    (part_c,), (next_m_fc1,), (next_v_fc1,) = fc1.result
    (part_a, part_b), (next_m_qkv, next_m_proj), (next_v_qkv, next_v_proj) = attn.result
    new_fc2, new_fc1 = made["fc2"][0].T, made["fc1"][0]
    new_qkv, new_proj = (part.T for part in made["attn"])
    grad_small = small.vector
    upd_small = adam_step(small_params.astype(f32), grad_small, moment_small, square_small)
    return (
        block_out, input_grad, part_a, part_b, part_c, part_d, grad_small,
        next_m_qkv, next_m_proj, next_m_fc1, next_m_fc2, upd_small[0],
        next_v_qkv, next_v_proj, next_v_fc1, next_v_fc2, upd_small[1],
        new_qkv, new_proj, new_fc1, new_fc2, upd_small[2],
    )


def solution(mesh):
    data, shard, same, part = P(AXES, None, None), P("win", "grp"), P(), P(None, "grp")
    in_specs = (data, P(AXES), data) + (same,) * 5 + ((shard,) * 4 + (same,)) * 2
    out_specs = (data,) * 2 + ((shard,) * 4 + (same,)) * 3 + (part,) * 4 + (same,)
    return jax.shard_map(
        per_device, mesh=mesh, in_specs=in_specs, out_specs=out_specs, check_vma=False
    )
```

```python
import functools

import jax
import jax.numpy as jnp
import numpy as np
from jax import lax
from jax.experimental import pallas as pl
from jax.experimental.pallas import tpu as pltpu
from jax.sharding import PartitionSpec as P

D = 768
HEADS = 12
HD = 64
FF = 3072
WS = 14
SIDE = 64
STEP = 4
TOKW = 196
GRID = 5
RELN = 27
TP = 224

root_half = 0.7071067811865476
inv_root_two_pi = 0.3989422804014327
learn_rate = 0.06
bf16 = jnp.bfloat16
f32 = jnp.float32
VMEM_LIMIT = 56 << 20


def dot(a, b):
    return lax.dot_general(a, b, (((1,), (0,)), ((), ())), preferred_element_type=f32)


def dot_nt(a, b):
    return lax.dot_general(a, b, (((1,), (1,)), ((), ())), preferred_element_type=f32)


def dot_tn(a, b):
    return lax.dot_general(a, b, (((0,), (0,)), ((), ())), preferred_element_type=f32)


def iota(shape, axis):
    return lax.broadcasted_iota(jnp.int32, shape, axis)


def spread():
    row, token = iota((TP, TOKW), 0), iota((TP, TOKW), 1)
    hit = ((row & 15) < WS) & (token == WS * (row >> 4) + (row & 15))
    return hit.astype(f32).astype(bf16)


def gather_rows():
    token, row = iota((TOKW, TP), 0), iota((TOKW, TP), 1)
    hit = ((row & 15) < WS) & (token == WS * (row >> 4) + (row & 15))
    return hit.astype(f32).astype(bf16)


def key_lanes():
    row, lane = iota((TP, 128), 0), iota((TP, 128), 1)
    i, j = row >> 4, row & 15
    hit = (lane == i) | ((lane >= 64) & (lane < 64 + WS) & (lane - 64 == j))
    shut = (lane == 127) & (j >= WS)
    hit = hit.astype(f32)
    return hit.astype(bf16), jnp.where(shut, -1e30, hit).astype(bf16)


def inside(limit_row, limit_col):
    row = iota((TP, 1), 0)
    i, j = row >> 4, row & 15
    return ((i < limit_row) & (j < jnp.minimum(limit_col, WS))).astype(f32)


def norm_parts(v):
    centered = v - jnp.mean(v, axis=-1, keepdims=True)
    scale_inv = lax.rsqrt(jnp.mean(centered * centered, axis=-1, keepdims=True) + 1e-06)
    return centered * scale_inv, scale_inv


def norm_back(e, normed, scale_inv):
    return scale_inv * (
        e
        - jnp.mean(e, axis=-1, keepdims=True)
        - normed * jnp.mean(e * normed, axis=-1, keepdims=True)
    )


def lane_mask(head):
    lane = iota((1, 128), 1)
    return ((lane < HD) if head == 0 else (lane >= HD)).astype(f32).astype(bf16)


def query_lanes(table):
    lane = iota((16, 128), 1)
    out = []
    for i in range(WS):
        tile = table[16 * i : 16 * i + 16]
        by_row = pltpu.roll(tile, 51 + i, 1)
        by_col = pltpu.roll(tile, 51, 1, stride=1, stride_axis=0)
        out.append(jnp.where(lane < 64, by_row, by_col))
    aug = jnp.concatenate(out, axis=0)
    high = aug.astype(bf16)
    low = (aug - high.astype(f32)).astype(bf16)
    return high, jnp.where(iota((TP, 128), 1) == 127, jnp.asarray(1.0, bf16), low)


def vectors(small):
    return small[: 8 * D + FF].astype(f32).reshape(-1, D)


def forward_tables(small):
    tables = small[8 * D + FF :].reshape(2, RELN, HD)[:, ::-1]
    gap = jnp.zeros((64 - RELN, HD), bf16)
    one = jnp.concatenate([tables[1], gap, tables[0], gap], axis=0).T
    none = jnp.zeros_like(one)
    return jnp.block([[one, none], [none, one]])


def backward_tables(small):
    tables = small[8 * D + FF :].reshape(2, RELN, HD)
    gap = jnp.zeros((32 - RELN, HD), bf16)
    half = jnp.concatenate([tables[0, ::-1], gap, tables[1], gap], axis=0)
    nil = jnp.zeros_like(half)
    return jnp.block([[nil, half], [half, nil]])


def params(**more):
    return dict(
        compiler_params=pltpu.CompilerParams(vmem_limit_bytes=VMEM_LIMIT),
        cost_estimate=pl.CostEstimate(flops=0, bytes_accessed=0, transcendentals=0),
        **more,
    )


def whole(a):
    return pl.BlockSpec(a.shape, lambda k, *s: (0,) * a.ndim)


def sds(*dims, dtype=bf16):
    return jax.ShapeDtypeStruct(dims, dtype)


def masks(info, windows):
    return [inside(info[k, 2], info[k, 3]) for k in range(windows)]


def window_forward(
    k, info, xs_ref, prev_ref, next_ref, wqkv_ref, wproj_ref, vec_ref, tab_ref,
    xpad_ref, n1_ref, qkv_ref, pt_ref, o_ref, h_ref, n2_ref,
):
    source = info[k, 1]
    x = jnp.where(source == 0, xs_ref[0], jnp.where(source == 1, prev_ref[0], next_ref[0]))
    big = dot(spread(), x)
    xpad_ref[0] = big.astype(bf16)
    mask = inside(info[k, 2], info[k, 3])
    vec = vec_ref[...]
    normed, _ = norm_parts(big)
    n1 = (mask * (normed * vec[0:1] + vec[2:3])).astype(bf16)
    n1_ref[0] = n1
    for part, bias in enumerate((vec[4:5], 0.0, vec[5:6])):
        at = slice(D * part, D * part + D)
        qkv_ref[0, :, at] = (dot(n1, wqkv_ref[:, at]) + bias).astype(bf16)
    keys_open, keys_extra = key_lanes()
    for pair in range(HEADS // 2):
        at = 128 * pair
        q = qkv_ref[0, :, at : at + 128]
        key = jnp.concatenate([qkv_ref[0, :, D + at : D + at + 128], keys_open, keys_extra], axis=1)
        v_t = qkv_ref[0, :, 2 * D + at : 2 * D + at + 128].T
        tables = dot(q, tab_ref[...])
        sides = [query_lanes(tables[:, 128 * head : 128 * head + 128]) for head in range(2)]
        scores = [
            dot_nt(key, jnp.concatenate([q * (lane_mask(head) * 0.125), *sides[head]], axis=1))
            for head in range(2)
        ]
        peaks = [jnp.max(s, axis=0, keepdims=True) for s in scores]
        es = [jnp.exp(s - m) for s, m in zip(scores, peaks)]
        sums = [jnp.sum(e, axis=0, keepdims=True) for e in es]
        ps = [(e * (1.0 / l)).astype(bf16) for e, l in zip(es, sums)]
        outs = []
        for head in range(2):
            pt_ref[0, 2 * pair + head] = ps[head]
            outs.append(dot(v_t[HD * head : HD * head + HD], ps[head]))
        o_ref[0, :, at : at + 128] = jnp.concatenate(outs, axis=0).T.astype(bf16)
    a = dot(o_ref[0], wproj_ref[...]) + vec[6:7]
    h = mask * (big + a)
    h_ref[0] = h
    normed_two, _ = norm_parts(h)
    rows = pl.ds(pl.multiple_of(TP * k, 16), TP)
    n2_ref[rows, :] = (mask * (normed_two * vec[1:2] + vec[3:4])).astype(bf16)


def forward_kernel(
    info, core, xs_ref, prev_ref, next_ref, wqkv_ref, wproj_ref, vec_ref, tab_ref, cot_ref, w1_ref,
    xpad_ref, n1_ref, qkv_ref, pt_ref, o_ref, h_ref, n2_ref,
    gl_ref, slope_ref, keep_ref, send_ref, dz_ref, b2_ref, dz_t,
):
    windows = cot_ref.shape[0]
    step = pl.program_id(0)

    @pl.when(step < windows)
    def _():
        window_forward(
            step, info, xs_ref, prev_ref, next_ref, wqkv_ref, wproj_ref, vec_ref, tab_ref,
            xpad_ref, n1_ref, qkv_ref, pt_ref, o_ref, h_ref, n2_ref,
        )

    @pl.when(step == windows)
    def _():
        total = jnp.zeros((1, D), f32)
        for k, mask in enumerate(masks(info, windows)):
            part = dot(spread(), cot_ref[k]) * mask
            dz_ref[TP * k : TP * k + TP] = part.astype(bf16)
            total += jnp.sum(part, axis=0, keepdims=True)
        b2_ref[...] = total
        dz_t[...] = dz_ref[...].T

    @pl.when(step >= windows)
    def _():
        u = dot(n2_ref[...], w1_ref[...]) + vec_ref[pl.ds(8 + step - windows, 1), :]
        half = 0.5 * (1.0 + lax.erf(u * root_half))
        gl = (u * half).astype(bf16)
        gl_ref[...] = gl
        slope_ref[...] = (half + u * jnp.exp(-0.5 * u * u) * inv_root_two_pi).astype(bf16)
        grad = dot(dz_t[...], gl).astype(bf16)
        even = core[0] == 0
        rows, cols = keep_ref.shape[2:]
        for y in range(keep_ref.shape[0]):
            for w in range(keep_ref.shape[1]):
                at = slice(cols * w, cols * w + cols)
                first = grad[2 * rows * y : 2 * rows * y + rows, at]
                second = grad[2 * rows * y + rows : 2 * rows * y + 2 * rows, at]
                keep_ref[y, w] = jnp.where(even, first, second)
                send_ref[y, w] = jnp.where(even, second, first)


def forward(info, core, x_slots, prev, nxt, cot, w_qkv, w_proj, w_fc1, vec, tab):
    windows = info.shape[0]
    rows = windows * TP
    now = lambda k: jnp.minimum(k, windows - 1)
    late = lambda k: jnp.maximum(k - windows, 0)
    one = lambda *tail: pl.BlockSpec((1,) + tail, lambda k, *s: (now(k),) + (0,) * len(tail))
    shape = lambda *tail, dtype=bf16: sds(windows, *tail, dtype=dtype)
    flat = pl.BlockSpec((rows, D), lambda k, *s: (0, late(k)))
    half = pl.BlockSpec((2, 2, 192, 384), lambda k, *s: (0, late(k), 0, 0))
    fixed = pl.BlockSpec((rows, D), lambda k, *s: (0, 0))
    return pl.pallas_call(
        forward_kernel,
        grid_spec=pltpu.PrefetchScalarGridSpec(
            num_scalar_prefetch=2,
            grid=(windows + FF // D,),
            in_specs=[
                pl.BlockSpec((1, TOKW, D), lambda k, s, c: (s[now(k), 0], 0, 0)),
                whole(prev), whole(nxt), whole(w_qkv), whole(w_proj), whole(vec), whole(tab), whole(cot),
                pl.BlockSpec((D, D), lambda k, *s: (0, late(k))),
            ],
            out_specs=[
                one(TP, D), one(TP, D), one(TP, 3 * D), one(HEADS, TP, TP), one(TP, D), one(TP, D), fixed,
                flat, flat, half, half, fixed, pl.BlockSpec((1, D), lambda k, *s: (0, 0)),
            ],
            scratch_shapes=[pltpu.VMEM((D, rows), bf16)],
        ),
        out_shape=[
            shape(TP, D), shape(TP, D), shape(TP, 3 * D), shape(HEADS, TP, TP), shape(TP, D),
            shape(TP, D, dtype=f32), sds(rows, D),
            sds(rows, FF), sds(rows, FF), sds(2, 8, 192, 384), sds(2, 8, 192, 384), sds(rows, D),
            sds(1, D, dtype=f32),
        ],
        name="forward",
        **params(),
    )(info, core, x_slots, prev, nxt, w_qkv, w_proj, vec, tab, cot, w_fc1)


def down_kernel(info, core, dz_ref, slope_ref, n2_ref, w2_ref, *refs, last):
    if last:
        vec_ref, h_hbm, wproj_hbm, w1_hbm, before_hbm = refs[:5]
        keep_ref, send_ref, b1_ref, dh_ref, da_ref, do_ref, sums_ref = refs[8:15]
        n2_t, du_all, acc, w1_ref, h_ref, wproj_ref, sems = refs[15:]
        begin = before_hbm.shape[1]
        pairs = (
            (before_hbm, du_all.at[:, pl.ds(0, begin)]), (w1_hbm, w1_ref), (h_hbm, h_ref),
            (wproj_hbm, wproj_ref),
        )
        copies = [pltpu.make_async_copy(src, dst, sems.at[k]) for k, (src, dst) in enumerate(pairs)]
    else:
        keep_ref, send_ref, b1_ref, du_ref, n2_t = refs
    step = pl.program_id(0)

    @pl.when(step == 0)
    def _():
        if last:
            for copy in copies:
                copy.start()
        n2_t[...] = n2_ref[...].T

    du = (dot_nt(dz_ref[...], w2_ref[...]) * slope_ref[...].astype(f32)).astype(bf16)
    b1_ref[...] = jnp.sum(du.astype(f32), axis=0, keepdims=True)
    mine = (step & 1) == core[0]
    grad = dot(n2_t[...], du).astype(bf16)

    @pl.when(mine)
    def _():
        keep_ref[0] = grad

    @pl.when(jnp.logical_not(mine))
    def _():
        send_ref[0] = grad

    if not last:
        du_ref[...] = du
        return
    width = du.shape[1]
    du_all[:, pl.ds(pl.multiple_of(begin + step * width, 128), width)] = du

    @pl.when(step == pl.num_programs(0) - 1)
    def _():
        for copy in copies:
            copy.wait()
        vec = vec_ref[...]
        gain = jnp.zeros((1, D), f32)
        shift = jnp.zeros((1, D), f32)
        bias = jnp.zeros((1, D), f32)
        acc[...] = dot_nt(du_all[...], w1_ref[...])
        for k, mask in enumerate(masks(info, dz_ref.shape[0] // TP)):
            at = slice(TP * k, TP * k + TP)
            dn = acc[at] * mask
            normed, scale_inv = norm_parts(h_ref[at])
            gain += jnp.sum(dn * normed, axis=0, keepdims=True)
            shift += jnp.sum(dn, axis=0, keepdims=True)
            dh = mask * (dz_ref[at].astype(f32) + norm_back(dn * vec[1:2], normed, scale_inv))
            dh_ref[at] = dh
            da = dh.astype(bf16)
            da_ref[at] = da
            bias += jnp.sum(da.astype(f32), axis=0, keepdims=True)
        do_ref[...] = dot_nt(da_ref[...], wproj_ref[...]).astype(bf16)
        sums_ref[0:1] = gain
        sums_ref[1:2] = shift
        sums_ref[2:3] = bias
        sums_ref[3:8] = jnp.zeros((5, D), f32)


def feed_down(info, core, dz, slope, n2, w_fc2, begin, steps, more=()):
    rows = n2.shape[0]
    step = D
    last = bool(more)
    hbm = pl.BlockSpec(memory_space=pl.ANY)
    inputs = [dz, slope, n2, w_fc2, *more]
    in_specs = [
        whole(dz),
        pl.BlockSpec((rows, step), lambda k, *s: (0, k + begin)),
        whole(n2),
        pl.BlockSpec((step, D), lambda k, *s: (k + begin, 0)),
    ]
    half = pl.BlockSpec((1, D, step), lambda k, *s: ((k + begin) // 2, 0, 0))
    out_specs = [half, half, pl.BlockSpec((1, step), lambda k, *s: (0, k + begin))]
    out_shape = [sds(2, D, D), sds(2, D, D), sds(1, FF, dtype=f32)]
    scratch = [pltpu.VMEM((D, rows), bf16)]
    aliases = {}
    if last:
        flat = pl.BlockSpec((rows, D), lambda k, *s: (0, 0))
        in_specs += [whole(more[0])] + [hbm] * 7
        aliases = {11: 0, 12: 1, 13: 2}
        out_specs += [flat] * 3 + [pl.BlockSpec((8, D), lambda k, *s: (0, 0))]
        out_shape += [sds(rows, D, dtype=f32), sds(rows, D), sds(rows, D), sds(8, D, dtype=f32)]
        scratch += [
            pltpu.VMEM((rows, FF), bf16), pltpu.VMEM((rows, D), f32), pltpu.VMEM((D, FF), bf16),
            pltpu.VMEM((rows, D), f32), pltpu.VMEM((D, D), bf16), pltpu.SemaphoreType.DMA((4,)),
        ]
    else:
        out_specs += [pl.BlockSpec((rows, step), lambda k, *s: (0, k))]
        out_shape += [sds(rows, step * steps)]
    return pl.pallas_call(
        functools.partial(down_kernel, last=last),
        grid_spec=pltpu.PrefetchScalarGridSpec(
            num_scalar_prefetch=2, grid=(steps,), in_specs=in_specs, out_specs=out_specs,
            scratch_shapes=scratch,
        ),
        out_shape=out_shape,
        input_output_aliases=aliases,
        name="feed_down",
        **params(),
    )(info, core, *inputs)


def out_kernel(info, gl_ref, w2_ref, h_ref, vec_ref, out_ref, acc):
    step = pl.program_id(0)

    @pl.when(step == 0)
    def _():
        acc[...] = h_ref[...]

    acc[...] += dot(gl_ref[...], w2_ref[...])

    @pl.when(step == pl.num_programs(0) - 1)
    def _():
        for k, mask in enumerate(masks(info, out_ref.shape[0])):
            at = slice(TP * k, TP * k + TP)
            y = (mask * (acc[at] + vec_ref[7:8])).astype(bf16)
            out_ref[k] = dot(gather_rows(), y).astype(bf16)


def feed_out(info, gl, w_fc2, h, vec):
    rows = gl.shape[0]
    windows = rows // TP
    step = D
    return pl.pallas_call(
        out_kernel,
        grid_spec=pltpu.PrefetchScalarGridSpec(
            num_scalar_prefetch=1,
            grid=(FF // step,),
            in_specs=[
                pl.BlockSpec((rows, step), lambda k, s: (0, k)),
                pl.BlockSpec((step, D), lambda k, s: (k, 0)),
                whole(h), whole(vec),
            ],
            out_specs=pl.BlockSpec((windows, TOKW, D), lambda k, s: (0, 0, 0)),
            scratch_shapes=[pltpu.VMEM((rows, D), f32)],
        ),
        out_shape=sds(windows, TOKW, D),
        name="feed_out",
        **params(),
    )(info, gl, w_fc2, h, vec)


def key_rows():
    lane, col = iota((64, TP), 0), iota((64, TP), 1)
    i, j = col >> 4, col & 15
    hit = ((lane < WS) & (lane == i)) | ((lane >= 32) & (lane < 32 + WS) & (lane - 32 == 13 - j))
    return hit.astype(f32).astype(bf16)


def grad_rolls(table, base):
    lane = iota((16, 128), 1)
    out = []
    for i in range(WS):
        tile = table[16 * i : 16 * i + 16]
        by_row = jnp.where((lane >= base) & (lane < base + WS), tile, 0.0)
        by_row = pltpu.roll(by_row, 13 - i, 1) if i < 13 else by_row
        by_col = jnp.where((lane >= base + 32) & (lane < base + 32 + WS), tile, 0.0)
        out.append(by_row + pltpu.roll(by_col, 0, 1, stride=1, stride_axis=0))
    return jnp.concatenate(out, axis=0)


def back_kernel(qkv_ref, pt_ref, do_ref, tab_ref, *refs):
    dqkv_ref, table_ref, sums_ref = refs[-3:]

    @pl.when(pl.program_id(0) == 0)
    def _():
        table_ref[...] = jnp.zeros_like(table_ref)
        sums_ref[...] = jnp.zeros_like(sums_ref)

    rows_extra = key_rows()
    lane = iota((TP, 128), 1)
    for pair in range(HEADS // 2):
        at = 128 * pair
        q = qkv_ref[0, :, at : at + 128]
        key_t = (qkv_ref[0, :, D + at : D + at + 128] * jnp.asarray(0.125, bf16)).T
        v = qkv_ref[0, :, 2 * D + at : 2 * D + at + 128]
        do = do_ref[0, :, at : at + 128]
        ds_all, dq_all, z_all = [], [], []
        for head in range(2):
            p_t = pt_ref[0, 2 * pair + head].astype(f32)
            dp_t = dot_nt(v, do * lane_mask(head))
            mean = jnp.sum(p_t * dp_t, axis=0, keepdims=True) / jnp.sum(p_t, axis=0, keepdims=True)
            ds_t = (p_t * (dp_t - mean)).astype(bf16)
            ds_all.append(ds_t)
            if head == 0:
                left = jnp.concatenate([key_t[:HD], rows_extra], axis=0)
            else:
                left = jnp.concatenate([rows_extra, key_t[HD:]], axis=0)
            back = dot(left, ds_t).T
            dq_all.append(back)
            z_all.append(grad_rolls(back, 64 if head == 0 else 0))
        z = jnp.where(lane < HD, z_all[1], z_all[0]).astype(bf16)
        dq = jnp.where(lane < HD, dq_all[0], dq_all[1]) + dot(z, tab_ref[...])
        table_ref[...] += dot(z.T, q)
        two = lambda a: jnp.concatenate([a * lane_mask(0), a * lane_mask(1)], axis=0)
        dk = dot(jnp.concatenate(ds_all, axis=1), two(q)) * 0.125
        p_two = jnp.concatenate([pt_ref[0, 2 * pair], pt_ref[0, 2 * pair + 1]], axis=1)
        dv = dot(p_two, two(do))
        dqkv_ref[0, :, at : at + 128] = dq.astype(bf16)
        dqkv_ref[0, :, D + at : D + at + 128] = dk.astype(bf16)
        dqkv_ref[0, :, 2 * D + at : 2 * D + at + 128] = dv.astype(bf16)
    sums_ref[...] += jnp.sum(dqkv_ref[0].astype(f32), axis=0, keepdims=True)


def backward_attention(qkv, p_t, do, tab, begin, count, into=None):
    windows = qkv.shape[0]
    one = lambda *tail: pl.BlockSpec((1,) + tail, lambda k: (k + begin,) + (0,) * len(tail))
    inputs = [qkv, p_t, do, tab]
    in_specs = [one(TP, 3 * D), one(HEADS, TP, TP), one(TP, D), whole(tab)]
    if into is not None:
        inputs.append(into)
        in_specs.append(pl.BlockSpec(memory_space=pl.ANY))
    return pl.pallas_call(
        back_kernel,
        grid=(count,),
        in_specs=in_specs,
        out_specs=[
            one(TP, 3 * D),
            pl.BlockSpec((128, 128), lambda k: (0, 0)),
            pl.BlockSpec((1, 3 * D), lambda k: (0, 0)),
        ],
        out_shape=[sds(windows, TP, 3 * D), sds(128, 128, dtype=f32), sds(1, 3 * D, dtype=f32)],
        input_output_aliases={} if into is None else {4: 0},
        name="attention_backward",
        **params(),
    )(*inputs)


def weight_kernel(
    core, n1_ref, dqkv_ref, o_ref, da_ref, keep_ref, send_ref, n1_t, o_t
):
    @pl.when(pl.program_id(0) == 0)
    def _():
        n1_t[...] = n1_ref[...].T
        o_t[...] = o_ref[...].T

    part = dot(n1_t[...], dqkv_ref[...])
    proj = dot(o_t[...], da_ref[...])
    lane = iota((D, 128), 1) < 64
    even = core[0] == 0

    def put(at, first, second):
        first, second = first.astype(bf16), second.astype(bf16)
        keep_ref[0, :, at] = jnp.where(even, first, second)
        send_ref[0, :, at] = jnp.where(even, second, first)

    moved = pltpu.roll(proj[:, 0:256], 64, 1)
    rolled = pltpu.roll(part[:, 512:1152], 576, 1)
    put(slice(0, 512), part[:, 0:512], rolled[:, 0:512])
    put(
        slice(512, 640),
        jnp.where(lane, part[:, 512:640], moved[:, 0:128]),
        jnp.where(lane, rolled[:, 512:640], proj[:, 128:256]),
    )
    put(slice(640, 768), moved[:, 128:256], proj[:, 256:384])


def attention_weights(core, n1, dqkv, o, da):
    rows = n1.shape[0]
    wide = 3 * D // 2
    half = pl.BlockSpec((1, D, D), lambda k, *s: (k, 0, 0))
    return pl.pallas_call(
        weight_kernel,
        grid_spec=pltpu.PrefetchScalarGridSpec(
            num_scalar_prefetch=1,
            grid=(2,),
            in_specs=[
                whole(n1),
                pl.BlockSpec((rows, wide), lambda k, *s: (0, k)),
                whole(o),
                pl.BlockSpec((rows, D // 2), lambda k, *s: (0, k)),
            ],
            out_specs=[half] * 2,
            scratch_shapes=[pltpu.VMEM((D, rows), bf16), pltpu.VMEM((D, rows), bf16)],
        ),
        out_shape=[sds(2, D, D)] * 2,
        name="attention_weights",
        **params(),
    )(core, n1, dqkv, o, da)


def input_kernel(info, dqkv_ref, wqkv_ref, xpad_ref, dh_ref, vec_ref, dx_ref, sums_ref):
    vec = vec_ref[...]
    acc = dot_nt(dqkv_ref[...], wqkv_ref[...])
    k = pl.program_id(0)
    mask = inside(info[k, 2], info[k, 3])
    dn = acc * mask
    normed, scale_inv = norm_parts(xpad_ref[...].astype(f32))
    dx = dh_ref[...] + norm_back(dn * vec[0:1], normed, scale_inv)
    dx_ref[0] = dot(gather_rows(), dx.astype(bf16)).astype(bf16)

    @pl.when(k == 0)
    def _():
        sums_ref[...] = jnp.zeros_like(sums_ref)

    sums_ref[0:1] += jnp.sum(dn * normed, axis=0, keepdims=True)
    sums_ref[1:2] += jnp.sum(dn, axis=0, keepdims=True)


def input_gradient(info, dqkv, w_qkv, xpad, dh, vec):
    rows = xpad.shape[0]
    windows = rows // TP
    return pl.pallas_call(
        input_kernel,
        grid_spec=pltpu.PrefetchScalarGridSpec(
            num_scalar_prefetch=1,
            grid=(windows,),
            in_specs=[
                pl.BlockSpec((TP, 3 * D), lambda k, s: (k, 0)),
                whole(w_qkv),
                pl.BlockSpec((TP, D), lambda k, s: (k, 0)),
                pl.BlockSpec((TP, D), lambda k, s: (k, 0)),
                whole(vec),
            ],
            out_specs=[
                pl.BlockSpec((1, TOKW, D), lambda k, s: (k, 0, 0)),
                pl.BlockSpec((8, D), lambda k, s: (0, 0)),
            ],
        ),
        out_shape=[sds(windows, TOKW, D), sds(8, D, dtype=f32)],
        name="input_gradient",
        **params(),
    )(info, dqkv, w_qkv, xpad, dh, vec)


first_fix = 1.0 - 0.5**STEP
second_fix = float(np.float32(1.0) - np.power(np.float32(0.999), np.float32(STEP)))


def adam_step(parameter, gradient, moment, square):
    moment_next = 0.5 * moment + 0.5 * gradient
    square_next = 0.999 * square + 0.001 * gradient * gradient
    fresh_weight = parameter - learn_rate * (moment_next / first_fix) / (
        jnp.sqrt(square_next / second_fix) + 1e-08
    )
    return moment_next, square_next, fresh_weight.astype(bf16)


def adam_kernel(kept_ref, came_ref, own_ref, *refs):
    parts = (len(refs) - 1) // 5
    moments, squares, grads, moments_next, squares_next = (
        refs[parts * k : parts * k + parts] for k in range(5)
    )
    total = kept_ref[...].astype(f32) + came_ref[...].astype(f32)
    own = own_ref[...].astype(f32)
    begin, fresh = 0, []
    for k in range(parts):
        at = slice(begin, begin + moments[k].shape[1])
        grads[k][...] = total[:, at]
        moment, square, weight = adam_step(own[:, at], total[:, at], moments[k][...], squares[k][...])
        moments_next[k][...] = moment
        squares_next[k][...] = square
        fresh.append(weight.astype(f32))
        begin = at.stop
    fresh = fresh[0] if parts == 1 else jnp.concatenate(fresh, axis=1)
    refs[-1][...] = fresh.astype(bf16)


def adam(kept, came, own, moments, squares):
    shapes = [sds(*m.shape, dtype=f32) for m in moments]
    out = pl.pallas_call(
        adam_kernel,
        out_shape=shapes * 3 + [sds(*kept.shape)],
        name="adam",
        **params(),
    )(kept, came, own, *moments, *squares)
    parts = len(moments)
    return [out[parts * k : parts * k + parts] for k in range(3)], out[-1]


def own_kernel(at, qkv_hbm, proj_hbm, fc1_hbm, fc2_hbm, attn_ref, fc1_ref, fc2_ref, qkv, proj, fc1, fc2, sems):
    win, grp = at[0], at[1]
    odd = (grp & 1) == 1

    def columns(width, more):
        return pl.ds(pl.multiple_of(width * grp - 64 * (grp & 1), 128), more)

    rows = fc1_ref.shape[0]
    some = pl.ds(pl.multiple_of(win * rows, 16), rows)
    many = pl.ds(pl.multiple_of(win * fc2.shape[0], 16), fc2.shape[0])
    copies = [
        pltpu.make_async_copy(qkv_hbm.at[some, columns(3 * D // 4, 640)], qkv, sems.at[0]),
        pltpu.make_async_copy(proj_hbm.at[some, columns(D // 4, 256)], proj, sems.at[1]),
        pltpu.make_async_copy(fc1_hbm.at[some, pl.ds(pl.multiple_of(D * grp, 128), D)], fc1, sems.at[2]),
        pltpu.make_async_copy(fc2_hbm.at[many, columns(D // 4, 256)], fc2, sems.at[3]),
    ]
    for copy in copies:
        copy.start()
    for copy in copies:
        copy.wait()

    def aligned(ref):
        whole = ref[...].astype(f32)
        return jnp.where(odd, pltpu.roll(whole, whole.shape[1] - 64, 1), whole)

    left, right = aligned(qkv), aligned(proj)
    attn_ref[:, 0:512] = left[:, 0:512].astype(bf16)
    right = pltpu.roll(right, 64, 1)
    lane = iota((rows, 128), 1) < 64
    attn_ref[:, 512:640] = jnp.where(lane, left[:, 512:640], right[:, 0:128]).astype(bf16)
    attn_ref[:, 640:768] = right[:, 128:256].astype(bf16)
    fc1_ref[...] = fc1[...]
    fc2_ref[...] = aligned(fc2).T[0 : D // 4].astype(bf16)


def own_blocks(win, grp, wins, grps, w_qkv, w_proj, w_fc1, w_fc2):
    rows, many = D // wins, FF // wins
    if grps != 4 or rows % 16 or many % 128:
        cut = lambda w, r, c: lax.dynamic_slice(w, (win * r, grp * c), (r, c))
        attn = [cut(w_qkv, rows, 3 * D // grps), cut(w_proj, rows, D // grps)]
        return jnp.concatenate(attn, axis=1), cut(w_fc1, rows, FF // grps), cut(w_fc2, many, D // grps).T
    hbm = pl.BlockSpec(memory_space=pl.ANY)
    vmem = pl.BlockSpec(memory_space=pltpu.VMEM)
    return pl.pallas_call(
        own_kernel,
        in_specs=[pl.BlockSpec(memory_space=pltpu.SMEM)] + [hbm] * 4,
        out_specs=[vmem] * 3,
        out_shape=[sds(rows, D), sds(rows, D), sds(D // 4, many)],
        scratch_shapes=[
            pltpu.VMEM((rows, 640), bf16), pltpu.VMEM((rows, 256), bf16), pltpu.VMEM((rows, D), bf16),
            pltpu.VMEM((many, 256), bf16), pltpu.SemaphoreType.DMA((4,)),
        ],
        name="own_blocks",
        **params(),
    )(jnp.stack([win, grp]).astype(jnp.int32), w_qkv, w_proj, w_fc1, w_fc2)


def place_kernel(at, have_ref, came_ref, *refs, way):
    half = have_ref.shape[0]
    rows, columns = have_ref.shape[1:]
    for target in range(2 * half):
        place = at[target]
        near = have_ref[jnp.minimum(place, half - 1)]
        far = came_ref[jnp.maximum(place - half, 0)]
        block = jnp.where(place < half, near, far)
        if way == "lanes":
            refs[0][:, columns * target : columns * target + columns] = block
        else:
            refs[-1 if way == "turned" else 0][rows * target : rows * target + rows] = block
    if way == "turned":
        whole = refs[-1][...].T
        begin = 0
        for out in refs[:-1]:
            out[...] = whole[begin : begin + out.shape[0]]
            begin += out.shape[0]


def put_in_place(at, have, came, way, widths=()):
    count, rows, columns = 2 * have.shape[0], have.shape[1], have.shape[2]
    smem = pl.BlockSpec(memory_space=pltpu.SMEM)
    vmem = pl.BlockSpec(memory_space=pltpu.VMEM)
    scratch = []
    if way == "lanes":
        shapes = [sds(rows, count * columns)]
    elif way == "rows":
        shapes = [sds(count * rows, columns)]
    else:
        shapes = [sds(width, count * rows) for width in widths]
        scratch = [pltpu.VMEM((count * rows, columns), bf16)]
    return pl.pallas_call(
        functools.partial(place_kernel, way=way),
        in_specs=[smem, vmem, vmem],
        out_specs=[vmem] * len(shapes),
        out_shape=shapes,
        scratch_shapes=scratch,
        name="put_in_place",
        **params(),
    )(at, have, came)


def slots_kernel(at, dx_hbm, prev_hbm, next_hbm, out_hbm, held, sems):
    count = dx_hbm.shape[0]
    loads = [
        pltpu.make_async_copy(ref, held.at[pl.ds(begin, ref.shape[0])], sems.at[k])
        for k, (begin, ref) in enumerate(((0, dx_hbm), (count, prev_hbm), (count + 1, next_hbm)))
    ]
    for load in loads:
        load.start()
    held[count + 2] = jnp.zeros(held.shape[1:], bf16)
    for load in loads:
        load.wait()
    stores = [
        pltpu.make_async_copy(held.at[at[slot]], out_hbm.at[slot], sems.at[3 + slot])
        for slot in range(out_hbm.shape[0])
    ]
    for store in stores:
        store.start()
    for store in stores:
        store.wait()


def to_slots(at, dx, prev, nxt):
    slots, count = at.shape[0], dx.shape[0]
    hbm = pl.BlockSpec(memory_space=pl.ANY)
    return pl.pallas_call(
        slots_kernel,
        in_specs=[pl.BlockSpec(memory_space=pltpu.SMEM), hbm, hbm, hbm],
        out_specs=hbm,
        out_shape=sds(slots, TOKW, D),
        scratch_shapes=[
            pltpu.VMEM((count + 3, TOKW, D), bf16), pltpu.SemaphoreType.DMA((3 + slots,)),
        ],
        name="to_slots",
        **params(),
    )(at, dx, prev, nxt)


AXES = ("win", "grp")


def bits_of(size):
    return [1 << k for k in range(size.bit_length() - 1)]


def flipped(axis, bit):
    wins, grps = lax.axis_size("win"), lax.axis_size("grp")
    out = []
    for d in range(wins * grps):
        w, g = divmod(d, grps)
        w, g = (w ^ bit, g) if axis == "win" else (w, g ^ bit)
        out.append((d, w * grps + g))
    return out


def windows_before(count, windows):
    total, before = count, jnp.zeros_like(count)
    bits = [(axis, bit) for axis in ("grp", "win") for bit in bits_of(lax.axis_size(axis))]
    for axis, bit in bits:
        last = (axis, bit) == bits[-1]
        other = windows - total if last else lax.ppermute(total, AXES, flipped(axis, bit))
        mine = (lax.axis_index(axis) & bit) != 0
        before = before + jnp.where(mine, other, 0)
        total = total + other
    return before


def neighbours(last, first):
    count = lax.axis_size("win") * lax.axis_size("grp")
    up = [(i, i + 1) for i in range(count - 1)]
    down = [(j, i) for i, j in up]
    return lax.ppermute(last, AXES, up), lax.ppermute(first, AXES, down)


def rising():
    return [(axis, bit) for axis in ("grp", "win") for bit in bits_of(lax.axis_size(axis))]


def tie(value, *others):
    return lax.optimization_barrier((value, *others))[0]


def places(order):
    apart = lax.axis_index("win") ^ jnp.arange(lax.axis_size("win"), dtype=jnp.int32)
    return sum(((apart & bit) != 0).astype(jnp.int32) << k for k, (_, bit) in enumerate(order))


class Piece:
    def __init__(self, kept, came, parts):
        self.kept, self.came, self.parts = kept, came, parts

    def halve(self, which, at=None, rider=None):
        axis, bit = which
        place = self.parts.index(which)
        parts = self.parts[:place] + self.parts[place + 1 :]
        mine = ((lax.axis_index(axis) & bit) != 0).astype(jnp.int32)
        split = (1 << place, 2, -1) + self.kept.shape[-2:]
        kept, came = self.kept.reshape(split), self.came.reshape(split)

        def pick(half):
            piece = lax.dynamic_index_in_dim(kept, half, 1, keepdims=False)
            other = lax.dynamic_index_in_dim(came, half, 1, keepdims=False)
            if at is not None:
                piece, other = piece[..., at[0], at[1]], other[..., at[0], at[1]]
            return (piece.astype(f32) + other.astype(f32)).astype(bf16)

        send, kept = pick(1 - mine), pick(mine)
        if rider is None:
            return send, Piece(kept, lax.ppermute(send, AXES, flipped(axis, bit)), parts)
        shape, columns = send.shape, send.shape[-1]
        send = jnp.concatenate([send.reshape(-1, columns), rider.rows(columns)], axis=0)
        came = lax.ppermute(send, AXES, flipped(axis, bit))
        rows = kept.size // columns
        rider.add(came[rows:])
        return send, Piece(kept, came[:rows].reshape(shape), parts)


class Chunk:
    def __init__(self, keep, send, axis):
        near, *self.grp = [one for one in rising() if one[0] == "grp"]
        self.win = [one for one in rising() if one[0] == "win"]
        parts = list(reversed(self.grp)) + list(reversed(self.win))
        self.pieces = [Piece(keep, lax.ppermute(send, AXES, flipped(*near)), parts)]
        self.block, self.axis, self.finish = keep.shape[-2:], axis, None
        self.cross = [(self.grp[-1], self.win[0]), (self.win[0], self.grp[-1])]
        self.order = self.grp[:-1] + self.win[1:]
        self.ways, self.back = list(reversed(self.win)), list(reversed(self.win))
        self.have, self.rider = None, None

    def left(self):
        return bool(self.cross or self.order or self.ways)

    def after(self, *others):
        if others:
            for piece in self.pieces:
                piece.came = tie(piece.came, *others)

    def step(self, *others):
        self.after(*others)
        if self.cross:
            whole, half = slice(None), self.block[self.axis] // 2
            cuts = [slice(0, half), slice(half, None)]
            ats = [(c, whole) if self.axis == 0 else (whole, c) for c in cuts]
            first, second = self.cross.pop(0)
            if len(self.pieces) == 1:
                (one,) = self.pieces
                made = [one.halve(first, ats[0]), one.halve(second, ats[1])]
            else:
                made = [self.pieces[0].halve(first, rider=self.rider), self.pieces[1].halve(second)]
            self.pieces = [piece for _, piece in made]
            return tuple(send for send, _ in made)
        if len(self.pieces) == 2:
            joined = lambda a, b: jnp.concatenate([a, b], axis=self.axis - 2)
            one, two = self.pieces
            shape = lambda a: a.reshape((-1,) + a.shape[-2:])
            self.pieces = [
                Piece(
                    joined(shape(one.kept), shape(two.kept)),
                    joined(shape(one.came), shape(two.came)),
                    one.parts,
                )
            ]
        (piece,) = self.pieces
        if self.order:
            send, piece = piece.halve(self.order.pop(0), rider=self.rider)
            self.pieces = [piece]
            return send
        if self.have is None:
            self.result, fresh = self.finish(piece.kept.reshape(self.block), piece.came.reshape(self.block))
            self.have = fresh[None]
        else:
            self.have = jnp.concatenate([self.have, piece.came], axis=0)
        piece.came = lax.ppermute(self.have, AXES, flipped(*self.ways.pop(0)))
        return self.have

    def all(self, way, widths=()):
        have, came = self.have, self.pieces[0].came
        if self.block[0] % 16 == 0 and self.block[1] % 128 == 0:
            return put_in_place(places(self.back), have, came, way, widths)
        blocks = jnp.concatenate([have, came], axis=0)[places(self.back)]
        if way == "lanes":
            return [blocks.transpose(1, 0, 2).reshape(blocks.shape[1], -1)]
        blocks = blocks.reshape(-1, blocks.shape[2])
        return [blocks] if way == "rows" else jnp.split(blocks.T, np.cumsum(widths)[:-1], axis=0)


class Total:
    def __init__(self, vector):
        self.vector = vector
        self.order = [one for one in rising() if one[0] == "grp"]

    def rows(self, columns):
        flat = jnp.pad(self.vector, (0, -self.vector.shape[0] % columns))
        return flat.reshape(-1, columns).astype(bf16)

    def add(self, rows):
        self.vector = self.vector + rows.reshape(-1)[: self.vector.shape[0]].astype(f32)

    def left(self):
        return bool(self.order)

    def step(self, *after):
        mine = tie(self.vector, *after)
        self.vector = mine + lax.ppermute(mine, AXES, flipped(*self.order.pop(0)))
        return mine


def per_device(
    x_slots, counts, cotangent, w_qkv, w_proj, w_fc1, w_fc2, small_params,
    moment_qkv, moment_proj, moment_fc1, moment_fc2, moment_small,
    square_qkv, square_proj, square_fc1, square_fc2, square_small,
):
    slots, per_even = x_slots.shape[0], cotangent.shape[0]
    win_at, grp_at = lax.axis_index("win"), lax.axis_index("grp")
    wins, grps = lax.axis_size("win"), lax.axis_size("grp")
    base = (win_at * grps + grp_at) * per_even
    count = counts[0]
    prev, nxt = neighbours(lax.dynamic_slice_in_dim(x_slots, count - 1, 1, 0), x_slots[:1])
    offset = windows_before(counts, per_even * wins * grps)[0]
    window = base + jnp.arange(per_even, dtype=jnp.int32)
    slot = window - offset
    spot = window % (GRID * GRID)
    info = jnp.stack(
        [
            jnp.clip(slot, 0, slots - 1),
            jnp.where(slot < 0, 1, jnp.where(slot >= count, 2, 0)),
            SIDE - WS * (spot // GRID),
            SIDE - WS * (spot % GRID),
        ],
        axis=1,
    ).astype(jnp.int32)
    vec, tab_fwd = vectors(small_params), forward_tables(small_params)
    blocks = lambda grad: grad.reshape(grps // 2, wins, D // wins, grad.shape[2])
    core = (grp_at & 1).astype(jnp.int32).reshape(1)
    flat = lambda a: a.reshape(per_even * TP, a.shape[2])
    xpad, n1, qkv, p_t, o, h, n2, gl, slope, keep, send, dz, sum_b2 = forward(
        info, core, x_slots, prev, nxt, cotangent, w_qkv, w_proj, w_fc1, vec, tab_fwd
    )
    tab_bwd = backward_tables(tie(small_params, n2))
    h, n1, o, xpad = flat(h), flat(n1), flat(o), flat(xpad)
    if wins != keep.shape[1]:
        again = lambda a: a.transpose(0, 2, 1, 3).reshape(grps // 2, D // grps, wins, FF // wins).transpose(0, 2, 1, 3)
        keep, send = again(keep), again(send)
    fc2 = Chunk(keep, send, 0)
    fc2.finish = lambda kept, came: adam(kept, came, own_fc2, [moment_fc2.T], [square_fc2.T])
    *half, du = feed_down(info, core, dz, slope, n2, w_fc2, 0, 2)
    sent = fc2.step(du)
    keep, send, sum_b1, dh, da, do, sums_two = feed_down(
        info, core, tie(dz, *sent), slope, n2, w_fc2, 2, 2, (vec, h, w_proj, w_fc1, du, *half)
    )
    do = do.reshape(per_even, TP, D)
    sent = fc2.step(do)
    fc1 = Chunk(blocks(tie(keep, *sent)), blocks(tie(send, *sent)), 1)
    fc1.finish = lambda kept, came: adam(kept, came, own_fc1, [moment_fc1], [square_fc1])
    dqkv, table, sum_qkv = backward_attention(qkv, p_t, tie(do, send, *sent), tab_bwd, 0, 1)
    sent = fc1.step(table)
    sent = (*sent, fc2.step(*sent))
    dqkv, table_two, sum_two = backward_attention(
        qkv, p_t, tie(do, *sent), tab_bwd, 1, per_even - 1, dqkv
    )
    table, sum_qkv = table + table_two, sum_qkv + sum_two
    sent = fc1.step(table_two)
    sent = (*sent, fc2.step(*sent))
    dqkv = flat(dqkv)
    keep, send = attention_weights(core, n1, tie(dqkv, *sent), o, da)
    fc1.after(keep)
    fc2.after(keep)
    send = tie(send, *(piece.came for piece in fc1.pieces + fc2.pieces))
    attn = Chunk(blocks(keep), blocks(send), 1)
    attn.finish = lambda kept, came: adam(
        kept, came, own_attn, [moment_qkv, moment_proj], [square_qkv, square_proj]
    )
    sent = fc1.step(send)
    win_later = tie(win_at, sent)
    own_attn, own_fc1, own_fc2 = own_blocks(win_later, grp_at, wins, grps, w_qkv, w_proj, w_fc1, w_fc2)
    sent = fc2.step(own_fc2)
    sent = attn.step(sent)
    dx, sums_one = input_gradient(info, tie(dqkv, *sent), w_qkv, xpad, dh, vec)
    sums = (table, sum_qkv, sums_one, sums_two, sum_b1, sum_b2)
    sums, offset = tie((sums, offset), sums_one)
    table, sum_qkv, sums_one, sums_two, sum_b1, sum_b2 = sums
    rel_h = (table[0:RELN, 64:] + table[64 : 64 + RELN, :64])[::-1]
    rel_w = table[32 : 32 + RELN, 64:] + table[96 : 96 + RELN, :64]
    small = Total(
        jnp.concatenate(
            [
                sums_one[0], sums_two[0], sums_one[1], sums_two[1], sum_qkv[0, :D], sum_qkv[0, 2 * D :],
                sums_two[2], sum_b2[0], sum_b1[0], rel_h.reshape(-1), rel_w.reshape(-1),
            ]
        )
    )
    place = offset + jnp.arange(slots, dtype=jnp.int32) - base
    back = jnp.where(place < 0, per_even, jnp.where(place >= per_even, per_even + 1, place))
    back = jnp.where(jnp.arange(slots) < count, back, per_even + 2).astype(jnp.int32)
    token = fc2.step(dx)
    token = fc1.step(token)
    attn.rider = small
    made, rounds = {}, 0

    def slots_gap(token):
        made["dx"] = to_slots(tie(back, token), dx, dx_prev, dx_next)
        return made["dx"]

    def place_gap(name, chunk, way):
        def gap(token):
            chunk.pieces[0].came = tie(chunk.pieces[0].came, token)
            made[name] = chunk.all(way)
            return made[name][0]

        return gap

    ends = [(fc2, place_gap("fc2", fc2, "lanes")), (fc1, place_gap("fc1", fc1, "rows"))]
    while attn.left() or fc2.left() or fc1.left() or small.left():
        done = [end for end in ends if not end[0].left()]
        for chunk in (attn, fc2, fc1, small):
            idle = chunk is fc1 and rounds in (1,) or chunk is small and attn.order
            if chunk.left() and not idle:
                token = chunk.step(token)
        for end in done[:1]:
            token = end[1](token)
            ends.remove(end)
        rounds += 1
    dx_prev, dx_next = neighbours(*tie((dx[per_even - 1 :], dx[:1]), token))
    made["out"] = token = feed_out(info, tie(gl, token), w_fc2, h, vec)
    for end in ends:
        token = end[1](token)
    attn.pieces[0].came = tie(attn.pieces[0].came, token)
    block_out = made["out"]
    made["attn"] = attn.all("turned", (3 * D // grps, D // grps))
    input_grad = slots_gap(made["attn"])
    part_d, next_m_fc2, next_v_fc2 = (one[0].T for one in fc2.result)
    (part_c,), (next_m_fc1,), (next_v_fc1,) = fc1.result
    (part_a, part_b), (next_m_qkv, next_m_proj), (next_v_qkv, next_v_proj) = attn.result
    new_fc2, new_fc1 = made["fc2"][0].T, made["fc1"][0]
    new_qkv, new_proj = (part.T for part in made["attn"])
    grad_small = small.vector
    upd_small = adam_step(small_params.astype(f32), grad_small, moment_small, square_small)
    return (
        block_out, input_grad, part_a, part_b, part_c, part_d, grad_small,
        next_m_qkv, next_m_proj, next_m_fc1, next_m_fc2, upd_small[0],
        next_v_qkv, next_v_proj, next_v_fc1, next_v_fc2, upd_small[1],
        new_qkv, new_proj, new_fc1, new_fc2, upd_small[2],
    )


def solution(mesh):
    data, shard, same, part = P(AXES, None, None), P("win", "grp"), P(), P(None, "grp")
    in_specs = (data, P(AXES), data) + (same,) * 5 + ((shard,) * 4 + (same,)) * 2
    out_specs = (data,) * 2 + ((shard,) * 4 + (same,)) * 3 + (part,) * 4 + (same,)
    return jax.shard_map(
        per_device, mesh=mesh, in_specs=in_specs, out_specs=out_specs, check_vma=False
    )
```

```python
import functools

import jax
import jax.numpy as jnp
import numpy as np
from jax import lax
from jax.experimental import pallas as pl
from jax.experimental.pallas import tpu as pltpu
from jax.sharding import PartitionSpec as P

D = 768
HEADS = 12
HD = 64
FF = 3072
WS = 14
SIDE = 64
STEP = 4
TOKW = 196
GRID = 5
RELN = 27
TP = 224

root_half = 0.7071067811865476
inv_root_two_pi = 0.3989422804014327
learn_rate = 0.06
bf16 = jnp.bfloat16
f32 = jnp.float32
VMEM_LIMIT = 56 << 20


def dot(a, b):
    return lax.dot_general(a, b, (((1,), (0,)), ((), ())), preferred_element_type=f32)


def dot_nt(a, b):
    return lax.dot_general(a, b, (((1,), (1,)), ((), ())), preferred_element_type=f32)


def dot_tn(a, b):
    return lax.dot_general(a, b, (((0,), (0,)), ((), ())), preferred_element_type=f32)


def iota(shape, axis):
    return lax.broadcasted_iota(jnp.int32, shape, axis)


def spread():
    row, token = iota((TP, TOKW), 0), iota((TP, TOKW), 1)
    hit = ((row & 15) < WS) & (token == WS * (row >> 4) + (row & 15))
    return hit.astype(f32).astype(bf16)


def gather_rows():
    token, row = iota((TOKW, TP), 0), iota((TOKW, TP), 1)
    hit = ((row & 15) < WS) & (token == WS * (row >> 4) + (row & 15))
    return hit.astype(f32).astype(bf16)


def key_lanes():
    row, lane = iota((TP, 128), 0), iota((TP, 128), 1)
    i, j = row >> 4, row & 15
    hit = (lane == i) | ((lane >= 64) & (lane < 64 + WS) & (lane - 64 == j))
    shut = (lane == 127) & (j >= WS)
    hit = hit.astype(f32)
    return hit.astype(bf16), jnp.where(shut, -1e30, hit).astype(bf16)


def inside(limit_row, limit_col):
    row = iota((TP, 1), 0)
    i, j = row >> 4, row & 15
    return ((i < limit_row) & (j < jnp.minimum(limit_col, WS))).astype(f32)


def norm_parts(v):
    centered = v - jnp.mean(v, axis=-1, keepdims=True)
    scale_inv = lax.rsqrt(jnp.mean(centered * centered, axis=-1, keepdims=True) + 1e-06)
    return centered * scale_inv, scale_inv


def norm_back(e, normed, scale_inv):
    return scale_inv * (
        e
        - jnp.mean(e, axis=-1, keepdims=True)
        - normed * jnp.mean(e * normed, axis=-1, keepdims=True)
    )


def lane_mask(head):
    lane = iota((1, 128), 1)
    return ((lane < HD) if head == 0 else (lane >= HD)).astype(f32).astype(bf16)


def query_lanes(table):
    lane = iota((16, 128), 1)
    out = []
    for i in range(WS):
        tile = table[16 * i : 16 * i + 16]
        by_row = pltpu.roll(tile, 51 + i, 1)
        by_col = pltpu.roll(tile, 51, 1, stride=1, stride_axis=0)
        out.append(jnp.where(lane < 64, by_row, by_col))
    aug = jnp.concatenate(out, axis=0)
    high = aug.astype(bf16)
    low = (aug - high.astype(f32)).astype(bf16)
    return high, jnp.where(iota((TP, 128), 1) == 127, jnp.asarray(1.0, bf16), low)


def vectors(small):
    return small[: 8 * D + FF].astype(f32).reshape(-1, D)


def forward_tables(small):
    tables = small[8 * D + FF :].reshape(2, RELN, HD)[:, ::-1]
    gap = jnp.zeros((64 - RELN, HD), bf16)
    one = jnp.concatenate([tables[1], gap, tables[0], gap], axis=0).T
    none = jnp.zeros_like(one)
    return jnp.block([[one, none], [none, one]])


def backward_tables(small):
    tables = small[8 * D + FF :].reshape(2, RELN, HD)
    gap = jnp.zeros((32 - RELN, HD), bf16)
    half = jnp.concatenate([tables[0, ::-1], gap, tables[1], gap], axis=0)
    nil = jnp.zeros_like(half)
    return jnp.block([[nil, half], [half, nil]])


def params(limit=VMEM_LIMIT, **more):
    return dict(
        compiler_params=pltpu.CompilerParams(vmem_limit_bytes=limit),
        cost_estimate=pl.CostEstimate(flops=0, bytes_accessed=0, transcendentals=0),
        **more,
    )


def whole(a):
    return pl.BlockSpec(a.shape, lambda k, *s: (0,) * a.ndim)


def sds(*dims, dtype=bf16):
    return jax.ShapeDtypeStruct(dims, dtype)


def masks(info, windows):
    return [inside(info[k, 2], info[k, 3]) for k in range(windows)]


def window_forward(
    k, info, xs_ref, prev_ref, next_ref, wqkv_ref, wproj_ref, vec_ref, tab_ref,
    xpad_ref, n1_ref, qkv_ref, pt_ref, o_ref, h_ref, n2_ref,
):
    source = info[k, 1]
    x = jnp.where(source == 0, xs_ref[0], jnp.where(source == 1, prev_ref[0], next_ref[0]))
    big = dot(spread(), x)
    xpad_ref[0] = big.astype(bf16)
    mask = inside(info[k, 2], info[k, 3])
    vec = vec_ref[...]
    normed, _ = norm_parts(big)
    n1 = (mask * (normed * vec[0:1] + vec[2:3])).astype(bf16)
    n1_ref[0] = n1
    for part, bias in enumerate((vec[4:5], 0.0, vec[5:6])):
        at = slice(D * part, D * part + D)
        qkv_ref[0, :, at] = (dot(n1, wqkv_ref[:, at]) + bias).astype(bf16)
    keys_open, keys_extra = key_lanes()
    for pair in range(HEADS // 2):
        at = 128 * pair
        q = qkv_ref[0, :, at : at + 128]
        key = jnp.concatenate([qkv_ref[0, :, D + at : D + at + 128], keys_open, keys_extra], axis=1)
        v_t = qkv_ref[0, :, 2 * D + at : 2 * D + at + 128].T
        tables = dot(q, tab_ref[...])
        sides = [query_lanes(tables[:, 128 * head : 128 * head + 128]) for head in range(2)]
        scores = [
            dot_nt(key, jnp.concatenate([q * (lane_mask(head) * 0.125), *sides[head]], axis=1))
            for head in range(2)
        ]
        peaks = [jnp.max(s, axis=0, keepdims=True) for s in scores]
        es = [jnp.exp(s - m) for s, m in zip(scores, peaks)]
        sums = [jnp.sum(e, axis=0, keepdims=True) for e in es]
        ps = [(e * (1.0 / l)).astype(bf16) for e, l in zip(es, sums)]
        outs = []
        for head in range(2):
            pt_ref[0, 2 * pair + head] = ps[head]
            outs.append(dot(v_t[HD * head : HD * head + HD], ps[head]))
        o_ref[0, :, at : at + 128] = jnp.concatenate(outs, axis=0).T.astype(bf16)
    a = dot(o_ref[0], wproj_ref[...]) + vec[6:7]
    h = mask * (big + a)
    h_ref[0] = h
    normed_two, _ = norm_parts(h)
    rows = pl.ds(pl.multiple_of(TP * k, 16), TP)
    n2_ref[rows, :] = (mask * (normed_two * vec[1:2] + vec[3:4])).astype(bf16)


def forward_kernel(
    info, core, xs_ref, prev_ref, next_ref, wqkv_ref, wproj_ref, vec_ref, tab_ref, cot_ref, w1_ref,
    xpad_ref, n1_ref, qkv_ref, pt_ref, o_ref, h_ref, n2_ref,
    gl_ref, slope_ref, keep_ref, send_ref, dz_ref, b2_ref, dz_t,
):
    windows = cot_ref.shape[0]
    step = pl.program_id(0)

    @pl.when(step < windows)
    def _():
        window_forward(
            step, info, xs_ref, prev_ref, next_ref, wqkv_ref, wproj_ref, vec_ref, tab_ref,
            xpad_ref, n1_ref, qkv_ref, pt_ref, o_ref, h_ref, n2_ref,
        )

    @pl.when(step == windows)
    def _():
        total = jnp.zeros((1, D), f32)
        for k, mask in enumerate(masks(info, windows)):
            part = dot(spread(), cot_ref[k]) * mask
            dz_ref[TP * k : TP * k + TP] = part.astype(bf16)
            total += jnp.sum(part, axis=0, keepdims=True)
        b2_ref[...] = total
        dz_t[...] = dz_ref[...].T

    @pl.when(step >= windows)
    def _():
        u = dot(n2_ref[...], w1_ref[...]) + vec_ref[pl.ds(8 + step - windows, 1), :]
        half = 0.5 * (1.0 + lax.erf(u * root_half))
        gl = (u * half).astype(bf16)
        gl_ref[...] = gl
        slope_ref[...] = (half + u * jnp.exp(-0.5 * u * u) * inv_root_two_pi).astype(bf16)
        grad = dot(dz_t[...], gl).astype(bf16)
        even = core[0] == 0
        rows, cols = keep_ref.shape[2:]
        for y in range(keep_ref.shape[0]):
            for w in range(keep_ref.shape[1]):
                at = slice(cols * w, cols * w + cols)
                first = grad[2 * rows * y : 2 * rows * y + rows, at]
                second = grad[2 * rows * y + rows : 2 * rows * y + 2 * rows, at]
                keep_ref[y, w] = jnp.where(even, first, second)
                send_ref[y, w] = jnp.where(even, second, first)


def forward(info, core, x_slots, prev, nxt, cot, w_qkv, w_proj, w_fc1, vec, tab):
    windows = info.shape[0]
    rows = windows * TP
    now = lambda k: jnp.minimum(k, windows - 1)
    late = lambda k: jnp.maximum(k - windows, 0)
    one = lambda *tail: pl.BlockSpec((1,) + tail, lambda k, *s: (now(k),) + (0,) * len(tail))
    shape = lambda *tail, dtype=bf16: sds(windows, *tail, dtype=dtype)
    flat = pl.BlockSpec((rows, D), lambda k, *s: (0, late(k)))
    half = pl.BlockSpec((2, 2, 192, 384), lambda k, *s: (0, late(k), 0, 0))
    fixed = pl.BlockSpec((rows, D), lambda k, *s: (0, 0))
    return pl.pallas_call(
        forward_kernel,
        grid_spec=pltpu.PrefetchScalarGridSpec(
            num_scalar_prefetch=2,
            grid=(windows + FF // D,),
            in_specs=[
                pl.BlockSpec((1, TOKW, D), lambda k, s, c: (s[now(k), 0], 0, 0)),
                whole(prev), whole(nxt), whole(w_qkv), whole(w_proj), whole(vec), whole(tab), whole(cot),
                pl.BlockSpec((D, D), lambda k, *s: (0, late(k))),
            ],
            out_specs=[
                one(TP, D), one(TP, D), one(TP, 3 * D), one(HEADS, TP, TP), one(TP, D), one(TP, D), fixed,
                flat, flat, half, half, fixed, pl.BlockSpec((1, D), lambda k, *s: (0, 0)),
            ],
            scratch_shapes=[pltpu.VMEM((D, rows), bf16)],
        ),
        out_shape=[
            shape(TP, D), shape(TP, D), shape(TP, 3 * D), shape(HEADS, TP, TP), shape(TP, D),
            shape(TP, D, dtype=f32), sds(rows, D),
            sds(rows, FF), sds(rows, FF), sds(2, 8, 192, 384), sds(2, 8, 192, 384), sds(rows, D),
            sds(1, D, dtype=f32),
        ],
        name="forward",
        **params(),
    )(info, core, x_slots, prev, nxt, w_qkv, w_proj, vec, tab, cot, w_fc1)


def down_kernel(info, core, dz_ref, slope_ref, n2_ref, w2_ref, *refs, last):
    if last:
        vec_ref, h_hbm, wproj_hbm, w1_hbm, before_hbm = refs[:5]
        keep_ref, send_ref, b1_ref, dh_ref, da_ref, do_ref, sums_ref = refs[8:15]
        n2_t, du_all, acc, w1_ref, h_ref, wproj_ref, sems = refs[15:]
        begin = before_hbm.shape[1]
        pairs = (
            (before_hbm, du_all.at[:, pl.ds(0, begin)]), (w1_hbm, w1_ref), (h_hbm, h_ref),
            (wproj_hbm, wproj_ref),
        )
        copies = [pltpu.make_async_copy(src, dst, sems.at[k]) for k, (src, dst) in enumerate(pairs)]
    else:
        keep_ref, send_ref, b1_ref, du_ref, n2_t = refs
    step = pl.program_id(0)

    @pl.when(step == 0)
    def _():
        if last:
            for copy in copies:
                copy.start()
        n2_t[...] = n2_ref[...].T

    du = (dot_nt(dz_ref[...], w2_ref[...]) * slope_ref[...].astype(f32)).astype(bf16)
    b1_ref[...] = jnp.sum(du.astype(f32), axis=0, keepdims=True)
    mine = (step & 1) == core[0]
    grad = dot(n2_t[...], du).astype(bf16)

    @pl.when(mine)
    def _():
        keep_ref[0] = grad

    @pl.when(jnp.logical_not(mine))
    def _():
        send_ref[0] = grad

    if not last:
        du_ref[...] = du
        return
    width = du.shape[1]
    du_all[:, pl.ds(pl.multiple_of(begin + step * width, 128), width)] = du

    @pl.when(step == pl.num_programs(0) - 1)
    def _():
        for copy in copies:
            copy.wait()
        vec = vec_ref[...]
        gain = jnp.zeros((1, D), f32)
        shift = jnp.zeros((1, D), f32)
        bias = jnp.zeros((1, D), f32)
        acc[...] = dot_nt(du_all[...], w1_ref[...])
        for k, mask in enumerate(masks(info, dz_ref.shape[0] // TP)):
            at = slice(TP * k, TP * k + TP)
            dn = acc[at] * mask
            normed, scale_inv = norm_parts(h_ref[at])
            gain += jnp.sum(dn * normed, axis=0, keepdims=True)
            shift += jnp.sum(dn, axis=0, keepdims=True)
            dh = mask * (dz_ref[at].astype(f32) + norm_back(dn * vec[1:2], normed, scale_inv))
            dh_ref[at] = dh
            da = dh.astype(bf16)
            da_ref[at] = da
            bias += jnp.sum(da.astype(f32), axis=0, keepdims=True)
        do_ref[...] = dot_nt(da_ref[...], wproj_ref[...]).astype(bf16)
        sums_ref[0:1] = gain
        sums_ref[1:2] = shift
        sums_ref[2:3] = bias
        sums_ref[3:8] = jnp.zeros((5, D), f32)


def feed_down(info, core, dz, slope, n2, w_fc2, begin, steps, more=()):
    rows = n2.shape[0]
    step = D
    last = bool(more)
    hbm = pl.BlockSpec(memory_space=pl.ANY)
    inputs = [dz, slope, n2, w_fc2, *more]
    in_specs = [
        whole(dz),
        pl.BlockSpec((rows, step), lambda k, *s: (0, k + begin)),
        whole(n2),
        pl.BlockSpec((step, D), lambda k, *s: (k + begin, 0)),
    ]
    half = pl.BlockSpec((1, D, step), lambda k, *s: ((k + begin) // 2, 0, 0))
    out_specs = [half, half, pl.BlockSpec((1, step), lambda k, *s: (0, k + begin))]
    out_shape = [sds(2, D, D), sds(2, D, D), sds(1, FF, dtype=f32)]
    scratch = [pltpu.VMEM((D, rows), bf16)]
    aliases = {}
    if last:
        flat = pl.BlockSpec((rows, D), lambda k, *s: (0, 0))
        in_specs += [whole(more[0])] + [hbm] * 7
        aliases = {11: 0, 12: 1, 13: 2}
        out_specs += [flat] * 3 + [pl.BlockSpec((8, D), lambda k, *s: (0, 0))]
        out_shape += [sds(rows, D, dtype=f32), sds(rows, D), sds(rows, D), sds(8, D, dtype=f32)]
        scratch += [
            pltpu.VMEM((rows, FF), bf16), pltpu.VMEM((rows, D), f32), pltpu.VMEM((D, FF), bf16),
            pltpu.VMEM((rows, D), f32), pltpu.VMEM((D, D), bf16), pltpu.SemaphoreType.DMA((4,)),
        ]
    else:
        out_specs += [pl.BlockSpec((rows, step), lambda k, *s: (0, k))]
        out_shape += [sds(rows, step * steps)]
    return pl.pallas_call(
        functools.partial(down_kernel, last=last),
        grid_spec=pltpu.PrefetchScalarGridSpec(
            num_scalar_prefetch=2, grid=(steps,), in_specs=in_specs, out_specs=out_specs,
            scratch_shapes=scratch,
        ),
        out_shape=out_shape,
        input_output_aliases=aliases,
        name="feed_down",
        **params(),
    )(info, core, *inputs)


def out_kernel(info, gl_ref, w2_ref, h_ref, vec_ref, out_ref, acc):
    step = pl.program_id(0)

    @pl.when(step == 0)
    def _():
        acc[...] = h_ref[...]

    acc[...] += dot(gl_ref[...], w2_ref[...])

    @pl.when(step == pl.num_programs(0) - 1)
    def _():
        for k, mask in enumerate(masks(info, out_ref.shape[0])):
            at = slice(TP * k, TP * k + TP)
            y = (mask * (acc[at] + vec_ref[7:8])).astype(bf16)
            out_ref[k] = dot(gather_rows(), y).astype(bf16)


def feed_out(info, gl, w_fc2, h, vec):
    rows = gl.shape[0]
    windows = rows // TP
    step = D
    return pl.pallas_call(
        out_kernel,
        grid_spec=pltpu.PrefetchScalarGridSpec(
            num_scalar_prefetch=1,
            grid=(FF // step,),
            in_specs=[
                pl.BlockSpec((rows, step), lambda k, s: (0, k)),
                pl.BlockSpec((step, D), lambda k, s: (k, 0)),
                whole(h), whole(vec),
            ],
            out_specs=pl.BlockSpec((windows, TOKW, D), lambda k, s: (0, 0, 0)),
            scratch_shapes=[pltpu.VMEM((rows, D), f32)],
        ),
        out_shape=sds(windows, TOKW, D),
        name="feed_out",
        **params(),
    )(info, gl, w_fc2, h, vec)


def key_rows():
    lane, col = iota((64, TP), 0), iota((64, TP), 1)
    i, j = col >> 4, col & 15
    hit = ((lane < WS) & (lane == i)) | ((lane >= 32) & (lane < 32 + WS) & (lane - 32 == 13 - j))
    return hit.astype(f32).astype(bf16)


def grad_rolls(table, base):
    lane = iota((16, 128), 1)
    out = []
    for i in range(WS):
        tile = table[16 * i : 16 * i + 16]
        by_row = jnp.where((lane >= base) & (lane < base + WS), tile, 0.0)
        by_row = pltpu.roll(by_row, 13 - i, 1) if i < 13 else by_row
        by_col = jnp.where((lane >= base + 32) & (lane < base + 32 + WS), tile, 0.0)
        out.append(by_row + pltpu.roll(by_col, 0, 1, stride=1, stride_axis=0))
    return jnp.concatenate(out, axis=0)


def back_kernel(qkv_ref, pt_ref, do_ref, tab_ref, *refs):
    dqkv_ref, table_ref, sums_ref = refs[-3:]

    @pl.when(pl.program_id(0) == 0)
    def _():
        table_ref[...] = jnp.zeros_like(table_ref)
        sums_ref[...] = jnp.zeros_like(sums_ref)

    rows_extra = key_rows()
    lane = iota((TP, 128), 1)
    for pair in range(HEADS // 2):
        at = 128 * pair
        q = qkv_ref[0, :, at : at + 128]
        key_t = (qkv_ref[0, :, D + at : D + at + 128] * jnp.asarray(0.125, bf16)).T
        v = qkv_ref[0, :, 2 * D + at : 2 * D + at + 128]
        do = do_ref[0, :, at : at + 128]
        ds_all, dq_all, z_all = [], [], []
        for head in range(2):
            p_t = pt_ref[0, 2 * pair + head].astype(f32)
            dp_t = dot_nt(v, do * lane_mask(head))
            mean = jnp.sum(p_t * dp_t, axis=0, keepdims=True) / jnp.sum(p_t, axis=0, keepdims=True)
            ds_t = (p_t * (dp_t - mean)).astype(bf16)
            ds_all.append(ds_t)
            if head == 0:
                left = jnp.concatenate([key_t[:HD], rows_extra], axis=0)
            else:
                left = jnp.concatenate([rows_extra, key_t[HD:]], axis=0)
            back = dot(left, ds_t).T
            dq_all.append(back)
            z_all.append(grad_rolls(back, 64 if head == 0 else 0))
        z = jnp.where(lane < HD, z_all[1], z_all[0]).astype(bf16)
        dq = jnp.where(lane < HD, dq_all[0], dq_all[1]) + dot(z, tab_ref[...])
        table_ref[...] += dot(z.T, q)
        two = lambda a: jnp.concatenate([a * lane_mask(0), a * lane_mask(1)], axis=0)
        dk = dot(jnp.concatenate(ds_all, axis=1), two(q)) * 0.125
        p_two = jnp.concatenate([pt_ref[0, 2 * pair], pt_ref[0, 2 * pair + 1]], axis=1)
        dv = dot(p_two, two(do))
        dqkv_ref[0, :, at : at + 128] = dq.astype(bf16)
        dqkv_ref[0, :, D + at : D + at + 128] = dk.astype(bf16)
        dqkv_ref[0, :, 2 * D + at : 2 * D + at + 128] = dv.astype(bf16)
    sums_ref[...] += jnp.sum(dqkv_ref[0].astype(f32), axis=0, keepdims=True)


def backward_attention(qkv, p_t, do, tab, begin, count, into=None):
    windows = qkv.shape[0]
    one = lambda *tail: pl.BlockSpec((1,) + tail, lambda k: (k + begin,) + (0,) * len(tail))
    inputs = [qkv, p_t, do, tab]
    in_specs = [one(TP, 3 * D), one(HEADS, TP, TP), one(TP, D), whole(tab)]
    if into is not None:
        inputs.append(into)
        in_specs.append(pl.BlockSpec(memory_space=pl.ANY))
    return pl.pallas_call(
        back_kernel,
        grid=(count,),
        in_specs=in_specs,
        out_specs=[
            one(TP, 3 * D),
            pl.BlockSpec((128, 128), lambda k: (0, 0)),
            pl.BlockSpec((1, 3 * D), lambda k: (0, 0)),
        ],
        out_shape=[sds(windows, TP, 3 * D), sds(128, 128, dtype=f32), sds(1, 3 * D, dtype=f32)],
        input_output_aliases={} if into is None else {4: 0},
        name="attention_backward",
        **params(),
    )(*inputs)


def weight_kernel(
    core, n1_ref, dqkv_ref, o_ref, da_ref, keep_ref, send_ref, n1_t, o_t
):
    @pl.when(pl.program_id(0) == 0)
    def _():
        n1_t[...] = n1_ref[...].T
        o_t[...] = o_ref[...].T

    part = dot(n1_t[...], dqkv_ref[...])
    proj = dot(o_t[...], da_ref[...])
    lane = iota((D, 128), 1) < 64
    even = core[0] == 0

    def put(at, first, second):
        first, second = first.astype(bf16), second.astype(bf16)
        keep_ref[0, :, at] = jnp.where(even, first, second)
        send_ref[0, :, at] = jnp.where(even, second, first)

    moved = pltpu.roll(proj[:, 0:256], 64, 1)
    rolled = pltpu.roll(part[:, 512:1152], 576, 1)
    put(slice(0, 512), part[:, 0:512], rolled[:, 0:512])
    put(
        slice(512, 640),
        jnp.where(lane, part[:, 512:640], moved[:, 0:128]),
        jnp.where(lane, rolled[:, 512:640], proj[:, 128:256]),
    )
    put(slice(640, 768), moved[:, 128:256], proj[:, 256:384])


def attention_weights(core, n1, dqkv, o, da):
    rows = n1.shape[0]
    wide = 3 * D // 2
    half = pl.BlockSpec((1, D, D), lambda k, *s: (k, 0, 0))
    return pl.pallas_call(
        weight_kernel,
        grid_spec=pltpu.PrefetchScalarGridSpec(
            num_scalar_prefetch=1,
            grid=(2,),
            in_specs=[
                whole(n1),
                pl.BlockSpec((rows, wide), lambda k, *s: (0, k)),
                whole(o),
                pl.BlockSpec((rows, D // 2), lambda k, *s: (0, k)),
            ],
            out_specs=[half] * 2,
            scratch_shapes=[pltpu.VMEM((D, rows), bf16), pltpu.VMEM((D, rows), bf16)],
        ),
        out_shape=[sds(2, D, D)] * 2,
        name="attention_weights",
        **params(),
    )(core, n1, dqkv, o, da)


def input_kernel(info, dqkv_ref, wqkv_ref, xpad_ref, dh_ref, vec_ref, dx_ref, sums_ref):
    vec = vec_ref[...]
    acc = dot_nt(dqkv_ref[...], wqkv_ref[...])
    k = pl.program_id(0)
    mask = inside(info[k, 2], info[k, 3])
    dn = acc * mask
    normed, scale_inv = norm_parts(xpad_ref[...].astype(f32))
    dx = dh_ref[...] + norm_back(dn * vec[0:1], normed, scale_inv)
    dx_ref[0] = dot(gather_rows(), dx.astype(bf16)).astype(bf16)

    @pl.when(k == 0)
    def _():
        sums_ref[...] = jnp.zeros_like(sums_ref)

    sums_ref[0:1] += jnp.sum(dn * normed, axis=0, keepdims=True)
    sums_ref[1:2] += jnp.sum(dn, axis=0, keepdims=True)


def input_gradient(info, dqkv, w_qkv, xpad, dh, vec):
    rows = xpad.shape[0]
    windows = rows // TP
    return pl.pallas_call(
        input_kernel,
        grid_spec=pltpu.PrefetchScalarGridSpec(
            num_scalar_prefetch=1,
            grid=(windows,),
            in_specs=[
                pl.BlockSpec((TP, 3 * D), lambda k, s: (k, 0)),
                whole(w_qkv),
                pl.BlockSpec((TP, D), lambda k, s: (k, 0)),
                pl.BlockSpec((TP, D), lambda k, s: (k, 0)),
                whole(vec),
            ],
            out_specs=[
                pl.BlockSpec((1, TOKW, D), lambda k, s: (k, 0, 0)),
                pl.BlockSpec((8, D), lambda k, s: (0, 0)),
            ],
        ),
        out_shape=[sds(windows, TOKW, D), sds(8, D, dtype=f32)],
        name="input_gradient",
        **params(),
    )(info, dqkv, w_qkv, xpad, dh, vec)


first_fix = 1.0 - 0.5**STEP
second_fix = float(np.float32(1.0) - np.power(np.float32(0.999), np.float32(STEP)))


def adam_step(parameter, gradient, moment, square):
    moment_next = 0.5 * moment + 0.5 * gradient
    square_next = 0.999 * square + 0.001 * gradient * gradient
    fresh_weight = parameter - learn_rate * (moment_next / first_fix) / (
        jnp.sqrt(square_next / second_fix) + 1e-08
    )
    return moment_next, square_next, fresh_weight.astype(bf16)


def adam_kernel(kept_ref, came_ref, own_ref, *refs):
    parts = (len(refs) - 1) // 5
    moments, squares, grads, moments_next, squares_next = (
        refs[parts * k : parts * k + parts] for k in range(5)
    )
    total = kept_ref[...].astype(f32) + came_ref[...].astype(f32)
    own = own_ref[...].astype(f32)
    begin, fresh = 0, []
    for k in range(parts):
        at = slice(begin, begin + moments[k].shape[1])
        grads[k][...] = total[:, at]
        moment, square, weight = adam_step(own[:, at], total[:, at], moments[k][...], squares[k][...])
        moments_next[k][...] = moment
        squares_next[k][...] = square
        fresh.append(weight.astype(f32))
        begin = at.stop
    fresh = fresh[0] if parts == 1 else jnp.concatenate(fresh, axis=1)
    refs[-1][...] = fresh.astype(bf16)


def adam(kept, came, own, moments, squares):
    shapes = [sds(*m.shape, dtype=f32) for m in moments]
    out = pl.pallas_call(
        adam_kernel,
        out_shape=shapes * 3 + [sds(*kept.shape)],
        name="adam",
        **params(12 << 20),
    )(kept, came, own, *moments, *squares)
    parts = len(moments)
    return [out[parts * k : parts * k + parts] for k in range(3)], out[-1]


def own_kernel(at, qkv_hbm, proj_hbm, fc1_hbm, fc2_hbm, attn_ref, fc1_ref, fc2_ref, qkv, proj, fc1, fc2, sems):
    win, grp = at[0], at[1]
    odd = (grp & 1) == 1

    def columns(width, more):
        return pl.ds(pl.multiple_of(width * grp - 64 * (grp & 1), 128), more)

    rows = fc1_ref.shape[0]
    some = pl.ds(pl.multiple_of(win * rows, 16), rows)
    many = pl.ds(pl.multiple_of(win * fc2.shape[0], 16), fc2.shape[0])
    copies = [
        pltpu.make_async_copy(qkv_hbm.at[some, columns(3 * D // 4, 640)], qkv, sems.at[0]),
        pltpu.make_async_copy(proj_hbm.at[some, columns(D // 4, 256)], proj, sems.at[1]),
        pltpu.make_async_copy(fc1_hbm.at[some, pl.ds(pl.multiple_of(D * grp, 128), D)], fc1, sems.at[2]),
        pltpu.make_async_copy(fc2_hbm.at[many, columns(D // 4, 256)], fc2, sems.at[3]),
    ]
    for copy in copies:
        copy.start()
    for copy in copies:
        copy.wait()

    def aligned(ref):
        whole = ref[...].astype(f32)
        return jnp.where(odd, pltpu.roll(whole, whole.shape[1] - 64, 1), whole)

    left, right = aligned(qkv), aligned(proj)
    attn_ref[:, 0:512] = left[:, 0:512].astype(bf16)
    right = pltpu.roll(right, 64, 1)
    lane = iota((rows, 128), 1) < 64
    attn_ref[:, 512:640] = jnp.where(lane, left[:, 512:640], right[:, 0:128]).astype(bf16)
    attn_ref[:, 640:768] = right[:, 128:256].astype(bf16)
    fc1_ref[...] = fc1[...]
    fc2_ref[...] = aligned(fc2).T[0 : D // 4].astype(bf16)


def own_blocks(win, grp, wins, grps, w_qkv, w_proj, w_fc1, w_fc2):
    rows, many = D // wins, FF // wins
    if grps != 4 or rows % 16 or many % 128:
        cut = lambda w, r, c: lax.dynamic_slice(w, (win * r, grp * c), (r, c))
        attn = [cut(w_qkv, rows, 3 * D // grps), cut(w_proj, rows, D // grps)]
        return jnp.concatenate(attn, axis=1), cut(w_fc1, rows, FF // grps), cut(w_fc2, many, D // grps).T
    hbm = pl.BlockSpec(memory_space=pl.ANY)
    vmem = pl.BlockSpec(memory_space=pltpu.VMEM)
    return pl.pallas_call(
        own_kernel,
        in_specs=[pl.BlockSpec(memory_space=pltpu.SMEM)] + [hbm] * 4,
        out_specs=[vmem] * 3,
        out_shape=[sds(rows, D), sds(rows, D), sds(D // 4, many)],
        scratch_shapes=[
            pltpu.VMEM((rows, 640), bf16), pltpu.VMEM((rows, 256), bf16), pltpu.VMEM((rows, D), bf16),
            pltpu.VMEM((many, 256), bf16), pltpu.SemaphoreType.DMA((4,)),
        ],
        name="own_blocks",
        **params(),
    )(jnp.stack([win, grp]).astype(jnp.int32), w_qkv, w_proj, w_fc1, w_fc2)


def place_kernel(at, have_ref, came_ref, *refs, way):
    half = have_ref.shape[0]
    rows, columns = have_ref.shape[1:]
    for target in range(2 * half):
        place = at[target]
        near = have_ref[jnp.minimum(place, half - 1)]
        far = came_ref[jnp.maximum(place - half, 0)]
        block = jnp.where(place < half, near, far)
        if way == "lanes":
            refs[0][:, columns * target : columns * target + columns] = block
        else:
            refs[-1 if way == "turned" else 0][rows * target : rows * target + rows] = block
    if way == "turned":
        whole = refs[-1][...].T
        begin = 0
        for out in refs[:-1]:
            out[...] = whole[begin : begin + out.shape[0]]
            begin += out.shape[0]


def put_in_place(at, have, came, way, widths=()):
    count, rows, columns = 2 * have.shape[0], have.shape[1], have.shape[2]
    smem = pl.BlockSpec(memory_space=pltpu.SMEM)
    vmem = pl.BlockSpec(memory_space=pltpu.VMEM)
    scratch = []
    if way == "lanes":
        shapes = [sds(rows, count * columns)]
    elif way == "rows":
        shapes = [sds(count * rows, columns)]
    else:
        shapes = [sds(width, count * rows) for width in widths]
        scratch = [pltpu.VMEM((count * rows, columns), bf16)]
    return pl.pallas_call(
        functools.partial(place_kernel, way=way),
        in_specs=[smem, vmem, vmem],
        out_specs=[vmem] * len(shapes),
        out_shape=shapes,
        scratch_shapes=scratch,
        name="put_in_place",
        **params(12 << 20),
    )(at, have, came)


def slots_kernel(at, dx_hbm, prev_hbm, next_hbm, out_hbm, held, sems):
    count = dx_hbm.shape[0]
    loads = [
        pltpu.make_async_copy(ref, held.at[pl.ds(begin, ref.shape[0])], sems.at[k])
        for k, (begin, ref) in enumerate(((0, dx_hbm), (count, prev_hbm), (count + 1, next_hbm)))
    ]
    for load in loads:
        load.start()
    held[count + 2] = jnp.zeros(held.shape[1:], bf16)
    for load in loads:
        load.wait()
    stores = [
        pltpu.make_async_copy(held.at[at[slot]], out_hbm.at[slot], sems.at[3 + slot])
        for slot in range(out_hbm.shape[0])
    ]
    for store in stores:
        store.start()
    for store in stores:
        store.wait()


def to_slots(at, dx, prev, nxt):
    slots, count = at.shape[0], dx.shape[0]
    hbm = pl.BlockSpec(memory_space=pl.ANY)
    return pl.pallas_call(
        slots_kernel,
        in_specs=[pl.BlockSpec(memory_space=pltpu.SMEM), hbm, hbm, hbm],
        out_specs=hbm,
        out_shape=sds(slots, TOKW, D),
        scratch_shapes=[
            pltpu.VMEM((count + 3, TOKW, D), bf16), pltpu.SemaphoreType.DMA((3 + slots,)),
        ],
        name="to_slots",
        **params(12 << 20),
    )(at, dx, prev, nxt)


AXES = ("win", "grp")


def bits_of(size):
    return [1 << k for k in range(size.bit_length() - 1)]


def flipped(axis, bit):
    wins, grps = lax.axis_size("win"), lax.axis_size("grp")
    out = []
    for d in range(wins * grps):
        w, g = divmod(d, grps)
        w, g = (w ^ bit, g) if axis == "win" else (w, g ^ bit)
        out.append((d, w * grps + g))
    return out


def windows_before(count, windows):
    total, before = count, jnp.zeros_like(count)
    bits = [(axis, bit) for axis in ("grp", "win") for bit in bits_of(lax.axis_size(axis))]
    for axis, bit in bits:
        last = (axis, bit) == bits[-1]
        other = windows - total if last else lax.ppermute(total, AXES, flipped(axis, bit))
        mine = (lax.axis_index(axis) & bit) != 0
        before = before + jnp.where(mine, other, 0)
        total = total + other
    return before


def neighbours(last, first):
    count = lax.axis_size("win") * lax.axis_size("grp")
    up = [(i, i + 1) for i in range(count - 1)]
    down = [(j, i) for i, j in up]
    return lax.ppermute(last, AXES, up), lax.ppermute(first, AXES, down)


def rising():
    return [(axis, bit) for axis in ("grp", "win") for bit in bits_of(lax.axis_size(axis))]


def tie(value, *others):
    return lax.optimization_barrier((value, *others))[0]


def places(order):
    apart = lax.axis_index("win") ^ jnp.arange(lax.axis_size("win"), dtype=jnp.int32)
    return sum(((apart & bit) != 0).astype(jnp.int32) << k for k, (_, bit) in enumerate(order))


class Piece:
    def __init__(self, kept, came, parts, rider=None):
        self.kept, self.came, self.parts, self.rider = kept, came, parts, rider

    def settle(self):
        if self.rider is not None:
            rows = self.kept.size // self.kept.shape[-1]
            self.rider.add(self.came[rows:])
            self.came, self.rider = self.came[:rows].reshape(self.kept.shape), None

    def halve(self, which, at=None, rider=None):
        self.settle()
        axis, bit = which
        place = self.parts.index(which)
        parts = self.parts[:place] + self.parts[place + 1 :]
        mine = ((lax.axis_index(axis) & bit) != 0).astype(jnp.int32)
        split = (1 << place, 2, -1) + self.kept.shape[-2:]
        kept, came = self.kept.reshape(split), self.came.reshape(split)

        def pick(half):
            piece = lax.dynamic_index_in_dim(kept, half, 1, keepdims=False)
            other = lax.dynamic_index_in_dim(came, half, 1, keepdims=False)
            if at is not None:
                piece, other = piece[..., at[0], at[1]], other[..., at[0], at[1]]
            return (piece.astype(f32) + other.astype(f32)).astype(bf16)

        send, kept = pick(1 - mine), pick(mine)
        if rider is None:
            return send, Piece(kept, lax.ppermute(send, AXES, flipped(axis, bit)), parts)
        columns = send.shape[-1]
        send = jnp.concatenate([send.reshape(-1, columns), rider.rows(columns)], axis=0)
        piece = Piece(kept, lax.ppermute(send, AXES, flipped(axis, bit)), parts, rider)
        piece.settle()
        return send, piece


class Chunk:
    def __init__(self, keep, send, axis):
        near, *self.grp = [one for one in rising() if one[0] == "grp"]
        self.win = [one for one in rising() if one[0] == "win"]
        parts = list(reversed(self.grp)) + list(reversed(self.win))
        self.pieces = [Piece(keep, lax.ppermute(send, AXES, flipped(*near)), parts)]
        self.block, self.axis, self.finish = keep.shape[-2:], axis, None
        self.cross = [(self.grp[-1], self.win[0]), (self.win[0], self.grp[-1])]
        self.order = self.grp[:-1] + self.win[1:]
        self.ways, self.back = list(reversed(self.win)), list(reversed(self.win))
        self.have, self.rider = None, None

    def left(self):
        return bool(self.cross or self.order or self.ways)

    def after(self, *others):
        if others:
            for piece in self.pieces:
                piece.came = tie(piece.came, *others)

    def step(self, *others):
        self.after(*others)
        if self.cross:
            whole, half = slice(None), self.block[self.axis] // 2
            cuts = [slice(0, half), slice(half, None)]
            ats = [(c, whole) if self.axis == 0 else (whole, c) for c in cuts]
            first, second = self.cross.pop(0)
            if len(self.pieces) == 1:
                (one,) = self.pieces
                made = [one.halve(first, ats[0]), one.halve(second, ats[1])]
            else:
                made = [self.pieces[0].halve(first, rider=self.rider), self.pieces[1].halve(second)]
            self.pieces = [piece for _, piece in made]
            return tuple(send for send, _ in made)
        for piece in self.pieces:
            piece.settle()
        if len(self.pieces) == 2:
            joined = lambda a, b: jnp.concatenate([a, b], axis=self.axis - 2)
            one, two = self.pieces
            shape = lambda a: a.reshape((-1,) + a.shape[-2:])
            self.pieces = [
                Piece(
                    joined(shape(one.kept), shape(two.kept)),
                    joined(shape(one.came), shape(two.came)),
                    one.parts,
                )
            ]
        (piece,) = self.pieces
        if self.order:
            send, piece = piece.halve(self.order.pop(0), rider=self.rider)
            self.pieces = [piece]
            return send
        if self.have is None:
            self.result, fresh = self.finish(piece.kept.reshape(self.block), piece.came.reshape(self.block))
            self.have = fresh[None]
        else:
            self.have = jnp.concatenate([self.have, piece.came], axis=0)
        piece.came = lax.ppermute(self.have, AXES, flipped(*self.ways.pop(0)))
        return self.have

    def all(self, way, widths=()):
        have, came = self.have, self.pieces[0].came
        if self.block[0] % 16 == 0 and self.block[1] % 128 == 0:
            return put_in_place(places(self.back), have, came, way, widths)
        blocks = jnp.concatenate([have, came], axis=0)[places(self.back)]
        if way == "lanes":
            return [blocks.transpose(1, 0, 2).reshape(blocks.shape[1], -1)]
        blocks = blocks.reshape(-1, blocks.shape[2])
        return [blocks] if way == "rows" else jnp.split(blocks.T, np.cumsum(widths)[:-1], axis=0)


class Total:
    def __init__(self, vector):
        self.vector = vector
        self.order = [one for one in rising() if one[0] == "grp"]

    def rows(self, columns):
        flat = jnp.pad(self.vector, (0, -self.vector.shape[0] % columns))
        return flat.reshape(-1, columns).astype(bf16)

    def add(self, rows):
        self.vector = self.vector + rows.reshape(-1)[: self.vector.shape[0]].astype(f32)

    def left(self):
        return bool(self.order)

    def step(self, *after):
        mine = tie(self.vector, *after)
        self.vector = mine + lax.ppermute(mine, AXES, flipped(*self.order.pop(0)))
        return mine


def per_device(
    x_slots, counts, cotangent, w_qkv, w_proj, w_fc1, w_fc2, small_params,
    moment_qkv, moment_proj, moment_fc1, moment_fc2, moment_small,
    square_qkv, square_proj, square_fc1, square_fc2, square_small,
):
    slots, per_even = x_slots.shape[0], cotangent.shape[0]
    win_at, grp_at = lax.axis_index("win"), lax.axis_index("grp")
    wins, grps = lax.axis_size("win"), lax.axis_size("grp")
    base = (win_at * grps + grp_at) * per_even
    count = counts[0]
    prev, nxt = neighbours(lax.dynamic_slice_in_dim(x_slots, count - 1, 1, 0), x_slots[:1])
    offset = windows_before(counts, per_even * wins * grps)[0]
    window = base + jnp.arange(per_even, dtype=jnp.int32)
    slot = window - offset
    spot = window % (GRID * GRID)
    info = jnp.stack(
        [
            jnp.clip(slot, 0, slots - 1),
            jnp.where(slot < 0, 1, jnp.where(slot >= count, 2, 0)),
            SIDE - WS * (spot // GRID),
            SIDE - WS * (spot % GRID),
        ],
        axis=1,
    ).astype(jnp.int32)
    vec, tab_fwd = vectors(small_params), forward_tables(small_params)
    blocks = lambda grad: grad.reshape(grps // 2, wins, D // wins, grad.shape[2])
    core = (grp_at & 1).astype(jnp.int32).reshape(1)
    flat = lambda a: a.reshape(per_even * TP, a.shape[2])
    xpad, n1, qkv, p_t, o, h, n2, gl, slope, keep, send, dz, sum_b2 = forward(
        info, core, x_slots, prev, nxt, cotangent, w_qkv, w_proj, w_fc1, vec, tab_fwd
    )
    tab_bwd = backward_tables(tie(small_params, n2))
    h, n1, o, xpad = flat(h), flat(n1), flat(o), flat(xpad)
    if wins != keep.shape[1]:
        again = lambda a: a.transpose(0, 2, 1, 3).reshape(grps // 2, D // grps, wins, FF // wins).transpose(0, 2, 1, 3)
        keep, send = again(keep), again(send)
    fc2 = Chunk(keep, send, 0)
    fc2.finish = lambda kept, came: adam(kept, came, own_fc2, [moment_fc2.T], [square_fc2.T])
    *half, du = feed_down(info, core, dz, slope, n2, w_fc2, 0, 2)
    sent = fc2.step(du)
    keep, send, sum_b1, dh, da, do, sums_two = feed_down(
        info, core, tie(dz, *sent), slope, n2, w_fc2, 2, 2, (vec, h, w_proj, w_fc1, du, *half)
    )
    do = do.reshape(per_even, TP, D)
    sent = fc2.step(do)
    fc1 = Chunk(blocks(tie(keep, *sent)), blocks(tie(send, *sent)), 1)
    fc1.finish = lambda kept, came: adam(kept, came, own_fc1, [moment_fc1], [square_fc1])
    dqkv, table, sum_qkv = backward_attention(qkv, p_t, tie(do, send, *sent), tab_bwd, 0, 1)
    sent = fc1.step(table)
    sent = (*sent, fc2.step(*sent))
    dqkv, table_two, sum_two = backward_attention(
        qkv, p_t, tie(do, *sent), tab_bwd, 1, per_even - 1, dqkv
    )
    table, sum_qkv = table + table_two, sum_qkv + sum_two
    sent = fc1.step(table_two)
    sent = (*sent, fc2.step(*sent))
    dqkv = flat(dqkv)
    keep, send = attention_weights(core, n1, tie(dqkv, *sent), o, da)
    fc1.after(keep)
    fc2.after(keep)
    send = tie(send, *(piece.came for piece in fc1.pieces + fc2.pieces))
    attn = Chunk(blocks(keep), blocks(send), 1)
    attn.finish = lambda kept, came: adam(
        kept, came, own_attn, [moment_qkv, moment_proj], [square_qkv, square_proj]
    )
    sent = fc1.step(send)
    win_later = tie(win_at, sent)
    own_attn, own_fc1, own_fc2 = own_blocks(win_later, grp_at, wins, grps, w_qkv, w_proj, w_fc1, w_fc2)
    sent = fc2.step(own_fc2)
    sent = attn.step(sent)
    dx, sums_one = input_gradient(info, tie(dqkv, *sent), w_qkv, xpad, dh, vec)
    sums = (table, sum_qkv, sums_one, sums_two, sum_b1, sum_b2)
    sums, offset = tie((sums, offset), sums_one)
    table, sum_qkv, sums_one, sums_two, sum_b1, sum_b2 = sums
    rel_h = (table[0:RELN, 64:] + table[64 : 64 + RELN, :64])[::-1]
    rel_w = table[32 : 32 + RELN, 64:] + table[96 : 96 + RELN, :64]
    small = Total(
        jnp.concatenate(
            [
                sums_one[0], sums_two[0], sums_one[1], sums_two[1], sum_qkv[0, :D], sum_qkv[0, 2 * D :],
                sums_two[2], sum_b2[0], sum_b1[0], rel_h.reshape(-1), rel_w.reshape(-1),
            ]
        )
    )
    place = offset + jnp.arange(slots, dtype=jnp.int32) - base
    back = jnp.where(place < 0, per_even, jnp.where(place >= per_even, per_even + 1, place))
    back = jnp.where(jnp.arange(slots) < count, back, per_even + 2).astype(jnp.int32)
    token = fc1.step(dx)
    token = fc2.step(token)
    attn.rider = small
    made, rounds = {}, 0

    def slots_gap(token):
        made["dx"] = to_slots(tie(back, token), dx, dx_prev, dx_next)
        return made["dx"]

    def place_gap(name, chunk, way):
        def gap(token):
            chunk.pieces[0].came = tie(chunk.pieces[0].came, token)
            made[name] = chunk.all(way)
            return made[name][0]

        return gap

    ends = [(fc2, place_gap("fc2", fc2, "lanes")), (fc1, place_gap("fc1", fc1, "rows"))]
    while attn.left() or fc2.left() or fc1.left() or small.left():
        done = [end for end in ends if not end[0].left()]
        for chunk in (attn, fc1, fc2, small):
            idle = chunk is fc1 and rounds in (1,) or chunk is small and attn.order
            if chunk.left() and not idle:
                token = chunk.step(token)
        for end in done[:1]:
            token = end[1](token)
            ends.remove(end)
        rounds += 1
    dx_prev, dx_next = neighbours(*tie((dx[per_even - 1 :], dx[:1]), token))
    made["out"] = token = feed_out(info, tie(gl, token), w_fc2, h, vec)
    for end in ends:
        token = end[1](token)
    attn.pieces[0].came = tie(attn.pieces[0].came, token)
    block_out = made["out"]
    made["attn"] = attn.all("turned", (3 * D // grps, D // grps))
    input_grad = slots_gap(made["attn"])
    part_d, next_m_fc2, next_v_fc2 = (one[0].T for one in fc2.result)
    (part_c,), (next_m_fc1,), (next_v_fc1,) = fc1.result
    (part_a, part_b), (next_m_qkv, next_m_proj), (next_v_qkv, next_v_proj) = attn.result
    new_fc2, new_fc1 = made["fc2"][0].T, made["fc1"][0]
    new_qkv, new_proj = (part.T for part in made["attn"])
    grad_small = small.vector
    upd_small = adam_step(small_params.astype(f32), grad_small, moment_small, square_small)
    return (
        block_out, input_grad, part_a, part_b, part_c, part_d, grad_small,
        next_m_qkv, next_m_proj, next_m_fc1, next_m_fc2, upd_small[0],
        next_v_qkv, next_v_proj, next_v_fc1, next_v_fc2, upd_small[1],
        new_qkv, new_proj, new_fc1, new_fc2, upd_small[2],
    )


def solution(mesh):
    data, shard, same, part = P(AXES, None, None), P("win", "grp"), P(), P(None, "grp")
    in_specs = (data, P(AXES), data) + (same,) * 5 + ((shard,) * 4 + (same,)) * 2
    out_specs = (data,) * 2 + ((shard,) * 4 + (same,)) * 3 + (part,) * 4 + (same,)
    return jax.shard_map(
        per_device, mesh=mesh, in_specs=in_specs, out_specs=out_specs, check_vma=False
    )
```
